32 devices in a mesh: dp: 8 (over z, x), mp: 4 (over y, core).
Axes of the slice: x: 2, y: 2, z: 4, core: 2. Of those that a mesh axis runs over, the one named last changes fastest.
Arguments:
- tokens: bfloat16 [32768, 768], P(('dp', 'mp')), may hold values from -6 to 6
- segments: int32 [64, 512], P(('dp', 'mp')), may hold values from 0 to 5, never falling along the last dimension, each value on 1 to 256 neighbouring positions
- head_mask: int32 [12], replicated, may hold values 0 or 1
- unit_mask: int32 [3072], replicated, may hold values 0 or 1
- hidden_mask: int32 [768], replicated, may hold values 0 or 1
- layer_gates: float32 [2], replicated, may hold values from 0.5 to 1.5
- qkv_weight: bfloat16 [768, 2304], P('mp'), may hold values from -0.21875 to 0.21875
- out_weight: bfloat16 [768, 768], P('mp'), may hold values from -1.75 to 1.75
- norm_gain: float32 [768], replicated, may hold values from 0.5 to 1.5
- norm_bias: float32 [768], replicated, may hold values from -3 to 3
- up_weight: bfloat16 [768, 3072], P(None, 'mp'), may hold values from -0.21875 to 0.21875
- down_weight: bfloat16 [768, 3072], P(None, 'mp'), may hold values from -0.109375 to 0.109375
- cotangent: bfloat16 [32768, 768], P(('dp', 'mp')), may hold values from -6 to 6
- owner_slot: int32 [48], replicated, may hold values from 0 to 47, as said below
- master: float32 [48, 384, 384], P('dp', 'mp'), may hold values from -0.21875 to 0.21875
- left_stats: float32 [48, 384, 384], P('dp', 'mp'), may hold values from -12582912 to 50331648
- right_stats: float32 [48, 384, 384], P('dp', 'mp'), may hold values from -12582912 to 50331648
- left_root: float32 [48, 384, 384], P('dp', 'mp'), may hold values from -1 to 1
- right_root: float32 [48, 384, 384], P('dp'), may hold values from -1 to 1
Outputs:
- output: bfloat16 [32768, 768], P(('dp', 'mp'))
- input_grad: float32 [32768, 768], P(('dp', 'mp'))
- head_grad: float32 [12], replicated
- unit_grad: float32 [3072], replicated
- hidden_grad: float32 [768], replicated
- layer_grad: float32 [2], replicated
- norm_grad: float32 [2, 768], replicated
- norm_new: float32 [2, 768], replicated
- block_grad: float32 [48, 384, 384], P('dp', 'mp')
- left_new: float32 [48, 384, 384], P('dp', 'mp')
- right_new: float32 [48, 384, 384], P('dp', 'mp')
- weight_new: float32 [48, 384, 384], P('dp', 'mp')
- weight_copy: bfloat16 [48, 384, 384], P('dp', 'mp')
The draws below stay inside these ranges and needn't reach their ends.
Inputs may be any that keep to these rules, and one draw needn't show every extreme that they name: `segments`: in every block of 512 positions the item numbers run from 0 to 5 and never fall; each item has 1 to 256 positions, and one item of each block has exactly 256. `owner_slot`: every slot number appears exactly once.
All inputs are finite; a program needn't handle non-finite values.
Results may differ from the reference program's by a relative error of at most 0.017.
Values may be sent and summed in bfloat16 or wider, within the bound.
A program may use at most 192 MiB of HBM per device.

```python
import math
import jax
import jax.numpy as jnp
import numpy as np
from jax import lax

D = 768
HEADS = 12
HEAD = 64
FF = 3072
BLOCK = 512
ITEMS = 6
SB = 384
BLOCKS_DEV = 2
TOKENS = 32768
NBLK = 48


def slot_numbers(key):
    return jax.random.permutation(jax.random.fold_in(key, 101), NBLK)


def block_scale(key):
    slot_order = jnp.argsort(slot_numbers(key))
    qkv_count = 3 * D * D // (SB * SB)
    out_count = D * D // (SB * SB)
    up_count = D * FF // (SB * SB)
    sigma = jnp.where(slot_order < qkv_count, 1.0, jnp.where(slot_order < qkv_count + out_count, 0.12, jnp.where(slot_order < qkv_count + out_count + up_count, 0.3, 0.6)))
    return sigma.astype(jnp.float32) ** 2 * float(SB * TOKENS)


def symmetric_noise(key):
    noise = jax.random.truncated_normal(key, -4.0, 4.0, (NBLK, SB, SB), jnp.float32)
    return (noise + jnp.swapaxes(noise, 1, 2)) * 0.7071


def statistic(key, salt):
    scaling = block_scale(key)
    first, second = jax.random.split(jax.random.fold_in(key, salt))
    diagonal = jax.random.uniform(first, (NBLK, SB), jnp.float32, 1.0, 4.0)
    identity = jnp.eye(SB, dtype=jnp.float32)
    matrix = diagonal[:, :, None] * identity + 0.04 * symmetric_noise(second) * (1.0 - identity)
    return matrix * scaling[:, None, None]


def root_matrix(key, salt):
    scaling = block_scale(key) ** (-0.25)
    first, second = jax.random.split(jax.random.fold_in(key, salt))
    diagonal = jax.random.uniform(first, (NBLK, SB), jnp.float32, 0.7, 1.4)
    identity = jnp.eye(SB, dtype=jnp.float32)
    matrix = diagonal[:, :, None] * identity + 0.02 * symmetric_noise(second) * (1.0 - identity)
    return matrix * scaling[:, None, None]


def draw_owner_slot(key, part):
    return slot_numbers(key).astype(jnp.int32)


def draw_left_stats(key, part):
    return statistic(key, 201)


def draw_right_stats(key, part):
    return statistic(key, 202)


def draw_left_root(key, part):
    return root_matrix(key, 203)


def draw_right_root(key, part):
    return root_matrix(key, 204)


def plant(values, stream_key, smallest, top_value):
    extent = values.shape
    index_at = [jax.random.randint(jax.random.fold_in(stream_key, axis), (), 0, extent[axis]) for axis in range(len(extent))]
    values = values.at[tuple(index_at)].set(smallest)
    longest = extent.index(max(extent))
    index_at[longest] = (index_at[longest] + 1) % extent[longest]
    return values.at[tuple(index_at)].set(top_value)


def steps_of(key, extent, cuts, smallest, high):
    gain, own = 1.0, jax.random.fold_in(key, 6)
    for dim, parts in cuts:
        draws = jnp.exp(jax.random.uniform(jax.random.fold_in(own, dim), (parts,), jnp.float32, smallest / len(cuts), high / len(cuts)))
        gain = gain * jnp.repeat(draws, extent[dim] // parts).reshape([-1 if axis == dim else 1 for axis in range(len(extent))])
    return gain


def profile(amount, total, reach, slope):
    weights = [(1 << 20) // math.isqrt(standing ** slope) + 1 for standing in range(2, amount + 1)]
    spare, counts = total - reach - (amount - 1), [1] * (amount - 1)
    while spare > 0:
        movable = [i for i in range(amount - 1) if counts[i] < reach]
        whole, remaining = sum([weights[i] for i in movable]), spare
        for i in movable:
            more = min(reach - counts[i], max(1, remaining * weights[i] // whole), spare)
            counts[i] = counts[i] + more
            spare = spare - more
    return np.array([reach] + counts)


def uneven(key, count, total, bound, lean):
    if count == 2:
        one = jax.random.randint(key, (), max(1, total - bound), min(bound, total - 1) + 1)
        return jnp.stack([one, total - one])
    lengths = jnp.asarray(profile(count, total, bound, lean), jnp.int32)
    twos = (count - 1) // 2
    giver, sink = lengths[1:1 + 2 * twos:2], lengths[2:2 + 2 * twos:2]
    room = jnp.minimum(giver - 1, bound - sink)
    moved = jax.random.randint(jax.random.fold_in(key, 1), (twos,), 0, 1 << 20) % (room + 1)
    lengths = lengths.at[1:1 + 2 * twos:2].set(giver - moved).at[2:2 + 2 * twos:2].set(sink + moved)
    return lengths[jax.random.permutation(jax.random.fold_in(key, 2), count)]


def centred(stream_key, dims, scale, bound, cuts=(), kind=jnp.bfloat16):
    values = scale * jax.random.normal(stream_key, dims, jnp.float32)
    if cuts:
        values = values * steps_of(stream_key, dims, cuts, -0.22, 0.18)
    return jnp.clip(values, -bound, bound).astype(kind)


def setup_inputs(seed: int = 0) -> dict:
    splits = jax.random.split(jax.random.key(seed), 20)
    return {
        "tokens": centred(splits[0], (TOKENS, D), 1.0, 6.0, ((0, 32),)),
        "segments": jax.vmap(lambda own: jnp.searchsorted(jnp.cumsum(uneven(own, ITEMS, BLOCK, BLOCK // 2, 0)), jnp.arange(BLOCK), side="right"))(jax.random.split(splits[1], (TOKENS // BLOCK))).reshape((TOKENS // BLOCK, BLOCK)).astype(jnp.int32),
        "head_mask": plant((jax.random.randint(splits[2], (HEADS,), 0, 4) < 3).astype(jnp.int32), jax.random.fold_in(splits[2], 1), 0, 1),
        "unit_mask": plant((jax.random.randint(splits[3], (FF,), 0, 4) < 3).astype(jnp.int32), jax.random.fold_in(splits[3], 1), 0, 1),
        "hidden_mask": plant((jax.random.randint(splits[4], (D,), 0, 8) < 7).astype(jnp.int32), jax.random.fold_in(splits[4], 1), 0, 1),
        "layer_gates": jnp.clip(jax.random.uniform(splits[5], (2,), jnp.float32, 0.5, 1.5), 0.5, 1.5),
        "qkv_weight": centred(splits[6], (D, 3 * D), D ** -0.5, 0.21875, ((0, 4),)),
        "out_weight": centred(splits[7], (D, D), (D // HEAD) ** -0.5, 1.75, ((0, 4),)),
        "norm_gain": jnp.clip(1.0 + 0.1 * jax.random.normal(splits[8], (D,), jnp.float32), 0.5, 1.5),
        "norm_bias": centred(splits[9], (D,), 0.5, 3.0, (), jnp.float32),
        "up_weight": centred(splits[10], (D, FF), D ** -0.5, 0.21875, ((1, 4),)),
        "down_weight": centred(splits[11], (D, FF), FF ** -0.5, 0.109375, ((1, 4),)),
        "cotangent": centred(splits[12], (TOKENS, D), 1.0, 6.0, ((0, 32),)),
        "owner_slot": draw_owner_slot(jax.random.fold_in(splits[19], 71), 0),
        "master": centred(splits[14], (NBLK, SB, SB), D ** -0.5, 0.21875, ((0, 8), (1, 4)), jnp.float32),
        "left_stats": draw_left_stats(jax.random.fold_in(splits[19], 71), 0),
        "right_stats": draw_right_stats(jax.random.fold_in(splits[19], 71), 0),
        "left_root": draw_left_root(jax.random.fold_in(splits[19], 71), 0),
        "right_root": draw_right_root(jax.random.fold_in(splits[19], 71), 0),
    }


@jax.custom_vjp
def low(v):
    return lax.optimization_barrier(v.astype(jnp.bfloat16)).astype(jnp.float32)

@jax.custom_vjp
def low_back(v):
    return v

def low_keep(v):
    return (low(v), None)

def low_pass(kept, grad):
    return (grad,)

def back_keep(v):
    return (v, None)

def back_low(kept, grad):
    return (low(grad),)
low.defvjp(low_keep, low_pass)
low_back.defvjp(back_keep, back_low)
HIGH = lax.Precision.HIGHEST
BETA = 0.5
RATE = 0.5
EPS = 1e-12
MASKED = -1e+30

def matmul(left, right):
    return jnp.dot(left, right, precision=HIGH, preferred_element_type=jnp.float32)

def attend(packed):
    block_queries, block_keys, block_values, labels = packed
    scores = jnp.einsum('qhd,khd->hqk', block_queries, block_keys, precision=HIGH) * HEAD ** (-0.5)
    scores = low_back(scores)
    allowed = labels[:, None] == labels[None, :]
    scores = jnp.where(allowed[None], scores, MASKED)
    weights = jax.nn.softmax(scores, axis=-1)
    return jnp.einsum('hqk,khd->qhd', low(weights), block_values, precision=HIGH)

def layer(params, group_rows, group_labels):
    qkv_weight, out_weight, norm_gain, norm_bias, up_weight, down_weight, head_gate, layer_gates, unit_gate, hidden_gate = params
    row_count = group_rows.shape[0]
    joined = low_back(low(matmul(group_rows, qkv_weight)))
    joined = joined.reshape(row_count // BLOCK, BLOCK, 3, HEADS, HEAD)
    context = lax.map(jax.checkpoint(attend), (joined[:, :, 0], joined[:, :, 1], joined[:, :, 2], group_labels))
    context = context.reshape(row_count, HEADS, HEAD) * head_gate[None, :, None]
    gated = low_back(low(context.reshape(row_count, D)))
    attn_out = low_back(matmul(gated, out_weight))
    summed = group_rows + layer_gates[0] * attn_out
    centre = summed - lax.optimization_barrier(jnp.mean(summed, axis=-1, keepdims=True))
    spread = lax.optimization_barrier(jnp.mean(centre * centre, axis=-1, keepdims=True))
    normed = centre * lax.rsqrt(spread + EPS)
    hidden = (normed * norm_gain + norm_bias) * hidden_gate
    pre_act = low_back(matmul(low(hidden), up_weight))
    active = low(jax.nn.gelu(pre_act, approximate=False) * unit_gate)
    branch = low_back(jnp.einsum('tf,df->td', active, down_weight, precision=HIGH))
    return hidden + layer_gates[1] * branch

def blocks_of(matrix):
    row_count, col_count = matrix.shape
    pieces = matrix.reshape(row_count // SB, SB, col_count // SB, SB).transpose(0, 2, 1, 3)
    return pieces.reshape(-1, SB, SB)

def reference(tokens, segments, head_mask, unit_mask, hidden_mask, layer_gates, qkv_weight, out_weight, norm_gain, norm_bias, up_weight, down_weight, cotangent, owner_slot, master, left_stats, right_stats, left_root, right_root):
    group_blocks = BLOCKS_DEV * 4
    group_rows = group_blocks * BLOCK
    group_count = TOKENS // group_rows
    inputs = tokens.astype(jnp.float32)
    params = (qkv_weight.astype(jnp.float32), out_weight.astype(jnp.float32), norm_gain, norm_bias, up_weight.astype(jnp.float32), down_weight.astype(jnp.float32), head_mask.astype(jnp.float32), layer_gates, unit_mask.astype(jnp.float32), hidden_mask.astype(jnp.float32))
    labels = segments.reshape(group_count, group_blocks, BLOCK)

    def forward(params, inputs):

        def single(packed):
            rows_in, group_labels = packed
            return layer(params, rows_in, group_labels)
        results = lax.map(jax.checkpoint(single), (inputs.reshape(group_count, group_rows, D), labels))
        return results.reshape(TOKENS, D)
    result, pullback = jax.vjp(forward, params, inputs)
    param_grads, input_grad = pullback(cotangent.astype(jnp.float32))
    qkv_grad, out_grad, gain_grad, bias_grad, up_grad, down_grad, head_grad, layer_grad, unit_grad, hidden_grad = param_grads
    stacked = jnp.concatenate([blocks_of(qkv_grad), blocks_of(out_grad), blocks_of(up_grad), blocks_of(down_grad)], axis=0)
    slot_order = jnp.argsort(owner_slot)
    slot_grads = stacked[slot_order]
    left_new = BETA * left_stats + (1.0 - BETA) * jnp.einsum('sij,skj->sik', slot_grads, slot_grads, precision=HIGH)
    right_new = BETA * right_stats + (1.0 - BETA) * jnp.einsum('sji,sjk->sik', slot_grads, slot_grads, precision=HIGH)
    update = jnp.einsum('sij,sjk->sik', jnp.einsum('sij,sjk->sik', left_root, slot_grads, precision=HIGH), right_root, precision=HIGH)
    weight_new = master - RATE * update
    norm_grad = jnp.stack([gain_grad, bias_grad])
    norm_new = jnp.stack([norm_gain, norm_bias]) - 0.2 / TOKENS ** 0.5 * norm_grad
    return (result.astype(jnp.bfloat16), input_grad, head_grad, unit_grad, hidden_grad, layer_grad, norm_grad, norm_new, slot_grads, left_new, right_new, weight_new, weight_new.astype(jnp.bfloat16))
```

```python
from functools import partial
import math

import jax
import jax.numpy as jnp
from jax import lax
from jax.experimental import pallas as pl
from jax.experimental.pallas import tpu as pltpu
from jax.sharding import PartitionSpec as P

FF = 3072
SB = 384


HIGH = lax.Precision.HIGHEST
BETA = 0.5
RATE = 0.5
EPS = 1e-12
MASKED = -1e30


def gelu_exact(values):
    return jax.nn.gelu(values, approximate=False)


def normalize(summed, gain_in, offset, hidden_gate):
    centre = summed - jnp.mean(summed, axis=-1, keepdims=True)
    spread = jnp.mean(centre * centre, axis=-1, keepdims=True)
    return (centre * lax.rsqrt(spread + EPS) * gain_in + offset) * hidden_gate


def split_heads(block_joined, head_count):
    pieces = block_joined.reshape(block_joined.shape[0], 3, head_count, -1)
    return (pieces[:, 0], pieces[:, 1], pieces[:, 2])


def masked_scores(queries, keys_in, labels, factor):
    scores = (
        jnp.einsum("qhd,khd->hqk", queries, keys_in, preferred_element_type=jnp.float32) * factor
    )
    allowed = labels[:, None] == labels[None, :]
    return jnp.where(allowed[None], scores, MASKED)


def attend_forward(packed, head_count, factor):
    block_joined, labels = packed
    queries, keys_in, values_in = split_heads(block_joined, head_count)
    scores = masked_scores(queries, keys_in, labels, factor)
    highest = jnp.max(scores, axis=-1, keepdims=True)
    raised = jnp.exp(scores - highest)
    totals = jnp.sum(raised, axis=-1, keepdims=True)
    weights_low = (raised / totals).astype(jnp.bfloat16)
    context = jnp.einsum("hqk,khd->qhd", weights_low, values_in, preferred_element_type=jnp.float32)
    return (context, (highest + jnp.log(totals))[:, :, 0])


def attend_backward(packed, head_count, factor):
    block_joined, log_totals, context_grad, labels = packed
    queries, keys_in, values_in = split_heads(block_joined, head_count)
    scores = masked_scores(queries, keys_in, labels, factor)
    weights_full = jnp.exp(scores - log_totals[:, :, None])
    weights_low = weights_full.astype(jnp.bfloat16)
    values_grad = jnp.einsum(
        "hqk,qhd->khd", weights_low, context_grad, preferred_element_type=jnp.float32
    )
    weights_grad = jnp.einsum(
        "qhd,khd->hqk", context_grad, values_in, preferred_element_type=jnp.float32
    )
    inner_sum = jnp.sum(weights_full * weights_grad, axis=-1, keepdims=True)
    scores_grad = (weights_full * (weights_grad - inner_sum)).astype(jnp.bfloat16)
    queries_grad = (
        jnp.einsum("hqk,khd->qhd", scores_grad, keys_in, preferred_element_type=jnp.float32)
        * factor
    )
    keys_grad = (
        jnp.einsum("hqk,qhd->khd", scores_grad, queries, preferred_element_type=jnp.float32)
        * factor
    )
    merged = jnp.concatenate([queries_grad, keys_grad, values_grad], axis=1)
    return merged.reshape(merged.shape[0], -1).astype(jnp.bfloat16)


def contract_rows(left, right):
    return lax.dot_general(
        left, right, (((0,), (0,)), ((), ())), preferred_element_type=jnp.float32
    )


def contract_cols(left, right):
    return lax.dot_general(
        left, right, (((1,), (1,)), ((), ())), preferred_element_type=jnp.float32
    )


def body(
    tokens,
    segments,
    head_mask,
    unit_mask,
    hidden_mask,
    layer_gates,
    qkv_weight,
    out_weight,
    norm_gain,
    norm_bias,
    up_weight,
    down_weight,
    cotangent,
    owner_slot,
    master,
    left_stats,
    right_stats,
    left_root,
    right_root,
):
    row_count = tokens.shape[0]
    width = tokens.shape[1]
    head_count = head_mask.shape[0]
    head_width = width // head_count
    block_rows = segments.shape[1]
    block_count = segments.shape[0]
    factor = 1.0 / math.sqrt(head_width)
    model_size = lax.axis_size("mp")
    share = FF // model_size
    part_rows = SB // model_size
    total_tokens = row_count * lax.axis_size("dp") * model_size
    head_gate = head_mask.astype(jnp.float32)
    unit_gate = unit_mask.astype(jnp.float32)
    hidden_gate = hidden_mask.astype(jnp.float32)
    inputs = tokens.astype(jnp.float32)
    back_full = cotangent.astype(jnp.float32)
    qkv_full, out_full, up_full, down_full = (
        lax.all_gather(qkv_weight, "mp", axis=0, tiled=True),
        lax.all_gather(out_weight, "mp", axis=0, tiled=True),
        lax.all_gather(up_weight, "mp", axis=1, tiled=True),
        lax.all_gather(down_weight, "mp", axis=1, tiled=True),
    )
    joined_qkv = jnp.dot(tokens, qkv_full, preferred_element_type=jnp.float32).astype(jnp.bfloat16)
    joined_blocks = joined_qkv.reshape(block_count, block_rows, 3 * width)
    context, log_totals = lax.map(
        partial(attend_forward, head_count=head_count, factor=factor), (joined_blocks, segments)
    )
    context = context.reshape(row_count, head_count, head_width)
    gated_low = (context * head_gate[None, :, None]).reshape(row_count, width).astype(jnp.bfloat16)
    attn_out = jnp.dot(gated_low, out_full, preferred_element_type=jnp.float32)
    summed = inputs + layer_gates[0] * attn_out
    hidden, norm_pull = jax.vjp(normalize, summed, norm_gain, norm_bias, hidden_gate)
    hidden_low = hidden.astype(jnp.bfloat16)
    pre_act = jnp.dot(hidden_low, up_full, preferred_element_type=jnp.float32)
    active, gelu_pull = jax.vjp(gelu_exact, pre_act)
    active_low = (active * unit_gate).astype(jnp.bfloat16)
    branch = contract_cols(active_low, down_full)
    output = (hidden + layer_gates[1] * branch).astype(jnp.bfloat16)
    back_rounded = (layer_gates[1] * back_full).astype(jnp.bfloat16)
    qkv_full, out_full, up_full, down_full = (
        lax.all_gather(qkv_weight, "mp", axis=0, tiled=True),
        lax.all_gather(out_weight, "mp", axis=0, tiled=True),
        lax.all_gather(up_weight, "mp", axis=1, tiled=True),
        lax.all_gather(down_weight, "mp", axis=1, tiled=True),
    )
    grad_active = jnp.dot(back_rounded, down_full, preferred_element_type=jnp.float32)
    unit_grad = jnp.sum(grad_active * active, axis=0)
    grad_inner = gelu_pull(grad_active * unit_gate)[0].astype(jnp.bfloat16)
    hidden_back = contract_cols(grad_inner, up_full)
    up_term = contract_rows(grad_inner, hidden_low)
    down_term = contract_rows(active_low, back_rounded)
    unit_local = (
        lax.psum_scatter(
            jnp.stack([up_term, down_term], axis=1).astype(jnp.bfloat16),
            "mp",
            scatter_dimension=0,
            tiled=True,
        )
        .astype(jnp.float32)
        .transpose(1, 2, 0)
    )
    summed_grad, gain_grad, bias_grad, mask_grad = norm_pull(back_full + hidden_back)
    layer_grad = jnp.stack([jnp.sum(summed_grad * attn_out), jnp.sum(back_full * branch)])
    out_back = (layer_gates[0] * summed_grad).astype(jnp.bfloat16)
    gated_grad = contract_cols(out_back, out_full).astype(jnp.bfloat16)
    gated_heads = gated_grad.reshape(row_count, head_count, head_width)
    head_grad = jnp.sum(context * gated_heads.astype(jnp.float32), axis=(0, 2))
    context_grad = gated_heads * head_mask.astype(jnp.bfloat16)[None, :, None]
    joined_grad = lax.map(
        partial(attend_backward, head_count=head_count, factor=factor),
        (
            joined_blocks,
            log_totals,
            context_grad.reshape(block_count, block_rows, head_count, head_width),
            segments,
        ),
    )
    joined_grad = joined_grad.reshape(row_count, 3 * width)
    input_grad = summed_grad + contract_cols(joined_grad, qkv_full)
    tiles = width // SB
    qkv_term = jnp.einsum(
        "tri,tcj->rcij",
        tokens.reshape(row_count, tiles, SB),
        joined_grad.reshape(row_count, 3 * tiles, SB),
        preferred_element_type=jnp.float32,
    )
    out_term = jnp.einsum(
        "tri,tcj->rcij",
        gated_low.reshape(row_count, tiles, SB),
        out_back.reshape(row_count, tiles, SB),
        preferred_element_type=jnp.float32,
    )
    attn_terms = jnp.concatenate(
        [
            qkv_term.reshape(-1, model_size, part_rows, SB),
            out_term.reshape(-1, model_size, part_rows, SB),
        ],
        axis=0,
    )
    attn_rows = (
        lax.psum_scatter(attn_terms.astype(jnp.bfloat16), "mp", scatter_dimension=1, tiled=True)
        .astype(jnp.float32)
        .reshape(-1, part_rows, SB)
    )
    unit_split = unit_local.reshape(2, tiles, model_size, part_rows, share)
    unit_rows = lax.all_to_all(
        unit_split.astype(jnp.bfloat16), "mp", split_axis=2, concat_axis=4, tiled=True
    ).astype(unit_split.dtype)
    unit_rows = (
        unit_rows.reshape(2, tiles, part_rows, FF // SB, SB)
        .transpose(0, 1, 3, 2, 4)
        .reshape(-1, part_rows, SB)
    )
    all_rows = jnp.concatenate([attn_rows, unit_rows], axis=0)
    slot_count = owner_slot.shape[0]
    pick = (owner_slot[None, :] == jnp.arange(slot_count)[:, None]).astype(jnp.bfloat16)
    flat_rows = all_rows.astype(jnp.bfloat16).reshape(slot_count, -1)
    slotted = jnp.dot(pick, flat_rows, preferred_element_type=jnp.float32).reshape(all_rows.shape)
    owned = lax.psum_scatter(
        slotted.astype(jnp.bfloat16), "dp", scatter_dimension=0, tiled=True
    ).astype(jnp.float32)
    full_grad = lax.all_gather(owned.astype(jnp.bfloat16), "mp", axis=1, tiled=True).astype(
        owned.dtype
    )
    row_start = lax.axis_index("mp") * part_rows
    columns = lax.dynamic_slice_in_dim(full_grad, row_start, part_rows, 2)
    left_new = BETA * left_stats + (1.0 - BETA) * jnp.einsum(
        "srj,skj->srk", owned, full_grad, precision=HIGH
    )
    right_new = BETA * right_stats + (1.0 - BETA) * jnp.einsum(
        "sjr,sjk->srk", columns, full_grad, precision=HIGH
    )
    left_part = jnp.einsum("sri,sij->srj", left_root, full_grad, precision=HIGH)
    update = jnp.einsum("srj,sjk->srk", left_part, right_root, precision=HIGH)
    weight_new = master - RATE * update
    norm_grad = jnp.stack([gain_grad, bias_grad])
    norm_grad, mask_grad, head_grad, layer_grad, unit_grad = lax.psum(
        (norm_grad, mask_grad, head_grad, layer_grad, unit_grad), ("dp", "mp")
    )
    norm_new = jnp.stack([norm_gain, norm_bias]) - 0.2 / math.sqrt(total_tokens) * norm_grad
    return (
        output,
        input_grad,
        head_grad,
        unit_grad,
        mask_grad,
        layer_grad,
        norm_grad,
        norm_new,
        owned,
        left_new,
        right_new,
        weight_new,
        weight_new.astype(jnp.bfloat16),
    )


F32 = jnp.float32
BF = jnp.bfloat16
MESH = pl.DeviceIdType.MESH
LOG2E = 1.4426950408889634
ROWS = 1024
D = 768
HD = 64
BLK = 512
NT_DIMS = (((1,), (1,)), ((), ()))
NN_DIMS = (((1,), (0,)), ((), ()))


def nn(left, right):
    return lax.dot_general(left, right, NN_DIMS, preferred_element_type=F32)


def nt(left, right):
    return lax.dot_general(left, right, NT_DIMS, preferred_element_type=F32)


def coords():
    d = lax.axis_index("dp")
    m = lax.axis_index("mp")
    return d // 2, d % 2, m // 2, m % 2


def at(z, x, y, c):
    return (2 * z + x, 2 * y + c)


def gelu_parts(x):
    ax = jnp.abs(x)
    e = jnp.exp2(x * x * (-0.5 * LOG2E))
    t = 1.0 / (1.0 + (0.3275911 * math.sqrt(0.5)) * ax)
    poly = t * (
        0.5 * 0.254829592
        + t
        * (
            -0.5 * 0.284496736
            + t * (0.5 * 1.421413741 + t * (-0.5 * 1.453152027 + t * (0.5 * 1.061405429)))
        )
    )
    tail = poly * e
    cdf = jnp.where(x < 0, tail, 1.0 - tail)
    active = x * cdf
    return active, cdf + x * (e * (1.0 / math.sqrt(2.0 * math.pi)))


def colsum(v):
    return jnp.sum(v, axis=0, keepdims=True)


def row_norm(summed):
    centre = summed - jnp.mean(summed, axis=-1, keepdims=True)
    spread = jnp.mean(centre * centre, axis=-1, keepdims=True)
    inv = lax.rsqrt(spread + EPS)
    return centre * inv, inv


NPIECE = 6


def forward_kernel(
    gates,
    tokens,
    cot,
    segcol,
    segrow,
    hgate,
    ugate,
    mgate,
    gain,
    bias,
    qkv_in,
    out_in,
    up_in,
    down_in,
    o_out,
    o_joined,
    o_ctx,
    o_ctxT,
    o_tokT,
    o_sgrad,
    o_grad,
    o_wq,
    o_wo,
    lse,
    small,
    wq,
    wo,
    wu,
    wd,
    joined,
    ctx,
    ctxT,
    tokT,
    attn,
    hlow,
    hT,
    blow,
    bT,
    branch,
    hback,
    act,
    inner,
    grads,
    outv,
    send_sem,
    recv_sem,
    loc_sem,
    out_sem,
    grad_sem,
):
    z, x, y, c = coords()
    m = 2 * y + c
    ms = 2 * y + 1 - c
    my = 2 * (1 - y) + c
    mys = 2 * (1 - y) + 1 - c
    sib = at(z, x, y, 1 - c)
    ypeer = at(z, x, 1 - y, c)
    xpeer = at(z, 1 - x, y, c)
    g0 = gates[0]
    g1 = gates[1]

    barrier = pltpu.get_barrier_semaphore()
    for peer in (sib, ypeer, xpeer):
        pl.semaphore_signal(barrier, inc=1, device_id=peer, device_id_type=MESH)
    pl.semaphore_wait(barrier, 3)

    def full(j, i, h=None):
        if j < 3:
            ref, n, cols = wq, 192, pl.ds(768 * j, 768)
        else:
            ref, n, cols = ((wo, 192), (wu, 768), (wd, 768))[j - 3] + (slice(None),)
        if h is None:
            return ref.at[i, :, cols]
        return ref.at[i, pl.ds(pl.multiple_of(h * (n // 2), 16), n // 2), cols]

    def own(j, h=None):
        if j < 3:
            ref, n, cols = qkv_in, 192, pl.ds(768 * j, 768)
        else:
            ref, n, cols = ((out_in, 192), (up_in, 768), (down_in, 768))[j - 3] + (slice(None),)
        if h is None:
            return ref.at[:, cols]
        return ref.at[pl.ds(pl.multiple_of(h * (n // 2), 16), n // 2), cols]

    def remote(src, dst, j, k, dev):
        return pltpu.make_async_remote_copy(
            src_ref=src,
            dst_ref=dst,
            send_sem=send_sem.at[j, k],
            recv_sem=recv_sem.at[j, k],
            device_id=dev,
            device_id_type=MESH,
        )

    def s1(j):
        return remote(own(j), full(j, m), j, 0, sib)

    def s2(j):
        return remote(own(j, x), full(j, m, x), j, 1, ypeer)

    def s3(j):
        return remote(full(j, my, x), full(j, my, x), j, 2, xpeer)

    def s4(j):
        return remote(full(j, my, x), full(j, my, x), j, 3, sib)

    def s5(j):
        return remote(full(j, my, 1 - x), full(j, my, 1 - x), j, 4, sib)

    def local(j):
        return pltpu.make_async_copy(own(j), full(j, m), loc_sem.at[j])

    def first(j):
        s2(j).start()
        s1(j).start()
        local(j).start()

    def second(j):
        s2(j).wait_recv()
        s3(j).start()
        s4(j).start()

    def third(j):
        s3(j).wait_recv()
        s5(j).start()

    def finish_near(j):
        local(j).wait()
        s1(j).wait_recv()

    def finish_far(j):
        s4(j).wait_recv()
        s5(j).wait_recv()

    def finish_sends(j):
        for s in (s1, s2, s3, s4, s5):
            s(j).wait_send()

    for j in range(3):
        first(j)

    tokT[...] = tokens[...].T
    tok_copy = pltpu.make_async_copy(tokT, o_tokT, out_sem.at[0])
    tok_copy.start()

    @pl.loop(0, 4)
    def _(r):
        rows = pl.ds(pl.multiple_of(r * 256, 256), 256)
        low = (g1 * cot[rows, :].astype(F32)).astype(BF)
        blow[rows, :] = low
        bT[:, rows] = low.T

    second(0)
    second(1)
    third(0)
    second(2)
    third(1)
    third(2)
    for j in range(3, NPIECE):
        first(j)
    for j in range(3):
        finish_near(j)
        finish_far(j)
    wq_copy = pltpu.make_async_copy(wq, o_wq, out_sem.at[1])
    wq_copy.start()

    for j in range(3):

        @pl.loop(0, 4)
        def _(r, j=j):
            rows = pl.ds(pl.multiple_of(r * 256, 256), 256)
            w = wq[:, :, pl.ds(768 * j, 768)].reshape(D, D)
            joined[rows, pl.ds(768 * j, 768)] = nn(tokens[rows, :], w).astype(BF)

    joined_copy = pltpu.make_async_copy(joined, o_joined, out_sem.at[2])
    joined_copy.start()

    scale = LOG2E / math.sqrt(HD)
    half_iota = lax.broadcasted_iota(jnp.int32, (1, 128), 1) // HD
    halves = [(half_iota == e).astype(F32).astype(BF) for e in range(2)]

    def attend(i):
        b = i // 6
        p = i % 6
        rows = pl.ds(pl.multiple_of(b * BLK, BLK), BLK)
        lane = pl.multiple_of(p * 128, 128)
        q = joined[rows, pl.ds(lane, 128)]
        k = joined[rows, pl.ds(D + lane, 128)]
        v = joined[rows, pl.ds(2 * D + lane, 128)]
        sc = segcol[b]
        sr = segrow[b]
        for qt in range(2):
            cols = slice(qt * 256, qt * 256 + 256)
            allowed = sc == sr[:, cols]
            total = None
            for e in range(2):
                s = nt(k * halves[e], q[cols, :])
                s = jnp.where(allowed, s * scale, MASKED)
                top = jnp.max(s, axis=0, keepdims=True)
                pr = jnp.exp2(s - top)
                tot = jnp.sum(pr, axis=0, keepdims=True)
                low = (pr * (1.0 / tot)).astype(BF)
                lse[2 * i + e, :, pl.ds(qt * 256, 256)] = top + jnp.log(tot) * LOG2E
                part = nn((v * halves[e]).T, low)
                total = part if total is None else total + part
            qrows = pl.ds(pl.multiple_of(b * BLK + qt * 256, 256), 256)
            ctxT[pl.ds(lane, 128), qrows] = total.astype(BF)
            ctx[qrows, pl.ds(lane, 128)] = total.T.astype(BF)

    pl.loop(0, 3)(attend)
    second(3)
    pl.loop(3, 5)(attend)
    third(3)
    pl.loop(5, 10)(attend)
    second(4)
    pl.loop(10, 12)(attend)
    ctx_copy = pltpu.make_async_copy(ctx, o_ctx, out_sem.at[3])
    ctx_copy.start()
    ctxT_copy = pltpu.make_async_copy(ctxT, o_ctxT, out_sem.at[4])
    ctxT_copy.start()
    finish_near(3)
    finish_far(3)
    wo_copy = pltpu.make_async_copy(wo, o_wo, out_sem.at[5])
    wo_copy.start()

    @pl.loop(0, 4)
    def _(r):
        rows = pl.ds(pl.multiple_of(r * 256, 256), 256)
        gated = ctx[rows, :] * hgate[...].astype(BF)
        a = nn(gated, wo[...].reshape(D, D))
        attn[rows, :] = a
        normed, _ = row_norm(tokens[rows, :].astype(F32) + g0 * a)
        low = ((normed * gain[...] + bias[...]) * mgate[...]).astype(BF)
        hlow[rows, :] = low
        hT[:, rows] = low.T

    third(4)
    second(5)

    small[...] = jnp.zeros_like(small)

    def feed(u, begin, slot):
        if not begin:
            pass
        w_up = wu.at[u]
        w_down = wd.at[u]

        @pl.loop(0, 4)
        def _(r):
            rows = pl.ds(pl.multiple_of(r * 256, 256), 256)
            pre = nn(hlow[rows, :], w_up[...])
            back = nn(blow[rows, :], w_down[...])
            active, slope = gelu_parts(pre)
            gate = ugate[u]
            small[pl.ds(u, 1), :] += colsum(back * active)
            a_low = (active * gate).astype(BF)
            i_low = (back * gate * slope).astype(BF)
            act[rows, :] = a_low
            inner[rows, :] = i_low
            up_part = nt(a_low, w_down[...])
            back_part = nt(i_low, w_up[...])
            if begin:
                branch[rows, :] = up_part
                hback[rows, :] = back_part
            else:
                branch[rows, :] += up_part
                hback[rows, :] += back_part

        for which, (left, right) in enumerate(((hT, inner), (bT, act))):

            @pl.loop(0, 8)
            def _(t, which=which, left=left, right=right):
                rr = pl.ds(pl.multiple_of(t * 96, 16), 96)
                g = nn(left[rr, :], right[...]).astype(BF)
                for j in range(2):
                    for h in range(2):
                        grads[slot, which, t // 4, j, t % 4 * 2 + h] = g[
                            48 * h : 48 * h + 48, 384 * j : 384 * j + 384
                        ]

    def grad_copies(u, slot):
        found = []
        for which in range(2):
            for r in range(2):
                found.append(
                    pltpu.make_async_copy(
                        grads.at[slot, which, r],
                        o_grad.at[which, r, pl.ds(2 * u, 2)],
                        grad_sem.at[slot, which, r],
                    )
                )
        return found

    finish_near(4)
    finish_near(5)
    feed(m, True, 0)
    for g in grad_copies(m, 0):
        g.start()
    third(5)
    feed(ms, False, 1)
    for g in grad_copies(ms, 1):
        g.start()
    finish_far(4)
    finish_far(5)
    for g in grad_copies(m, 0):
        g.wait()
    feed(my, False, 0)
    for g in grad_copies(my, 0):
        g.start()
    for g in grad_copies(ms, 1):
        g.wait()
    feed(mys, False, 1)
    for g in grad_copies(mys, 1):
        g.start()

    lane = lax.broadcasted_iota(jnp.int32, (1, D), 1)

    @pl.loop(0, 4)
    def _(r):
        rows = pl.ds(pl.multiple_of(r * 256, 256), 256)
        a = attn[rows, :]
        normed, inv = row_norm(tokens[rows, :].astype(F32) + g0 * a)
        plain = normed * gain[...] + bias[...]
        back = cot[rows, :].astype(F32)
        br = branch[rows, :]
        outv[rows, :] = (plain * mgate[...] + g1 * br).astype(BF)
        total = back + hback[rows, :]
        masked = total * mgate[...]
        small[4:5, :] += colsum(masked * normed)
        small[5:6, :] += colsum(masked)
        small[6:7, :] += colsum(total * plain)
        n = masked * gain[...]
        grad = (
            n
            - jnp.mean(n, axis=-1, keepdims=True)
            - normed * jnp.mean(n * normed, axis=-1, keepdims=True)
        ) * inv
        hback[rows, :] = grad
        small[7:8, :] += colsum(grad * a)
        small[8:9, :] += colsum(back * br)

    out_copy = pltpu.make_async_copy(outv, o_out, out_sem.at[6])
    out_copy.start()
    sgrad_copy = pltpu.make_async_copy(hback, o_sgrad, out_sem.at[7])
    sgrad_copy.start()
    for g in grad_copies(my, 0):
        g.wait()
    for g in grad_copies(mys, 1):
        g.wait()
    for copy in (tok_copy, wq_copy, joined_copy, ctx_copy, ctxT_copy, wo_copy, out_copy, sgrad_copy):
        copy.wait()
    for j in range(NPIECE):
        finish_sends(j)


def run_forward(gates, tokens, cot, segcol, segrow, hgate, ugate, mgate, gain, bias, qkv, out, up, down):
    sds = jax.ShapeDtypeStruct
    outs = (
        sds((ROWS, D), BF),
        sds((ROWS, 3 * D), BF),
        sds((ROWS, D), BF),
        sds((D, ROWS), BF),
        sds((D, ROWS), BF),
        sds((ROWS, D), F32),
        sds((2, 2, 8, 8, 48, SB), BF),
        sds((4, 192, 3 * D), BF),
        sds((4, 192, D), BF),
        sds((24, 1, BLK), F32),
        sds((16, D), F32),
    )
    any_ = pl.BlockSpec(memory_space=pl.ANY)
    vm = pl.BlockSpec(memory_space=pltpu.VMEM)
    sm = pl.BlockSpec(memory_space=pltpu.SMEM)
    return pl.pallas_call(
        forward_kernel,
        out_shape=outs,
        in_specs=[sm] + [vm] * 9 + [any_] * 4,
        out_specs=[any_] * 9 + [vm] * 2,
        scratch_shapes=[
            pltpu.VMEM((4, 192, 3 * D), BF),
            pltpu.VMEM((4, 192, D), BF),
            pltpu.VMEM((4, D, D), BF),
            pltpu.VMEM((4, D, D), BF),
            pltpu.VMEM((ROWS, 3 * D), BF),
            pltpu.VMEM((ROWS, D), BF),
            pltpu.VMEM((D, ROWS), BF),
            pltpu.VMEM((D, ROWS), BF),
            pltpu.VMEM((ROWS, D), F32),
            pltpu.VMEM((ROWS, D), BF),
            pltpu.VMEM((D, ROWS), BF),
            pltpu.VMEM((ROWS, D), BF),
            pltpu.VMEM((D, ROWS), BF),
            pltpu.VMEM((ROWS, D), F32),
            pltpu.VMEM((ROWS, D), F32),
            pltpu.VMEM((ROWS, D), BF),
            pltpu.VMEM((ROWS, D), BF),
            pltpu.VMEM((2, 2, 2, 2, 8, 48, SB), BF),
            pltpu.VMEM((ROWS, D), BF),
            pltpu.SemaphoreType.DMA((NPIECE, 5)),
            pltpu.SemaphoreType.DMA((NPIECE, 5)),
            pltpu.SemaphoreType.DMA((NPIECE,)),
            pltpu.SemaphoreType.DMA((8,)),
            pltpu.SemaphoreType.DMA((2, 2, 2)),
        ],
        compiler_params=pltpu.CompilerParams(
            collective_id=1, has_side_effects=True, vmem_limit_bytes=64 << 20
        ),
    )(gates, tokens, cot, segcol, segrow, hgate, ugate, mgate, gain, bias, qkv, out, up, down)


def fast_body(
    tokens,
    segments,
    head_mask,
    unit_mask,
    hidden_mask,
    layer_gates,
    qkv_weight,
    out_weight,
    norm_gain,
    norm_bias,
    up_weight,
    down_weight,
    cotangent,
    owner_slot,
    master,
    left_stats,
    right_stats,
    left_root,
    right_root,
):
    segcol = segments[:, :, None]
    segrow = segments[:, None, :]
    head_lanes = jnp.repeat(head_mask.astype(F32), HD)
    hgate = head_lanes[None]
    ugate = unit_mask.astype(F32).reshape(4, 1, D)
    mgate = hidden_mask.astype(F32)[None]
    (output, joined, ctx, ctxT, tokT, summed_grad, ff_grad, wq, wo, lse, small) = run_forward(
        layer_gates,
        tokens,
        cotangent,
        segcol,
        segrow,
        hgate,
        ugate,
        mgate,
        norm_gain[None],
        norm_bias[None],
        qkv_weight,
        out_weight,
        up_weight,
        down_weight,
    )
    factor = 1.0 / math.sqrt(HD)
    qkv_full = wq.reshape(D, 3 * D)
    out_full = wo.reshape(D, D)
    out_back = (layer_gates[0] * summed_grad).astype(BF)
    gated_grad = contract_cols(out_back, out_full).astype(BF)
    head_row = jnp.sum(ctx.astype(F32) * gated_grad.astype(F32), axis=0)
    context_grad = (gated_grad * hgate.astype(BF)).reshape(2, BLK, 12, HD)
    log_totals = lse.reshape(2, 12, BLK) * math.log(2.0)
    joined_grad = jax.vmap(partial(attend_backward, head_count=12, factor=factor))(
        (joined.reshape(2, BLK, 3 * D), log_totals, context_grad, segments)
    ).reshape(ROWS, 3 * D)
    input_grad = summed_grad + contract_cols(joined_grad, qkv_full)
    qkv_term = jnp.dot(tokT, joined_grad, preferred_element_type=F32).astype(BF)
    out_term = jnp.dot(ctxT, out_back, preferred_element_type=F32) * head_lanes[:, None]
    out_term = out_term.astype(BF)
    tile = lambda v: v.reshape(2, SB, -1, SB).transpose(0, 2, 1, 3).reshape(-1, SB, SB)
    blocks = jnp.concatenate([tile(qkv_term), tile(out_term), ff_grad.reshape(32, SB, SB)], axis=0)
    small = small.at[9].set(head_row)
    rows = lax.psum_scatter(
        blocks.reshape(48, 4, 96, SB), "mp", scatter_dimension=1, tiled=True
    ).reshape(48, 96, SB)
    pick = (owner_slot[None, :] == jnp.arange(48)[:, None]).astype(BF)
    slotted = jnp.dot(pick, rows.reshape(48, -1), preferred_element_type=F32).astype(BF)
    owned = lax.psum_scatter(
        slotted.reshape(48, 96, SB), "dp", scatter_dimension=0, tiled=True
    )
    full_grad = lax.all_gather(owned, "mp", axis=1, tiled=True).astype(F32)
    owned = owned.astype(F32)
    columns = lax.dynamic_slice_in_dim(full_grad, lax.axis_index("mp") * 96, 96, 2)
    left_new = BETA * left_stats + (1.0 - BETA) * jnp.einsum(
        "srj,skj->srk", owned, full_grad, precision=HIGH
    )
    right_new = BETA * right_stats + (1.0 - BETA) * jnp.einsum(
        "sjr,sjk->srk", columns, full_grad, precision=HIGH
    )
    left_part = jnp.einsum("sri,sij->srj", left_root, full_grad, precision=HIGH)
    update = jnp.einsum("srj,sjk->srk", left_part, right_root, precision=HIGH)
    weight_new = master - RATE * update
    small = lax.psum(small, ("dp", "mp"))
    unit_grad = small[:4].reshape(-1)
    norm_grad = small[4:6]
    mask_grad = small[6]
    layer_grad = jnp.sum(small[7:9], axis=1)
    head_grad = jnp.sum(small[9].reshape(12, HD), axis=1)
    norm_new = jnp.stack([norm_gain, norm_bias]) - 0.2 / math.sqrt(ROWS * 32) * norm_grad
    return (
        output,
        input_grad,
        head_grad,
        unit_grad,
        mask_grad,
        layer_grad,
        norm_grad,
        norm_new,
        owned,
        left_new,
        right_new,
        weight_new,
        weight_new.astype(BF),
    )


def solution(mesh):
    return jax.shard_map(
        fast_body if dict(mesh.shape) == {"dp": 8, "mp": 4} else body,
        mesh=mesh,
        in_specs=(
            P(("dp", "mp"), None),
            P(("dp", "mp"), None),
            P(),
            P(),
            P(),
            P(),
            P("mp", None),
            P("mp", None),
            P(),
            P(),
            P(None, "mp"),
            P(None, "mp"),
            P(("dp", "mp"), None),
            P(),
            P("dp", "mp", None),
            P("dp", "mp", None),
            P("dp", "mp", None),
            P("dp", "mp", None),
            P("dp", None, None),
        ),
        out_specs=(
            P(("dp", "mp"), None),
            P(("dp", "mp"), None),
            P(),
            P(),
            P(),
            P(),
            P(),
            P(),
            P("dp", "mp", None),
            P("dp", "mp", None),
            P("dp", "mp", None),
            P("dp", "mp", None),
            P("dp", "mp", None),
        ),
        check_vma=False,
    )
```

```python
from functools import partial
import math

import jax
import jax.numpy as jnp
from jax import lax
from jax.experimental import pallas as pl
from jax.experimental.pallas import tpu as pltpu
from jax.sharding import PartitionSpec as P

FF = 3072
SB = 384


HIGH = lax.Precision.HIGHEST
BETA = 0.5
RATE = 0.5
EPS = 1e-12
MASKED = -1e30


def gelu_exact(values):
    return jax.nn.gelu(values, approximate=False)


def normalize(summed, gain_in, offset, hidden_gate):
    centre = summed - jnp.mean(summed, axis=-1, keepdims=True)
    spread = jnp.mean(centre * centre, axis=-1, keepdims=True)
    return (centre * lax.rsqrt(spread + EPS) * gain_in + offset) * hidden_gate


def split_heads(block_joined, head_count):
    pieces = block_joined.reshape(block_joined.shape[0], 3, head_count, -1)
    return (pieces[:, 0], pieces[:, 1], pieces[:, 2])


def masked_scores(queries, keys_in, labels, factor):
    scores = (
        jnp.einsum("qhd,khd->hqk", queries, keys_in, preferred_element_type=jnp.float32) * factor
    )
    allowed = labels[:, None] == labels[None, :]
    return jnp.where(allowed[None], scores, MASKED)


def attend_forward(packed, head_count, factor):
    block_joined, labels = packed
    queries, keys_in, values_in = split_heads(block_joined, head_count)
    scores = masked_scores(queries, keys_in, labels, factor)
    highest = jnp.max(scores, axis=-1, keepdims=True)
    raised = jnp.exp(scores - highest)
    totals = jnp.sum(raised, axis=-1, keepdims=True)
    weights_low = (raised / totals).astype(jnp.bfloat16)
    context = jnp.einsum("hqk,khd->qhd", weights_low, values_in, preferred_element_type=jnp.float32)
    return (context, (highest + jnp.log(totals))[:, :, 0])


def attend_backward(packed, head_count, factor):
    block_joined, log_totals, context_grad, labels = packed
    queries, keys_in, values_in = split_heads(block_joined, head_count)
    scores = masked_scores(queries, keys_in, labels, factor)
    weights_full = jnp.exp(scores - log_totals[:, :, None])
    weights_low = weights_full.astype(jnp.bfloat16)
    values_grad = jnp.einsum(
        "hqk,qhd->khd", weights_low, context_grad, preferred_element_type=jnp.float32
    )
    weights_grad = jnp.einsum(
        "qhd,khd->hqk", context_grad, values_in, preferred_element_type=jnp.float32
    )
    inner_sum = jnp.sum(weights_full * weights_grad, axis=-1, keepdims=True)
    scores_grad = (weights_full * (weights_grad - inner_sum)).astype(jnp.bfloat16)
    queries_grad = (
        jnp.einsum("hqk,khd->qhd", scores_grad, keys_in, preferred_element_type=jnp.float32)
        * factor
    )
    keys_grad = (
        jnp.einsum("hqk,qhd->khd", scores_grad, queries, preferred_element_type=jnp.float32)
        * factor
    )
    merged = jnp.concatenate([queries_grad, keys_grad, values_grad], axis=1)
    return merged.reshape(merged.shape[0], -1).astype(jnp.bfloat16)


def contract_rows(left, right):
    return lax.dot_general(
        left, right, (((0,), (0,)), ((), ())), preferred_element_type=jnp.float32
    )


def contract_cols(left, right):
    return lax.dot_general(
        left, right, (((1,), (1,)), ((), ())), preferred_element_type=jnp.float32
    )


def body(
    tokens,
    segments,
    head_mask,
    unit_mask,
    hidden_mask,
    layer_gates,
    qkv_weight,
    out_weight,
    norm_gain,
    norm_bias,
    up_weight,
    down_weight,
    cotangent,
    owner_slot,
    master,
    left_stats,
    right_stats,
    left_root,
    right_root,
):
    row_count = tokens.shape[0]
    width = tokens.shape[1]
    head_count = head_mask.shape[0]
    head_width = width // head_count
    block_rows = segments.shape[1]
    block_count = segments.shape[0]
    factor = 1.0 / math.sqrt(head_width)
    model_size = lax.axis_size("mp")
    share = FF // model_size
    part_rows = SB // model_size
    total_tokens = row_count * lax.axis_size("dp") * model_size
    head_gate = head_mask.astype(jnp.float32)
    unit_gate = unit_mask.astype(jnp.float32)
    hidden_gate = hidden_mask.astype(jnp.float32)
    inputs = tokens.astype(jnp.float32)
    back_full = cotangent.astype(jnp.float32)
    qkv_full, out_full, up_full, down_full = (
        lax.all_gather(qkv_weight, "mp", axis=0, tiled=True),
        lax.all_gather(out_weight, "mp", axis=0, tiled=True),
        lax.all_gather(up_weight, "mp", axis=1, tiled=True),
        lax.all_gather(down_weight, "mp", axis=1, tiled=True),
    )
    joined_qkv = jnp.dot(tokens, qkv_full, preferred_element_type=jnp.float32).astype(jnp.bfloat16)
    joined_blocks = joined_qkv.reshape(block_count, block_rows, 3 * width)
    context, log_totals = lax.map(
        partial(attend_forward, head_count=head_count, factor=factor), (joined_blocks, segments)
    )
    context = context.reshape(row_count, head_count, head_width)
    gated_low = (context * head_gate[None, :, None]).reshape(row_count, width).astype(jnp.bfloat16)
    attn_out = jnp.dot(gated_low, out_full, preferred_element_type=jnp.float32)
    summed = inputs + layer_gates[0] * attn_out
    hidden, norm_pull = jax.vjp(normalize, summed, norm_gain, norm_bias, hidden_gate)
    hidden_low = hidden.astype(jnp.bfloat16)
    pre_act = jnp.dot(hidden_low, up_full, preferred_element_type=jnp.float32)
    active, gelu_pull = jax.vjp(gelu_exact, pre_act)
    active_low = (active * unit_gate).astype(jnp.bfloat16)
    branch = contract_cols(active_low, down_full)
    output = (hidden + layer_gates[1] * branch).astype(jnp.bfloat16)
    back_rounded = (layer_gates[1] * back_full).astype(jnp.bfloat16)
    qkv_full, out_full, up_full, down_full = (
        lax.all_gather(qkv_weight, "mp", axis=0, tiled=True),
        lax.all_gather(out_weight, "mp", axis=0, tiled=True),
        lax.all_gather(up_weight, "mp", axis=1, tiled=True),
        lax.all_gather(down_weight, "mp", axis=1, tiled=True),
    )
    grad_active = jnp.dot(back_rounded, down_full, preferred_element_type=jnp.float32)
    unit_grad = jnp.sum(grad_active * active, axis=0)
    grad_inner = gelu_pull(grad_active * unit_gate)[0].astype(jnp.bfloat16)
    hidden_back = contract_cols(grad_inner, up_full)
    up_term = contract_rows(grad_inner, hidden_low)
    down_term = contract_rows(active_low, back_rounded)
    unit_local = (
        lax.psum_scatter(
            jnp.stack([up_term, down_term], axis=1).astype(jnp.bfloat16),
            "mp",
            scatter_dimension=0,
            tiled=True,
        )
        .astype(jnp.float32)
        .transpose(1, 2, 0)
    )
    summed_grad, gain_grad, bias_grad, mask_grad = norm_pull(back_full + hidden_back)
    layer_grad = jnp.stack([jnp.sum(summed_grad * attn_out), jnp.sum(back_full * branch)])
    out_back = (layer_gates[0] * summed_grad).astype(jnp.bfloat16)
    gated_grad = contract_cols(out_back, out_full).astype(jnp.bfloat16)
    gated_heads = gated_grad.reshape(row_count, head_count, head_width)
    head_grad = jnp.sum(context * gated_heads.astype(jnp.float32), axis=(0, 2))
    context_grad = gated_heads * head_mask.astype(jnp.bfloat16)[None, :, None]
    joined_grad = lax.map(
        partial(attend_backward, head_count=head_count, factor=factor),
        (
            joined_blocks,
            log_totals,
            context_grad.reshape(block_count, block_rows, head_count, head_width),
            segments,
        ),
    )
    joined_grad = joined_grad.reshape(row_count, 3 * width)
    input_grad = summed_grad + contract_cols(joined_grad, qkv_full)
    tiles = width // SB
    qkv_term = jnp.einsum(
        "tri,tcj->rcij",
        tokens.reshape(row_count, tiles, SB),
        joined_grad.reshape(row_count, 3 * tiles, SB),
        preferred_element_type=jnp.float32,
    )
    out_term = jnp.einsum(
        "tri,tcj->rcij",
        gated_low.reshape(row_count, tiles, SB),
        out_back.reshape(row_count, tiles, SB),
        preferred_element_type=jnp.float32,
    )
    attn_terms = jnp.concatenate(
        [
            qkv_term.reshape(-1, model_size, part_rows, SB),
            out_term.reshape(-1, model_size, part_rows, SB),
        ],
        axis=0,
    )
    attn_rows = (
        lax.psum_scatter(attn_terms.astype(jnp.bfloat16), "mp", scatter_dimension=1, tiled=True)
        .astype(jnp.float32)
        .reshape(-1, part_rows, SB)
    )
    unit_split = unit_local.reshape(2, tiles, model_size, part_rows, share)
    unit_rows = lax.all_to_all(
        unit_split.astype(jnp.bfloat16), "mp", split_axis=2, concat_axis=4, tiled=True
    ).astype(unit_split.dtype)
    unit_rows = (
        unit_rows.reshape(2, tiles, part_rows, FF // SB, SB)
        .transpose(0, 1, 3, 2, 4)
        .reshape(-1, part_rows, SB)
    )
    all_rows = jnp.concatenate([attn_rows, unit_rows], axis=0)
    slot_count = owner_slot.shape[0]
    pick = (owner_slot[None, :] == jnp.arange(slot_count)[:, None]).astype(jnp.bfloat16)
    flat_rows = all_rows.astype(jnp.bfloat16).reshape(slot_count, -1)
    slotted = jnp.dot(pick, flat_rows, preferred_element_type=jnp.float32).reshape(all_rows.shape)
    owned = lax.psum_scatter(
        slotted.astype(jnp.bfloat16), "dp", scatter_dimension=0, tiled=True
    ).astype(jnp.float32)
    full_grad = lax.all_gather(owned.astype(jnp.bfloat16), "mp", axis=1, tiled=True).astype(
        owned.dtype
    )
    row_start = lax.axis_index("mp") * part_rows
    columns = lax.dynamic_slice_in_dim(full_grad, row_start, part_rows, 2)
    left_new = BETA * left_stats + (1.0 - BETA) * jnp.einsum(
        "srj,skj->srk", owned, full_grad, precision=HIGH
    )
    right_new = BETA * right_stats + (1.0 - BETA) * jnp.einsum(
        "sjr,sjk->srk", columns, full_grad, precision=HIGH
    )
    left_part = jnp.einsum("sri,sij->srj", left_root, full_grad, precision=HIGH)
    update = jnp.einsum("srj,sjk->srk", left_part, right_root, precision=HIGH)
    weight_new = master - RATE * update
    norm_grad = jnp.stack([gain_grad, bias_grad])
    norm_grad, mask_grad, head_grad, layer_grad, unit_grad = lax.psum(
        (norm_grad, mask_grad, head_grad, layer_grad, unit_grad), ("dp", "mp")
    )
    norm_new = jnp.stack([norm_gain, norm_bias]) - 0.2 / math.sqrt(total_tokens) * norm_grad
    return (
        output,
        input_grad,
        head_grad,
        unit_grad,
        mask_grad,
        layer_grad,
        norm_grad,
        norm_new,
        owned,
        left_new,
        right_new,
        weight_new,
        weight_new.astype(jnp.bfloat16),
    )


F32 = jnp.float32
BF = jnp.bfloat16
MESH = pl.DeviceIdType.MESH
LOG2E = 1.4426950408889634
ROWS = 1024
D = 768
HD = 64
BLK = 512
NT_DIMS = (((1,), (1,)), ((), ()))
NN_DIMS = (((1,), (0,)), ((), ()))


def nn(left, right):
    return lax.dot_general(left, right, NN_DIMS, preferred_element_type=F32)


def nt(left, right):
    return lax.dot_general(left, right, NT_DIMS, preferred_element_type=F32)


def coords():
    d = lax.axis_index("dp")
    m = lax.axis_index("mp")
    return d // 2, d % 2, m // 2, m % 2


def at(z, x, y, c):
    return (2 * z + x, 2 * y + c)


def gelu_parts(x):
    ax = jnp.abs(x)
    e = jnp.exp2(x * x * (-0.5 * LOG2E))
    t = 1.0 / (1.0 + (0.3275911 * math.sqrt(0.5)) * ax)
    poly = t * (
        0.5 * 0.254829592
        + t
        * (
            -0.5 * 0.284496736
            + t * (0.5 * 1.421413741 + t * (-0.5 * 1.453152027 + t * (0.5 * 1.061405429)))
        )
    )
    tail = poly * e
    cdf = jnp.where(x < 0, tail, 1.0 - tail)
    active = x * cdf
    return active, cdf + x * (e * (1.0 / math.sqrt(2.0 * math.pi)))


def colsum(v):
    return jnp.sum(v, axis=0, keepdims=True)


def row_norm(summed):
    centre = summed - jnp.mean(summed, axis=-1, keepdims=True)
    spread = jnp.mean(centre * centre, axis=-1, keepdims=True)
    inv = lax.rsqrt(spread + EPS)
    return centre * inv, inv


NPIECE = 6


def forward_kernel(
    gates,
    tokens,
    cot,
    segcol,
    segrow,
    hgate,
    ugate,
    mgate,
    gain,
    bias,
    qkv_in,
    out_in,
    up_in,
    down_in,
    o_out,
    o_joined,
    o_ctx,
    o_ctxT,
    o_tokT,
    o_sgrad,
    o_grad,
    o_wq,
    o_wo,
    lse,
    small,
    wq,
    wo,
    wu,
    wd,
    joined,
    ctx,
    ctxT,
    tokT,
    attn,
    hlow,
    hT,
    blow,
    bT,
    branch,
    hback,
    act,
    inner,
    grads,
    outv,
    send_sem,
    recv_sem,
    loc_sem,
    out_sem,
    grad_sem,
):
    z, x, y, c = coords()
    m = 2 * y + c
    ms = 2 * y + 1 - c
    my = 2 * (1 - y) + c
    mys = 2 * (1 - y) + 1 - c
    sib = at(z, x, y, 1 - c)
    ypeer = at(z, x, 1 - y, c)
    xpeer = at(z, 1 - x, y, c)
    g0 = gates[0]
    g1 = gates[1]

    barrier = pltpu.get_barrier_semaphore()
    for peer in (sib, ypeer, xpeer):
        pl.semaphore_signal(barrier, inc=1, device_id=peer, device_id_type=MESH)
    pl.semaphore_wait(barrier, 3)

    def full(j, i, h=None):
        if j < 3:
            ref, n, cols = wq, 192, pl.ds(768 * j, 768)
        else:
            ref, n, cols = ((wo, 192), (wu, 768), (wd, 768))[j - 3] + (slice(None),)
        if h is None:
            return ref.at[i, :, cols]
        return ref.at[i, pl.ds(pl.multiple_of(h * (n // 2), 16), n // 2), cols]

    def own(j, h=None):
        if j < 3:
            ref, n, cols = qkv_in, 192, pl.ds(768 * j, 768)
        else:
            ref, n, cols = ((out_in, 192), (up_in, 768), (down_in, 768))[j - 3] + (slice(None),)
        if h is None:
            return ref.at[:, cols]
        return ref.at[pl.ds(pl.multiple_of(h * (n // 2), 16), n // 2), cols]

    def remote(src, dst, j, k, dev):
        return pltpu.make_async_remote_copy(
            src_ref=src,
            dst_ref=dst,
            send_sem=send_sem.at[j, k],
            recv_sem=recv_sem.at[j, k],
            device_id=dev,
            device_id_type=MESH,
        )

    def s1(j):
        return remote(own(j), full(j, m), j, 0, sib)

    def s2(j):
        return remote(own(j, x), full(j, m, x), j, 1, ypeer)

    def s3(j):
        return remote(full(j, my, x), full(j, my, x), j, 2, xpeer)

    def s4(j):
        return remote(full(j, my, x), full(j, my, x), j, 3, sib)

    def s5(j):
        return remote(full(j, my, 1 - x), full(j, my, 1 - x), j, 4, sib)

    def local(j):
        return pltpu.make_async_copy(own(j), full(j, m), loc_sem.at[j])

    def first(j):
        s2(j).start()
        s1(j).start()
        local(j).start()

    def second(j):
        s2(j).wait_recv()
        s3(j).start()
        s4(j).start()

    def third(j):
        s3(j).wait_recv()
        s5(j).start()

    def finish_near(j):
        local(j).wait()
        s1(j).wait_recv()

    def finish_far(j):
        s4(j).wait_recv()
        s5(j).wait_recv()

    def finish_sends(j):
        for s in (s1, s2, s3, s4, s5):
            s(j).wait_send()

    for j in range(3):
        first(j)

    tokT[...] = tokens[...].T
    tok_copy = pltpu.make_async_copy(tokT, o_tokT, out_sem.at[0])
    tok_copy.start()

    @pl.loop(0, 4)
    def _(r):
        rows = pl.ds(pl.multiple_of(r * 256, 256), 256)
        low = (g1 * cot[rows, :].astype(F32)).astype(BF)
        blow[rows, :] = low
        bT[:, rows] = low.T

    second(0)
    second(1)
    third(0)
    second(2)
    third(1)
    third(2)
    for j in range(3, NPIECE):
        first(j)
    for j in range(3):
        finish_near(j)
        finish_far(j)
    wq_copy = pltpu.make_async_copy(wq, o_wq, out_sem.at[1])
    wq_copy.start()

    for j in range(3):

        @pl.loop(0, 4)
        def _(r, j=j):
            rows = pl.ds(pl.multiple_of(r * 256, 256), 256)
            w = wq[:, :, pl.ds(768 * j, 768)].reshape(D, D)
            joined[rows, pl.ds(768 * j, 768)] = nn(tokens[rows, :], w).astype(BF)

    joined_copy = pltpu.make_async_copy(joined, o_joined, out_sem.at[2])
    joined_copy.start()

    scale = LOG2E / math.sqrt(HD)
    half_iota = lax.broadcasted_iota(jnp.int32, (1, 128), 1) // HD
    halves = [(half_iota == e).astype(F32).astype(BF) for e in range(2)]

    def attend(i):
        b = i // 6
        p = i % 6
        rows = pl.ds(pl.multiple_of(b * BLK, BLK), BLK)
        lane = pl.multiple_of(p * 128, 128)
        q = joined[rows, pl.ds(lane, 128)]
        k = joined[rows, pl.ds(D + lane, 128)]
        v = joined[rows, pl.ds(2 * D + lane, 128)]
        sc = segcol[b]
        sr = segrow[b]
        for qt in range(2):
            cols = slice(qt * 256, qt * 256 + 256)
            allowed = sc == sr[:, cols]
            total = None
            for e in range(2):
                s = nt(k * halves[e], q[cols, :])
                s = jnp.where(allowed, s * scale, MASKED)
                top = jnp.max(s, axis=0, keepdims=True)
                pr = jnp.exp2(s - top)
                tot = jnp.sum(pr, axis=0, keepdims=True)
                low = (pr * (1.0 / tot)).astype(BF)
                lse[2 * i + e, :, pl.ds(qt * 256, 256)] = top + jnp.log(tot) * LOG2E
                part = nn((v * halves[e]).T, low)
                total = part if total is None else total + part
            qrows = pl.ds(pl.multiple_of(b * BLK + qt * 256, 256), 256)
            ctxT[pl.ds(lane, 128), qrows] = total.astype(BF)
            ctx[qrows, pl.ds(lane, 128)] = total.T.astype(BF)

    pl.loop(0, 3)(attend)
    second(3)
    pl.loop(3, 5)(attend)
    third(3)
    pl.loop(5, 10)(attend)
    second(4)
    pl.loop(10, 12)(attend)
    ctx_copy = pltpu.make_async_copy(ctx, o_ctx, out_sem.at[3])
    ctx_copy.start()
    ctxT_copy = pltpu.make_async_copy(ctxT, o_ctxT, out_sem.at[4])
    ctxT_copy.start()
    finish_near(3)
    finish_far(3)
    wo_copy = pltpu.make_async_copy(wo, o_wo, out_sem.at[5])
    wo_copy.start()

    @pl.loop(0, 4)
    def _(r):
        rows = pl.ds(pl.multiple_of(r * 256, 256), 256)
        gated = ctx[rows, :] * hgate[...].astype(BF)
        a = nn(gated, wo[...].reshape(D, D))
        attn[rows, :] = a
        normed, _ = row_norm(tokens[rows, :].astype(F32) + g0 * a)
        low = ((normed * gain[...] + bias[...]) * mgate[...]).astype(BF)
        hlow[rows, :] = low
        hT[:, rows] = low.T

    third(4)
    second(5)

    small[...] = jnp.zeros_like(small)

    def feed(u, begin, slot):
        if not begin:
            pass
        w_up = wu.at[u]
        w_down = wd.at[u]

        @pl.loop(0, 4)
        def _(r):
            rows = pl.ds(pl.multiple_of(r * 256, 256), 256)
            pre = nn(hlow[rows, :], w_up[...])
            back = nn(blow[rows, :], w_down[...])
            active, slope = gelu_parts(pre)
            gate = ugate[u]
            small[pl.ds(u, 1), :] += colsum(back * active)
            a_low = (active * gate).astype(BF)
            i_low = (back * gate * slope).astype(BF)
            act[rows, :] = a_low
            inner[rows, :] = i_low
            up_part = nt(a_low, w_down[...])
            back_part = nt(i_low, w_up[...])
            if begin:
                branch[rows, :] = up_part
                hback[rows, :] = back_part
            else:
                branch[rows, :] += up_part
                hback[rows, :] += back_part

        for which, (left, right) in enumerate(((hT, inner), (bT, act))):

            @pl.loop(0, 8)
            def _(t, which=which, left=left, right=right):
                rr = pl.ds(pl.multiple_of(t * 96, 16), 96)
                g = nn(left[rr, :], right[...]).astype(BF)
                for j in range(2):
                    for h in range(2):
                        grads[slot, which, t // 4, j, t % 4 * 2 + h] = g[
                            48 * h : 48 * h + 48, 384 * j : 384 * j + 384
                        ]

    def grad_copies(u, slot):
        found = []
        for which in range(2):
            for r in range(2):
                found.append(
                    pltpu.make_async_copy(
                        grads.at[slot, which, r],
                        o_grad.at[which, r, pl.ds(2 * u, 2)],
                        grad_sem.at[slot, which, r],
                    )
                )
        return found

    finish_near(4)
    finish_near(5)
    feed(m, True, 0)
    for g in grad_copies(m, 0):
        g.start()
    third(5)
    feed(ms, False, 1)
    for g in grad_copies(ms, 1):
        g.start()
    finish_far(4)
    finish_far(5)
    for g in grad_copies(m, 0):
        g.wait()
    feed(my, False, 0)
    for g in grad_copies(my, 0):
        g.start()
    for g in grad_copies(ms, 1):
        g.wait()
    feed(mys, False, 1)
    for g in grad_copies(mys, 1):
        g.start()

    lane = lax.broadcasted_iota(jnp.int32, (1, D), 1)

    @pl.loop(0, 4)
    def _(r):
        rows = pl.ds(pl.multiple_of(r * 256, 256), 256)
        a = attn[rows, :]
        normed, inv = row_norm(tokens[rows, :].astype(F32) + g0 * a)
        plain = normed * gain[...] + bias[...]
        back = cot[rows, :].astype(F32)
        br = branch[rows, :]
        outv[rows, :] = (plain * mgate[...] + g1 * br).astype(BF)
        total = back + hback[rows, :]
        masked = total * mgate[...]
        small[4:5, :] += colsum(masked * normed)
        small[5:6, :] += colsum(masked)
        small[6:7, :] += colsum(total * plain)
        n = masked * gain[...]
        grad = (
            n
            - jnp.mean(n, axis=-1, keepdims=True)
            - normed * jnp.mean(n * normed, axis=-1, keepdims=True)
        ) * inv
        hback[rows, :] = grad
        small[7:8, :] += colsum(grad * a)
        small[8:9, :] += colsum(back * br)

    out_copy = pltpu.make_async_copy(outv, o_out, out_sem.at[6])
    out_copy.start()
    sgrad_copy = pltpu.make_async_copy(hback, o_sgrad, out_sem.at[7])
    sgrad_copy.start()
    for g in grad_copies(my, 0):
        g.wait()
    for g in grad_copies(mys, 1):
        g.wait()
    for copy in (tok_copy, wq_copy, joined_copy, ctx_copy, ctxT_copy, wo_copy, out_copy, sgrad_copy):
        copy.wait()
    for j in range(NPIECE):
        finish_sends(j)


def run_forward(gates, tokens, cot, segcol, segrow, hgate, ugate, mgate, gain, bias, qkv, out, up, down):
    sds = jax.ShapeDtypeStruct
    outs = (
        sds((ROWS, D), BF),
        sds((ROWS, 3 * D), BF),
        sds((ROWS, D), BF),
        sds((D, ROWS), BF),
        sds((D, ROWS), BF),
        sds((ROWS, D), F32),
        sds((2, 2, 8, 8, 48, SB), BF),
        sds((4, 192, 3 * D), BF),
        sds((4, 192, D), BF),
        sds((24, 1, BLK), F32),
        sds((16, D), F32),
    )
    any_ = pl.BlockSpec(memory_space=pl.ANY)
    vm = pl.BlockSpec(memory_space=pltpu.VMEM)
    sm = pl.BlockSpec(memory_space=pltpu.SMEM)
    return pl.pallas_call(
        forward_kernel,
        out_shape=outs,
        in_specs=[sm] + [vm] * 9 + [any_] * 4,
        out_specs=[any_] * 9 + [vm] * 2,
        scratch_shapes=[
            pltpu.VMEM((4, 192, 3 * D), BF),
            pltpu.VMEM((4, 192, D), BF),
            pltpu.VMEM((4, D, D), BF),
            pltpu.VMEM((4, D, D), BF),
            pltpu.VMEM((ROWS, 3 * D), BF),
            pltpu.VMEM((ROWS, D), BF),
            pltpu.VMEM((D, ROWS), BF),
            pltpu.VMEM((D, ROWS), BF),
            pltpu.VMEM((ROWS, D), F32),
            pltpu.VMEM((ROWS, D), BF),
            pltpu.VMEM((D, ROWS), BF),
            pltpu.VMEM((ROWS, D), BF),
            pltpu.VMEM((D, ROWS), BF),
            pltpu.VMEM((ROWS, D), F32),
            pltpu.VMEM((ROWS, D), F32),
            pltpu.VMEM((ROWS, D), BF),
            pltpu.VMEM((ROWS, D), BF),
            pltpu.VMEM((2, 2, 2, 2, 8, 48, SB), BF),
            pltpu.VMEM((ROWS, D), BF),
            pltpu.SemaphoreType.DMA((NPIECE, 5)),
            pltpu.SemaphoreType.DMA((NPIECE, 5)),
            pltpu.SemaphoreType.DMA((NPIECE,)),
            pltpu.SemaphoreType.DMA((8,)),
            pltpu.SemaphoreType.DMA((2, 2, 2)),
        ],
        compiler_params=pltpu.CompilerParams(
            collective_id=1, has_side_effects=True, vmem_limit_bytes=64 << 20
        ),
    )(gates, tokens, cot, segcol, segrow, hgate, ugate, mgate, gain, bias, qkv, out, up, down)


SENT = (12, 13, 14, 15, 0, 2, 4, 6, 8, 10, 1, 3, 5, 7, 9, 11)
GROUPS = ((0, 8), (8, 8), (16, 8), (24, 8), (32, 10), (42, 6))
FF_BLOCKS = 32


def backward_kernel(
    gates,
    order,
    small_in,
    hgate,
    hcol,
    segcol,
    segrow,
    lse,
    g_in,
    joined_in,
    ctx_in,
    ctxT_in,
    tokT_in,
    sgrad_in,
    wq_in,
    wo_in,
    o_igrad,
    o_full,
    small_out,
    joined,
    ctx,
    ctxT,
    tokT,
    sgrad,
    wq,
    wo,
    outb,
    cgrad,
    igrad,
    half,
    ga,
    got1,
    got2,
    got3,
    part,
    slots,
    gotz,
    gz,
    gfull,
    sm,
    gots,
    load_sem,
    half_sem,
    send_sem,
    recv_sem,
    z_send,
    z_recv,
    f_send,
    f_recv,
    s_send,
    s_recv,
    out_sem,
):
    z, x, y, c = coords()
    g0 = gates[0]
    sib = at(z, x, y, 1 - c)
    ypeer = at(z, x, 1 - y, c)
    xpeer = at(z, 1 - x, y, c)
    diag = at(z, 1 - x, 1 - y, c)
    zpeers = [at((z + k) % 4, x, y, c) for k in (1, 2, 3)]

    loads = [
        pltpu.make_async_copy(src, dst, load_sem.at[i])
        for i, (src, dst) in enumerate(
            (
                (sgrad_in, sgrad),
                (wo_in, wo),
                (ctx_in, ctx),
                (ctxT_in, ctxT),
                (joined_in, joined),
                (tokT_in, tokT),
                (wq_in, wq),
            )
        )
    ]
    halves_in = [
        pltpu.make_async_copy(
            g_in.at[pl.ds(8 * g, 8), c], half.at[pl.ds(8 * g, 8)], half_sem.at[g]
        )
        for g in range(4)
    ]
    for copy in loads[:4]:
        copy.start()

    barrier = pltpu.get_barrier_semaphore()
    for peer in [sib, ypeer, xpeer, diag] + zpeers:
        pl.semaphore_signal(barrier, inc=1, device_id=peer, device_id_type=MESH)
    pl.semaphore_wait(barrier, 7)

    def remote(src, dst, sems, dev):
        return pltpu.make_async_remote_copy(
            src_ref=src,
            dst_ref=dst,
            send_sem=sems[0],
            recv_sem=sems[1],
            device_id=dev,
            device_id_type=MESH,
        )

    def pair(g, k):
        return send_sem.at[g, k], recv_sem.at[g, k]

    def block(n):
        def ref(i):
            return half.at[i] if n < FF_BLOCKS else ga.at[i - FF_BLOCKS, c]

        return ref

    def mine(g, first, count):
        base = GROUPS[g][0] + first
        if base < FF_BLOCKS:
            return half.at[pl.ds(base, count)]
        return ga.at[pl.ds(base - FF_BLOCKS, count), c]

    def swap1(g):
        base, count = GROUPS[g]
        if base < FF_BLOCKS:
            src = g_in.at[pl.ds(base, count), 1 - c]
        else:
            src = ga.at[pl.ds(base - FF_BLOCKS, count), 1 - c]
        return remote(src, got1.at[pl.ds(base, count)], pair(g, 0), sib)

    def swap2(g):
        base, count = GROUPS[g]
        n = count // 2
        return (
            remote(mine(g, 0, n).at[:, 1 - y], got2.at[pl.ds(base, n)], pair(g, 1), ypeer),
            remote(
                mine(g, n, n).at[:, :, 1 - x], got2.at[pl.ds(base + n, n)], pair(g, 2), xpeer
            ),
        )

    def swap3(g):
        base, count = GROUPS[g]
        n = count // 2
        return (
            remote(mine(g, 0, n).at[:, y, 1 - x], got3.at[pl.ds(base, n)], pair(g, 3), xpeer),
            remote(
                mine(g, n, n).at[:, 1 - y, x], got3.at[pl.ds(base + n, n)], pair(g, 4), ypeer
            ),
        )

    def plus(left, right):
        return (left.astype(F32) + right.astype(F32)).astype(BF)

    def step1(g):
        base, count = GROUPS[g]
        if g < 4:
            halves_in[g].wait()
        swap1(g).wait_recv()

        @pl.loop(base, base + count)
        def _(i):
            ref = block(base)(i)
            ref[...] = plus(ref[...], got1[i])

        for copy in swap2(g):
            copy.start()

    def step2(g):
        base, count = GROUPS[g]
        n = count // 2
        for copy in swap2(g):
            copy.wait_recv()

        @pl.loop(base, base + n)
        def _(i):
            ref = block(base)(i)
            ref[y] = plus(ref[y], got2[i])

        @pl.loop(base + n, base + count)
        def _(i):
            ref = block(base)(i)
            ref[0, x] = plus(ref[0, x], got2[i, 0])
            ref[1, x] = plus(ref[1, x], got2[i, 1])

        for copy in swap3(g):
            copy.start()

    def step3(g):
        base, count = GROUPS[g]
        for copy in swap3(g):
            copy.wait_recv()

        @pl.loop(base, base + count)
        def _(i):
            part[i] = plus(block(base)(i)[y, x], got3[i])

    small_peers = [sib, ypeer, xpeer] + zpeers

    def small_copy(k):
        return remote(sm.at[min(k, 3)], gots.at[k], (s_send.at[k], s_recv.at[k]), small_peers[k])

    def small_step(k):
        small_copy(k).wait_recv()
        if k < 3:
            sm[k + 1] = sm[k] + gots[k]
            if k < 2:
                small_copy(k + 1).start()
            else:
                for j in (3, 4, 5):
                    small_copy(j).start()
        else:
            small_copy(4).wait_recv()
            small_copy(5).wait_recv()
            small_out[...] = sm[3] + gots[3] + gots[4] + gots[5]

    for g in range(4):
        swap1(g).start()
        halves_in[g].start()
    for copy in loads[4:]:
        copy.start()

    loads[0].wait()
    loads[1].wait()
    loads[2].wait()
    sm[0] = small_in[...]

    @pl.loop(0, 4)
    def _(r):
        rows = pl.ds(pl.multiple_of(r * 256, 256), 256)
        low = (g0 * sgrad[rows, :]).astype(BF)
        outb[rows, :] = low
        grad = nt(low, wo[...].reshape(D, D)).astype(BF)
        sm[0, 9:10, :] += colsum(ctx[rows, :].astype(F32) * grad.astype(F32))
        cgrad[rows, :] = grad * hgate[...].astype(BF)

    small_copy(0).start()
    loads[3].wait()

    def weight_tiles(left, right, lane, rowgate, places):
        @pl.loop(0, 8)
        def _(t):
            rr = pl.ds(pl.multiple_of(t * 96, 16), 96)
            g = nn(left[rr, :], right[:, pl.ds(lane, SB)])
            if rowgate is not None:
                g = g * rowgate[rr, :]
            g = g.astype(BF)
            to = places[0] + (t // 4) * (places[1] - places[0])
            u = t % 4
            for h in range(2):
                ga[to, u // 2, u % 2, h] = g[48 * h : 48 * h + 48]

    for j in range(2):
        weight_tiles(ctxT, outb, SB * j, hcol, (SENT.index(12 + j), SENT.index(14 + j)))

    step1(0)
    step1(1)
    step1(2)
    step1(3)
    loads[4].wait()

    scale = LOG2E / math.sqrt(HD)
    factor = 1.0 / math.sqrt(HD)
    half_iota = lax.broadcasted_iota(jnp.int32, (1, 128), 1) // HD
    halves = [(half_iota == e).astype(F32).astype(BF) for e in range(2)]

    def attend_back(i):
        p = i // 2
        b = i % 2
        rows = pl.ds(pl.multiple_of(b * BLK, BLK), BLK)
        lane = pl.multiple_of(p * 128, 128)
        q = joined[rows, pl.ds(lane, 128)]
        k = joined[rows, pl.ds(D + lane, 128)]
        v = joined[rows, pl.ds(2 * D + lane, 128)]
        do = cgrad[rows, pl.ds(lane, 128)]
        sc = segcol[b]
        sr = segrow[b]
        dv = None
        dk = None
        for qt in range(2):
            cols = slice(qt * 256, qt * 256 + 256)
            allowed = sc == sr[:, cols]
            dqT = None
            for e in range(2):
                ke = k * halves[e]
                s = nt(ke, q[cols])
                s = jnp.where(allowed, s * scale, MASKED)
                pr = jnp.exp2(s - lse[2 * (b * 6 + p) + e, :, pl.ds(qt * 256, 256)])
                dp = nt(v * halves[e], do[cols])
                delta = jnp.sum(pr * dp, axis=0, keepdims=True)
                ds = (pr * (dp - delta)).astype(BF)
                dv_part = nn(pr.astype(BF), do[cols] * halves[e])
                dk_part = nn(ds, q[cols] * halves[e])
                dq_part = nn(ke.T, ds)
                dv = dv_part if dv is None else dv + dv_part
                dk = dk_part if dk is None else dk + dk_part
                dqT = dq_part if dqT is None else dqT + dq_part
            qrows = pl.ds(pl.multiple_of(b * BLK + qt * 256, 256), 256)
            joined[qrows, pl.ds(lane, 128)] = (dqT * factor).T.astype(BF)
        joined[rows, pl.ds(D + lane, 128)] = (dk * factor).astype(BF)
        joined[rows, pl.ds(2 * D + lane, 128)] = dv.astype(BF)

    def qkv_tiles(h):
        for j in (h, 2 + h, 4 + h):
            weight_tiles(tokT, joined, SB * j, None, (SENT.index(j), SENT.index(6 + j)))

    def middle():
        loads[5].wait()
        qkv_tiles(0)
        swap1(4).start()

    plan = {
        0: [lambda: small_step(0)],
        1: [lambda: step2(0), lambda: small_step(1)],
        2: [lambda: small_step(2)],
        3: [lambda: step2(1), lambda: small_step(3)],
        5: [lambda: step2(2), middle],
        6: [lambda: step1(4), lambda: step3(0)],
        7: [lambda: step2(3), lambda: step3(1)],
        8: [lambda: step3(2)],
        10: [lambda: step2(4), lambda: step3(3)],
    }

    @pl.loop(0, 12)
    def _(i):
        attend_back(i)
        for at_step, todo in plan.items():

            @pl.when(i == at_step)
            def _(todo=todo):
                for f in todo:
                    f()

    qkv_tiles(1)
    swap1(5).start()
    loads[6].wait()

    def input_rows(lo, hi):
        @pl.loop(lo, hi)
        def _(r):
            rows = pl.ds(pl.multiple_of(r * 128, 128), 128)
            igrad[rows, :] = sgrad[rows, :] + nt(joined[rows, :], wq[...].reshape(D, 3 * D))

    input_rows(0, 2)
    step1(5)
    step3(4)
    input_rows(2, 6)
    step2(5)
    input_rows(6, 8)
    igrad_copy = pltpu.make_async_copy(igrad, o_igrad, out_sem.at[0])
    igrad_copy.start()
    step3(5)

    @pl.loop(0, 48)
    def _(s):
        slots[s] = part[order[s]]

    z_copies = []
    for k in (1, 2, 3):
        other = (z + k) % 4
        z_copies.append(
            remote(
                slots.at[pl.ds(12 * other, 12)],
                gotz.at[k - 1],
                (z_send.at[k - 1], z_recv.at[k - 1]),
                zpeers[k - 1],
            )
        )
    for copy in z_copies:
        copy.start()
    for copy in z_copies:
        copy.wait_recv()

    @pl.loop(0, 12)
    def _(s):
        total = slots[12 * z + s].astype(F32)
        for k in range(3):
            total = total + gotz[k, s].astype(F32)
        gz[s] = total.astype(BF)

    def piece(cc, yy, xx):
        return gfull.at[:, 4 * cc + 2 * yy + xx]

    here = gz.at[pl.ds(6 * x, 6)]
    there = gz.at[pl.ds(6 * (1 - x), 6)]

    def fsem(k):
        return f_send.at[k], f_recv.at[k]

    near = [
        remote(there, piece(c, y, x), fsem(0), xpeer),
        remote(here, piece(c, y, x), fsem(1), ypeer),
        remote(there, piece(c, y, x), fsem(2), diag),
        remote(here, piece(c, y, x), fsem(3), sib),
    ]
    for copy in near:
        copy.start()
    own_copy = pltpu.make_async_copy(here, piece(c, y, x), out_sem.at[1])
    own_copy.start()
    onward = []
    for k, (yy, xx) in enumerate(((y, 1 - x), (1 - y, x), (1 - y, 1 - x))):
        near[k].wait_recv()
        copy = remote(piece(c, yy, xx), piece(c, yy, xx), fsem(4 + k), sib)
        copy.start()
        onward.append(copy)
    near[3].wait_recv()
    for copy in onward:
        copy.wait_recv()
    own_copy.wait()
    full_copy = pltpu.make_async_copy(gfull, o_full, out_sem.at[2])
    full_copy.start()
    for copy in near + onward + z_copies:
        copy.wait_send()
    for k in range(6):
        small_copy(k).wait_send()
    for g in range(len(GROUPS)):
        for copy in (swap1(g),) + swap2(g) + swap3(g):
            copy.wait_send()
    igrad_copy.wait()
    full_copy.wait()


def run_backward(gates, order, small, hgate, hcol, segcol, segrow, lse, *arrays):
    sds = jax.ShapeDtypeStruct
    outs = (sds((ROWS, D), F32), sds((6, 8, 48, SB), BF), sds((16, D), F32))
    any_ = pl.BlockSpec(memory_space=pl.ANY)
    vm = pl.BlockSpec(memory_space=pltpu.VMEM)
    sm = pl.BlockSpec(memory_space=pltpu.SMEM)
    dma = pltpu.SemaphoreType.DMA
    return pl.pallas_call(
        backward_kernel,
        out_shape=outs,
        in_specs=[sm] * 2 + [vm] * 6 + [any_] * 8,
        out_specs=[any_] * 2 + [vm],
        scratch_shapes=[
            pltpu.VMEM((ROWS, 3 * D), BF),
            pltpu.VMEM((ROWS, D), BF),
            pltpu.VMEM((D, ROWS), BF),
            pltpu.VMEM((D, ROWS), BF),
            pltpu.VMEM((ROWS, D), F32),
            pltpu.VMEM((4, 192, 3 * D), BF),
            pltpu.VMEM((4, 192, D), BF),
            pltpu.VMEM((ROWS, D), BF),
            pltpu.VMEM((ROWS, D), BF),
            pltpu.VMEM((ROWS, D), F32),
            pltpu.VMEM((32, 2, 2, 48, SB), BF),
            pltpu.VMEM((16, 2, 2, 2, 48, SB), BF),
            pltpu.VMEM((48, 2, 2, 48, SB), BF),
            pltpu.VMEM((48, 2, 48, SB), BF),
            pltpu.VMEM((48, 48, SB), BF),
            pltpu.VMEM((48, 48, SB), BF),
            pltpu.VMEM((48, 48, SB), BF),
            pltpu.VMEM((3, 12, 48, SB), BF),
            pltpu.VMEM((12, 48, SB), BF),
            pltpu.VMEM((6, 8, 48, SB), BF),
            pltpu.VMEM((4, 16, D), F32),
            pltpu.VMEM((6, 16, D), F32),
            dma((7,)),
            dma((4,)),
            dma((6, 5)),
            dma((6, 5)),
            dma((3,)),
            dma((3,)),
            dma((7,)),
            dma((7,)),
            dma((6,)),
            dma((6,)),
            dma((3,)),
        ],
        compiler_params=pltpu.CompilerParams(
            collective_id=2, has_side_effects=True, vmem_limit_bytes=64 << 20
        ),
    )(gates, order, small, hgate, hcol, segcol, segrow, lse, *arrays)


def split(value):
    high = value.astype(BF)
    return high, (value - high.astype(F32)).astype(BF)


def update_kernel(
    full, master, left_stats, right_stats, left_root, right_root, o_grad, o_left, o_right, o_new, o_copy, turned
):
    start = pl.multiple_of(lax.axis_index("mp") * 96, 16)
    own = full[0, pl.ds(start, 96), :]
    whole = full[0]
    o_grad[0] = own.astype(F32)
    o_left[0] = BETA * left_stats[0] + (1.0 - BETA) * nt(own, whole)
    turned[...] = whole.T
    o_right[0] = BETA * right_stats[0] + (1.0 - BETA) * nn(turned[pl.ds(start, 96), :], whole)
    root_high, root_low = split(left_root[0])
    left_part = nn(root_high, whole) + nn(root_low, whole)
    part_high, part_low = split(left_part)
    right_high, right_low = split(right_root[0])
    update = nn(part_high, right_high) + nn(part_low, right_high) + nn(part_high, right_low)
    new = master[0] - RATE * update
    o_new[0] = new
    o_copy[0] = new.astype(BF)


def run_update(full, master, left_stats, right_stats, left_root, right_root):
    sds = jax.ShapeDtypeStruct
    whole = pl.BlockSpec((1, SB, SB), lambda s: (s, 0, 0))
    rows = pl.BlockSpec((1, 96, SB), lambda s: (s, 0, 0))
    return pl.pallas_call(
        update_kernel,
        grid=(6,),
        out_shape=(sds((6, 96, SB), F32),) * 4 + (sds((6, 96, SB), BF),),
        in_specs=[whole] + [rows] * 4 + [whole],
        out_specs=[rows] * 5,
        scratch_shapes=[pltpu.VMEM((SB, SB), BF)],
        compiler_params=pltpu.CompilerParams(vmem_limit_bytes=32 << 20),
    )(full, master, left_stats, right_stats, left_root, right_root)


PLACE = tuple(FF_BLOCKS + SENT.index(b) for b in range(16)) + tuple(range(32))


def fast_body(
    tokens,
    segments,
    head_mask,
    unit_mask,
    hidden_mask,
    layer_gates,
    qkv_weight,
    out_weight,
    norm_gain,
    norm_bias,
    up_weight,
    down_weight,
    cotangent,
    owner_slot,
    master,
    left_stats,
    right_stats,
    left_root,
    right_root,
):
    segcol = segments[:, :, None]
    segrow = segments[:, None, :]
    head_lanes = jnp.repeat(head_mask.astype(F32), HD)
    hgate = head_lanes[None]
    ugate = unit_mask.astype(F32).reshape(4, 1, D)
    mgate = hidden_mask.astype(F32)[None]
    (output, joined, ctx, ctxT, tokT, summed_grad, ff_grad, wq, wo, lse, small) = run_forward(
        layer_gates,
        tokens,
        cotangent,
        segcol,
        segrow,
        hgate,
        ugate,
        mgate,
        norm_gain[None],
        norm_bias[None],
        qkv_weight,
        out_weight,
        up_weight,
        down_weight,
    )
    slot_order = jnp.sum(
        jnp.where(owner_slot[None, :] == jnp.arange(48)[:, None], jnp.asarray(PLACE)[None, :], 0), axis=1
    )
    input_grad, full, small = run_backward(
        layer_gates,
        slot_order,
        small,
        hgate,
        head_lanes[:, None],
        segcol,
        segrow,
        lse,
        ff_grad.reshape(32, 2, 2, 2, 48, SB),
        joined,
        ctx,
        ctxT,
        tokT,
        summed_grad,
        wq,
        wo,
    )
    owned, left_new, right_new, weight_new, weight_copy = run_update(
        full.reshape(6, SB, SB), master, left_stats, right_stats, left_root, right_root
    )
    unit_grad = small[:4].reshape(-1)
    norm_grad = small[4:6]
    mask_grad = small[6]
    layer_grad = jnp.sum(small[7:9], axis=1)
    head_grad = jnp.sum(small[9].reshape(12, HD), axis=1)
    norm_new = jnp.stack([norm_gain, norm_bias]) - 0.2 / math.sqrt(ROWS * 32) * norm_grad
    return (
        output,
        input_grad,
        head_grad,
        unit_grad,
        mask_grad,
        layer_grad,
        norm_grad,
        norm_new,
        owned,
        left_new,
        right_new,
        weight_new,
        weight_copy,
    )


def solution(mesh):
    return jax.shard_map(
        fast_body if dict(mesh.shape) == {"dp": 8, "mp": 4} else body,
        mesh=mesh,
        in_specs=(
            P(("dp", "mp"), None),
            P(("dp", "mp"), None),
            P(),
            P(),
            P(),
            P(),
            P("mp", None),
            P("mp", None),
            P(),
            P(),
            P(None, "mp"),
            P(None, "mp"),
            P(("dp", "mp"), None),
            P(),
            P("dp", "mp", None),
            P("dp", "mp", None),
            P("dp", "mp", None),
            P("dp", "mp", None),
            P("dp", None, None),
        ),
        out_specs=(
            P(("dp", "mp"), None),
            P(("dp", "mp"), None),
            P(),
            P(),
            P(),
            P(),
            P(),
            P(),
            P("dp", "mp", None),
            P("dp", "mp", None),
            P("dp", "mp", None),
            P("dp", "mp", None),
            P("dp", "mp", None),
        ),
        check_vma=False,
    )
```

```python
from functools import partial
import math

import jax
import jax.numpy as jnp
from jax import lax
from jax.experimental import pallas as pl
from jax.experimental.pallas import tpu as pltpu
from jax.sharding import PartitionSpec as P

FF = 3072
SB = 384


HIGH = lax.Precision.HIGHEST
BETA = 0.5
RATE = 0.5
EPS = 1e-12
MASKED = -1e30


def gelu_exact(values):
    return jax.nn.gelu(values, approximate=False)


def normalize(summed, gain_in, offset, hidden_gate):
    centre = summed - jnp.mean(summed, axis=-1, keepdims=True)
    spread = jnp.mean(centre * centre, axis=-1, keepdims=True)
    return (centre * lax.rsqrt(spread + EPS) * gain_in + offset) * hidden_gate


def split_heads(block_joined, head_count):
    pieces = block_joined.reshape(block_joined.shape[0], 3, head_count, -1)
    return (pieces[:, 0], pieces[:, 1], pieces[:, 2])


def masked_scores(queries, keys_in, labels, factor):
    scores = (
        jnp.einsum("qhd,khd->hqk", queries, keys_in, preferred_element_type=jnp.float32) * factor
    )
    allowed = labels[:, None] == labels[None, :]
    return jnp.where(allowed[None], scores, MASKED)


def attend_forward(packed, head_count, factor):
    block_joined, labels = packed
    queries, keys_in, values_in = split_heads(block_joined, head_count)
    scores = masked_scores(queries, keys_in, labels, factor)
    highest = jnp.max(scores, axis=-1, keepdims=True)
    raised = jnp.exp(scores - highest)
    totals = jnp.sum(raised, axis=-1, keepdims=True)
    weights_low = (raised / totals).astype(jnp.bfloat16)
    context = jnp.einsum("hqk,khd->qhd", weights_low, values_in, preferred_element_type=jnp.float32)
    return (context, (highest + jnp.log(totals))[:, :, 0])


def attend_backward(packed, head_count, factor):
    block_joined, log_totals, context_grad, labels = packed
    queries, keys_in, values_in = split_heads(block_joined, head_count)
    scores = masked_scores(queries, keys_in, labels, factor)
    weights_full = jnp.exp(scores - log_totals[:, :, None])
    weights_low = weights_full.astype(jnp.bfloat16)
    values_grad = jnp.einsum(
        "hqk,qhd->khd", weights_low, context_grad, preferred_element_type=jnp.float32
    )
    weights_grad = jnp.einsum(
        "qhd,khd->hqk", context_grad, values_in, preferred_element_type=jnp.float32
    )
    inner_sum = jnp.sum(weights_full * weights_grad, axis=-1, keepdims=True)
    scores_grad = (weights_full * (weights_grad - inner_sum)).astype(jnp.bfloat16)
    queries_grad = (
        jnp.einsum("hqk,khd->qhd", scores_grad, keys_in, preferred_element_type=jnp.float32)
        * factor
    )
    keys_grad = (
        jnp.einsum("hqk,qhd->khd", scores_grad, queries, preferred_element_type=jnp.float32)
        * factor
    )
    merged = jnp.concatenate([queries_grad, keys_grad, values_grad], axis=1)
    return merged.reshape(merged.shape[0], -1).astype(jnp.bfloat16)


def contract_rows(left, right):
    return lax.dot_general(
        left, right, (((0,), (0,)), ((), ())), preferred_element_type=jnp.float32
    )


def contract_cols(left, right):
    return lax.dot_general(
        left, right, (((1,), (1,)), ((), ())), preferred_element_type=jnp.float32
    )


def body(
    tokens,
    segments,
    head_mask,
    unit_mask,
    hidden_mask,
    layer_gates,
    qkv_weight,
    out_weight,
    norm_gain,
    norm_bias,
    up_weight,
    down_weight,
    cotangent,
    owner_slot,
    master,
    left_stats,
    right_stats,
    left_root,
    right_root,
):
    row_count = tokens.shape[0]
    width = tokens.shape[1]
    head_count = head_mask.shape[0]
    head_width = width // head_count
    block_rows = segments.shape[1]
    block_count = segments.shape[0]
    factor = 1.0 / math.sqrt(head_width)
    model_size = lax.axis_size("mp")
    share = FF // model_size
    part_rows = SB // model_size
    total_tokens = row_count * lax.axis_size("dp") * model_size
    head_gate = head_mask.astype(jnp.float32)
    unit_gate = unit_mask.astype(jnp.float32)
    hidden_gate = hidden_mask.astype(jnp.float32)
    inputs = tokens.astype(jnp.float32)
    back_full = cotangent.astype(jnp.float32)
    qkv_full, out_full, up_full, down_full = (
        lax.all_gather(qkv_weight, "mp", axis=0, tiled=True),
        lax.all_gather(out_weight, "mp", axis=0, tiled=True),
        lax.all_gather(up_weight, "mp", axis=1, tiled=True),
        lax.all_gather(down_weight, "mp", axis=1, tiled=True),
    )
    joined_qkv = jnp.dot(tokens, qkv_full, preferred_element_type=jnp.float32).astype(jnp.bfloat16)
    joined_blocks = joined_qkv.reshape(block_count, block_rows, 3 * width)
    context, log_totals = lax.map(
        partial(attend_forward, head_count=head_count, factor=factor), (joined_blocks, segments)
    )
    context = context.reshape(row_count, head_count, head_width)
    gated_low = (context * head_gate[None, :, None]).reshape(row_count, width).astype(jnp.bfloat16)
    attn_out = jnp.dot(gated_low, out_full, preferred_element_type=jnp.float32)
    summed = inputs + layer_gates[0] * attn_out
    hidden, norm_pull = jax.vjp(normalize, summed, norm_gain, norm_bias, hidden_gate)
    hidden_low = hidden.astype(jnp.bfloat16)
    pre_act = jnp.dot(hidden_low, up_full, preferred_element_type=jnp.float32)
    active, gelu_pull = jax.vjp(gelu_exact, pre_act)
    active_low = (active * unit_gate).astype(jnp.bfloat16)
    branch = contract_cols(active_low, down_full)
    output = (hidden + layer_gates[1] * branch).astype(jnp.bfloat16)
    back_rounded = (layer_gates[1] * back_full).astype(jnp.bfloat16)
    qkv_full, out_full, up_full, down_full = (
        lax.all_gather(qkv_weight, "mp", axis=0, tiled=True),
        lax.all_gather(out_weight, "mp", axis=0, tiled=True),
        lax.all_gather(up_weight, "mp", axis=1, tiled=True),
        lax.all_gather(down_weight, "mp", axis=1, tiled=True),
    )
    grad_active = jnp.dot(back_rounded, down_full, preferred_element_type=jnp.float32)
    unit_grad = jnp.sum(grad_active * active, axis=0)
    grad_inner = gelu_pull(grad_active * unit_gate)[0].astype(jnp.bfloat16)
    hidden_back = contract_cols(grad_inner, up_full)
    up_term = contract_rows(grad_inner, hidden_low)
    down_term = contract_rows(active_low, back_rounded)
    unit_local = (
        lax.psum_scatter(
            jnp.stack([up_term, down_term], axis=1).astype(jnp.bfloat16),
            "mp",
            scatter_dimension=0,
            tiled=True,
        )
        .astype(jnp.float32)
        .transpose(1, 2, 0)
    )
    summed_grad, gain_grad, bias_grad, mask_grad = norm_pull(back_full + hidden_back)
    layer_grad = jnp.stack([jnp.sum(summed_grad * attn_out), jnp.sum(back_full * branch)])
    out_back = (layer_gates[0] * summed_grad).astype(jnp.bfloat16)
    gated_grad = contract_cols(out_back, out_full).astype(jnp.bfloat16)
    gated_heads = gated_grad.reshape(row_count, head_count, head_width)
    head_grad = jnp.sum(context * gated_heads.astype(jnp.float32), axis=(0, 2))
    context_grad = gated_heads * head_mask.astype(jnp.bfloat16)[None, :, None]
    joined_grad = lax.map(
        partial(attend_backward, head_count=head_count, factor=factor),
        (
            joined_blocks,
            log_totals,
            context_grad.reshape(block_count, block_rows, head_count, head_width),
            segments,
        ),
    )
    joined_grad = joined_grad.reshape(row_count, 3 * width)
    input_grad = summed_grad + contract_cols(joined_grad, qkv_full)
    tiles = width // SB
    qkv_term = jnp.einsum(
        "tri,tcj->rcij",
        tokens.reshape(row_count, tiles, SB),
        joined_grad.reshape(row_count, 3 * tiles, SB),
        preferred_element_type=jnp.float32,
    )
    out_term = jnp.einsum(
        "tri,tcj->rcij",
        gated_low.reshape(row_count, tiles, SB),
        out_back.reshape(row_count, tiles, SB),
        preferred_element_type=jnp.float32,
    )
    attn_terms = jnp.concatenate(
        [
            qkv_term.reshape(-1, model_size, part_rows, SB),
            out_term.reshape(-1, model_size, part_rows, SB),
        ],
        axis=0,
    )
    attn_rows = (
        lax.psum_scatter(attn_terms.astype(jnp.bfloat16), "mp", scatter_dimension=1, tiled=True)
        .astype(jnp.float32)
        .reshape(-1, part_rows, SB)
    )
    unit_split = unit_local.reshape(2, tiles, model_size, part_rows, share)
    unit_rows = lax.all_to_all(
        unit_split.astype(jnp.bfloat16), "mp", split_axis=2, concat_axis=4, tiled=True
    ).astype(unit_split.dtype)
    unit_rows = (
        unit_rows.reshape(2, tiles, part_rows, FF // SB, SB)
        .transpose(0, 1, 3, 2, 4)
        .reshape(-1, part_rows, SB)
    )
    all_rows = jnp.concatenate([attn_rows, unit_rows], axis=0)
    slot_count = owner_slot.shape[0]
    pick = (owner_slot[None, :] == jnp.arange(slot_count)[:, None]).astype(jnp.bfloat16)
    flat_rows = all_rows.astype(jnp.bfloat16).reshape(slot_count, -1)
    slotted = jnp.dot(pick, flat_rows, preferred_element_type=jnp.float32).reshape(all_rows.shape)
    owned = lax.psum_scatter(
        slotted.astype(jnp.bfloat16), "dp", scatter_dimension=0, tiled=True
    ).astype(jnp.float32)
    full_grad = lax.all_gather(owned.astype(jnp.bfloat16), "mp", axis=1, tiled=True).astype(
        owned.dtype
    )
    row_start = lax.axis_index("mp") * part_rows
    columns = lax.dynamic_slice_in_dim(full_grad, row_start, part_rows, 2)
    left_new = BETA * left_stats + (1.0 - BETA) * jnp.einsum(
        "srj,skj->srk", owned, full_grad, precision=HIGH
    )
    right_new = BETA * right_stats + (1.0 - BETA) * jnp.einsum(
        "sjr,sjk->srk", columns, full_grad, precision=HIGH
    )
    left_part = jnp.einsum("sri,sij->srj", left_root, full_grad, precision=HIGH)
    update = jnp.einsum("srj,sjk->srk", left_part, right_root, precision=HIGH)
    weight_new = master - RATE * update
    norm_grad = jnp.stack([gain_grad, bias_grad])
    norm_grad, mask_grad, head_grad, layer_grad, unit_grad = lax.psum(
        (norm_grad, mask_grad, head_grad, layer_grad, unit_grad), ("dp", "mp")
    )
    norm_new = jnp.stack([norm_gain, norm_bias]) - 0.2 / math.sqrt(total_tokens) * norm_grad
    return (
        output,
        input_grad,
        head_grad,
        unit_grad,
        mask_grad,
        layer_grad,
        norm_grad,
        norm_new,
        owned,
        left_new,
        right_new,
        weight_new,
        weight_new.astype(jnp.bfloat16),
    )


F32 = jnp.float32
BF = jnp.bfloat16
MESH = pl.DeviceIdType.MESH
LOG2E = 1.4426950408889634
ROWS = 1024
D = 768
HD = 64
BLK = 512
NT_DIMS = (((1,), (1,)), ((), ()))
NN_DIMS = (((1,), (0,)), ((), ()))


def nn(left, right):
    return lax.dot_general(left, right, NN_DIMS, preferred_element_type=F32)


def nt(left, right):
    return lax.dot_general(left, right, NT_DIMS, preferred_element_type=F32)


def coords():
    d = lax.axis_index("dp")
    m = lax.axis_index("mp")
    return d // 2, d % 2, m // 2, m % 2


def at(z, x, y, c):
    return (2 * z + x, 2 * y + c)


def gelu_parts(x):
    ax = jnp.abs(x)
    e = jnp.exp2(x * x * (-0.5 * LOG2E))
    t = 1.0 / (1.0 + (0.3275911 * math.sqrt(0.5)) * ax)
    poly = t * (
        0.5 * 0.254829592
        + t
        * (
            -0.5 * 0.284496736
            + t * (0.5 * 1.421413741 + t * (-0.5 * 1.453152027 + t * (0.5 * 1.061405429)))
        )
    )
    tail = poly * e
    cdf = jnp.where(x < 0, tail, 1.0 - tail)
    active = x * cdf
    return active, cdf + x * (e * (1.0 / math.sqrt(2.0 * math.pi)))


def colsum(v):
    return jnp.sum(v, axis=0, keepdims=True)


def row_norm(summed):
    centre = summed - jnp.mean(summed, axis=-1, keepdims=True)
    spread = jnp.mean(centre * centre, axis=-1, keepdims=True)
    inv = lax.rsqrt(spread + EPS)
    return centre * inv, inv


def one_row(v):
    return jnp.concatenate([v[i : i + 1] for i in range(v.shape[0])], axis=1)


def many_rows(v):
    return jnp.concatenate([v[:, 128 * i : 128 * i + 128] for i in range(v.shape[1] // 128)], axis=0)


def head_lanes(heads):
    which = lax.broadcasted_iota(jnp.int32, (1, D), 1) // HD
    row = jnp.zeros((1, D), F32)
    for h in range(12):
        row = row + jnp.where(which == h, heads[h].astype(F32), 0.0)
    return row


def columns_of(segs, segcol):
    for b in range(2):
        row = segs[b : b + 1, :].astype(F32)
        segcol[b] = jnp.broadcast_to(row, (8, BLK)).T[:, 0:1].astype(jnp.int32)


NPIECE = 8


def forward_kernel(
    gates,
    heads,
    tokens,
    cot,
    segs,
    units,
    hidden,
    gain_in,
    bias_in,
    qkv_in,
    out_in,
    up_in,
    down_in,
    o_out,
    o_joined,
    o_ctx,
    o_ctxT,
    o_tokT,
    o_sgrad,
    o_grad,
    o_wq,
    o_wo,
    lse,
    small,
    wq,
    wo,
    wu,
    wd,
    joined,
    ctx,
    ctxT,
    tokT,
    attn,
    hlow,
    hT,
    blow,
    bT,
    branch,
    hback,
    act,
    inner,
    grads,
    outv,
    segcol,
    ugate,
    vec,
    send_sem,
    recv_sem,
    loc_sem,
    out_sem,
    grad_sem,
):
    z, x, y, c = coords()
    m = 2 * y + c
    ms = 2 * y + 1 - c
    my = 2 * (1 - y) + c
    mys = 2 * (1 - y) + 1 - c
    sib = at(z, x, y, 1 - c)
    ypeer = at(z, x, 1 - y, c)
    xpeer = at(z, 1 - x, y, c)
    g0 = gates[0]
    g1 = gates[1]

    barrier = pltpu.get_barrier_semaphore()
    for peer in (sib, ypeer, xpeer):
        pl.semaphore_signal(barrier, inc=1, device_id=peer, device_id_type=MESH)
    pl.semaphore_wait(barrier, 3)

    def spot(j):
        if j < 3:
            return 0, 192, pl.ds(768 * j, 768)
        if j == 3:
            return 1, 192, slice(None)
        return 2 + (j - 4) // 2, 768, pl.ds(384 * (j % 2), 384)

    def full(j, i, h=None):
        which, n, cols = spot(j)
        ref = (wq, wo, wu, wd)[which]
        if h is None:
            return ref.at[i, :, cols]
        return ref.at[i, pl.ds(pl.multiple_of(h * (n // 2), 16), n // 2), cols]

    def own(j, h=None):
        which, n, cols = spot(j)
        ref = (qkv_in, out_in, up_in, down_in)[which]
        if h is None:
            return ref.at[:, cols]
        return ref.at[pl.ds(pl.multiple_of(h * (n // 2), 16), n // 2), cols]

    def remote(src, dst, j, k, dev):
        return pltpu.make_async_remote_copy(
            src_ref=src,
            dst_ref=dst,
            send_sem=send_sem.at[j, k],
            recv_sem=recv_sem.at[j, k],
            device_id=dev,
            device_id_type=MESH,
        )

    def s1(j):
        return remote(own(j), full(j, m), j, 0, sib)

    def s2(j):
        return remote(own(j, x), full(j, m, x), j, 1, ypeer)

    def s3(j):
        return remote(full(j, my, x), full(j, my, x), j, 2, xpeer)

    def s4(j):
        return remote(full(j, my, x), full(j, my, x), j, 3, sib)

    def s5(j):
        return remote(full(j, my, 1 - x), full(j, my, 1 - x), j, 4, sib)

    def local(j):
        return pltpu.make_async_copy(own(j), full(j, m), loc_sem.at[j])

    def first(j):
        s2(j).start()
        s1(j).start()
        local(j).start()

    def second(j):
        s2(j).wait_recv()
        s3(j).start()
        s4(j).start()

    def third(j):
        s3(j).wait_recv()
        s5(j).start()

    def finish_near(j):
        local(j).wait()
        s1(j).wait_recv()

    def finish_far(j):
        s4(j).wait_recv()
        s5(j).wait_recv()

    def finish_sends(j):
        for s in (s1, s2, s3, s4, s5):
            s(j).wait_send()

    for j in range(3):
        first(j)

    columns_of(segs, segcol)
    for i in range(4):
        ugate[i] = one_row(units[6 * i : 6 * i + 6, :].astype(F32))
    vec[0:1, :] = head_lanes(heads)
    vec[1:2, :] = one_row(hidden[...].astype(F32))
    vec[2:3, :] = one_row(gain_in[...])
    vec[3:4, :] = one_row(bias_in[...])
    hgate, mgate, gain, bias = (vec.at[i : i + 1] for i in range(4))
    tokT[...] = tokens[...].T
    tok_copy = pltpu.make_async_copy(tokT, o_tokT, out_sem.at[0])
    tok_copy.start()

    @pl.loop(0, 4)
    def _(r):
        rows = pl.ds(pl.multiple_of(r * 256, 256), 256)
        low = (g1 * cot[rows, :].astype(F32)).astype(BF)
        blow[rows, :] = low
        bT[:, rows] = low.T

    def project(j):
        @pl.loop(0, 2)
        def _(r):
            rows = pl.ds(pl.multiple_of(r * 512, 512), 512)
            w = wq[:, :, pl.ds(768 * j, 768)].reshape(D, D)
            joined[rows, pl.ds(768 * j, 768)] = nn(tokens[rows, :], w).astype(BF)

    second(0)
    second(1)
    third(0)
    second(2)
    for j in range(3, NPIECE):
        first(j)
    third(1)
    finish_near(0)
    finish_far(0)
    project(0)
    third(2)
    finish_near(1)
    finish_far(1)
    project(1)
    finish_near(2)
    finish_far(2)
    wq_copy = pltpu.make_async_copy(wq, o_wq, out_sem.at[1])
    wq_copy.start()
    project(2)
    joined_copy = pltpu.make_async_copy(joined, o_joined, out_sem.at[2])
    joined_copy.start()

    scale = LOG2E / math.sqrt(HD)
    half_iota = lax.broadcasted_iota(jnp.int32, (1, 128), 1) // HD
    halves = [(half_iota == e).astype(F32).astype(BF) for e in range(2)]

    def attend(i):
        b = i // 6
        p = i % 6
        rows = pl.ds(pl.multiple_of(b * BLK, BLK), BLK)
        lane = pl.multiple_of(p * 128, 128)
        q = joined[rows, pl.ds(lane, 128)]
        k = joined[rows, pl.ds(D + lane, 128)]
        v = joined[rows, pl.ds(2 * D + lane, 128)]
        sc = segcol[b]
        sr = segs[pl.ds(b, 1), :]
        for qt in range(2):
            cols = slice(qt * 256, qt * 256 + 256)
            allowed = sc == sr[:, cols]
            total = None
            for e in range(2):
                s = nt(k * halves[e], q[cols, :])
                s = jnp.where(allowed, s * scale, MASKED)
                top = jnp.max(s, axis=0, keepdims=True)
                pr = jnp.exp2(s - top)
                tot = jnp.sum(pr, axis=0, keepdims=True)
                low = (pr * (1.0 / tot)).astype(BF)
                lse[2 * i + e, :, pl.ds(qt * 256, 256)] = top + jnp.log(tot) * LOG2E
                part = nn((v * halves[e]).T, low)
                total = part if total is None else total + part
            qrows = pl.ds(pl.multiple_of(b * BLK + qt * 256, 256), 256)
            ctxT[pl.ds(lane, 128), qrows] = total.astype(BF)
            ctx[qrows, pl.ds(lane, 128)] = total.T.astype(BF)

    plan = {
        0: [lambda: second(3)],
        3: [lambda: second(4), lambda: third(3)],
        8: [lambda: second(5), lambda: third(4)],
        11: [lambda: second(6)],
    }

    @pl.loop(0, 12)
    def _(i):
        attend(i)
        for at_step, todo in plan.items():

            @pl.when(i == at_step)
            def _(todo=todo):
                for f in todo:
                    f()

    ctx_copy = pltpu.make_async_copy(ctx, o_ctx, out_sem.at[3])
    ctx_copy.start()
    ctxT_copy = pltpu.make_async_copy(ctxT, o_ctxT, out_sem.at[4])
    ctxT_copy.start()
    finish_near(3)
    finish_far(3)
    wo_copy = pltpu.make_async_copy(wo, o_wo, out_sem.at[5])
    wo_copy.start()

    @pl.loop(0, 4)
    def _(r):
        rows = pl.ds(pl.multiple_of(r * 256, 256), 256)
        gated = ctx[rows, :] * hgate[...].astype(BF)
        a = nn(gated, wo[...].reshape(D, D))
        attn[rows, :] = a
        normed, _ = row_norm(tokens[rows, :].astype(F32) + g0 * a)
        low = ((normed * gain[...] + bias[...]) * mgate[...]).astype(BF)
        hlow[rows, :] = low
        hT[:, rows] = low.T

    third(5)

    small[...] = jnp.zeros_like(small)

    def feed(u, begin, slot, between=None):
        w_up = wu.at[u]
        w_down = wd.at[u]

        @pl.loop(0, 2)
        def _(r):
            rows = pl.ds(pl.multiple_of(r * 512, 512), 512)
            pre = nn(hlow[rows, :], w_up[...])
            back = nn(blow[rows, :], w_down[...])
            active, slope = gelu_parts(pre)
            gate = ugate[u]
            small[pl.ds(u, 1), :] += colsum(back * active)
            a_low = (active * gate).astype(BF)
            i_low = (back * gate * slope).astype(BF)
            act[rows, :] = a_low
            inner[rows, :] = i_low
            up_part = nt(a_low, w_down[...])
            back_part = nt(i_low, w_up[...])
            if begin:
                branch[rows, :] = up_part
                hback[rows, :] = back_part
            else:
                branch[rows, :] += up_part
                hback[rows, :] += back_part

        if between is not None:
            between()

        for which, (left, right) in enumerate(((hT, inner), (bT, act))):

            @pl.loop(0, 2)
            def _(r, which=which, left=left, right=right):
                rr = pl.ds(pl.multiple_of(r * SB, 128), SB)
                g = nn(left[rr, :], right[...]).astype(BF)
                for j in range(2):
                    grads[slot, which, r, j] = g[:, SB * j : SB * j + SB].reshape(8, 48, SB)

    def grad_copies(u, slot):
        found = []
        for which in range(2):
            for r in range(2):
                found.append(
                    pltpu.make_async_copy(
                        grads.at[slot, which, r],
                        o_grad.at[which, r, pl.ds(2 * u, 2)],
                        grad_sem.at[slot, which, r],
                    )
                )
        return found

    for j in range(4, NPIECE):
        finish_near(j)

    def forward_rest():
        second(7)
        third(6)

    feed(m, True, 0, forward_rest)
    for g in grad_copies(m, 0):
        g.start()
    third(7)
    feed(ms, False, 1)
    for g in grad_copies(ms, 1):
        g.start()
    for j in range(4, NPIECE):
        finish_far(j)
    for g in grad_copies(m, 0):
        g.wait()
    feed(my, False, 0)
    for g in grad_copies(my, 0):
        g.start()
    for g in grad_copies(ms, 1):
        g.wait()
    feed(mys, False, 1)
    for g in grad_copies(mys, 1):
        g.start()

    lane = lax.broadcasted_iota(jnp.int32, (1, D), 1)

    @pl.loop(0, 4)
    def _(r):
        rows = pl.ds(pl.multiple_of(r * 256, 256), 256)
        a = attn[rows, :]
        normed, inv = row_norm(tokens[rows, :].astype(F32) + g0 * a)
        plain = normed * gain[...] + bias[...]
        back = cot[rows, :].astype(F32)
        br = branch[rows, :]
        outv[rows, :] = (plain * mgate[...] + g1 * br).astype(BF)
        total = back + hback[rows, :]
        masked = total * mgate[...]
        small[4:5, :] += colsum(masked * normed)
        small[5:6, :] += colsum(masked)
        small[6:7, :] += colsum(total * plain)
        n = masked * gain[...]
        grad = (
            n
            - jnp.mean(n, axis=-1, keepdims=True)
            - normed * jnp.mean(n * normed, axis=-1, keepdims=True)
        ) * inv
        hback[rows, :] = grad
        small[7:8, :] += colsum(grad * a)
        small[8:9, :] += colsum(back * br)

    out_copy = pltpu.make_async_copy(outv, o_out, out_sem.at[6])
    out_copy.start()
    sgrad_copy = pltpu.make_async_copy(hback, o_sgrad, out_sem.at[7])
    sgrad_copy.start()
    for g in grad_copies(my, 0):
        g.wait()
    for g in grad_copies(mys, 1):
        g.wait()
    for copy in (tok_copy, wq_copy, joined_copy, ctx_copy, ctxT_copy, wo_copy, out_copy, sgrad_copy):
        copy.wait()
    for j in range(NPIECE):
        finish_sends(j)


def run_forward(*arrays):
    sds = jax.ShapeDtypeStruct
    outs = (
        sds((ROWS, D), BF),
        sds((ROWS, 3 * D), BF),
        sds((ROWS, D), BF),
        sds((D, ROWS), BF),
        sds((D, ROWS), BF),
        sds((ROWS, D), F32),
        sds((2, 2, 8, 8, 48, SB), BF),
        sds((4, 192, 3 * D), BF),
        sds((4, 192, D), BF),
        sds((24, 1, BLK), F32),
        sds((16, D), F32),
    )
    any_ = pl.BlockSpec(memory_space=pl.ANY)
    vm = pl.BlockSpec(memory_space=pltpu.VMEM)
    sm = pl.BlockSpec(memory_space=pltpu.SMEM)
    return pl.pallas_call(
        forward_kernel,
        out_shape=outs,
        in_specs=[sm] * 2 + [vm] * 7 + [any_] * 4,
        out_specs=[any_] * 9 + [vm] * 2,
        scratch_shapes=[
            pltpu.VMEM((4, 192, 3 * D), BF),
            pltpu.VMEM((4, 192, D), BF),
            pltpu.VMEM((4, D, D), BF),
            pltpu.VMEM((4, D, D), BF),
            pltpu.VMEM((ROWS, 3 * D), BF),
            pltpu.VMEM((ROWS, D), BF),
            pltpu.VMEM((D, ROWS), BF),
            pltpu.VMEM((D, ROWS), BF),
            pltpu.VMEM((ROWS, D), F32),
            pltpu.VMEM((ROWS, D), BF),
            pltpu.VMEM((D, ROWS), BF),
            pltpu.VMEM((ROWS, D), BF),
            pltpu.VMEM((D, ROWS), BF),
            pltpu.VMEM((ROWS, D), F32),
            pltpu.VMEM((ROWS, D), F32),
            pltpu.VMEM((ROWS, D), BF),
            pltpu.VMEM((ROWS, D), BF),
            pltpu.VMEM((2, 2, 2, 2, 8, 48, SB), BF),
            pltpu.VMEM((ROWS, D), BF),
            pltpu.VMEM((2, BLK, 1), jnp.int32),
            pltpu.VMEM((4, 1, D), F32),
            pltpu.VMEM((8, D), F32),
            pltpu.SemaphoreType.DMA((NPIECE, 5)),
            pltpu.SemaphoreType.DMA((NPIECE, 5)),
            pltpu.SemaphoreType.DMA((NPIECE,)),
            pltpu.SemaphoreType.DMA((8,)),
            pltpu.SemaphoreType.DMA((2, 2, 2)),
        ],
        compiler_params=pltpu.CompilerParams(
            collective_id=1, has_side_effects=True, vmem_limit_bytes=64 << 20
        ),
    )(*arrays)


SENT = (12, 13, 14, 15, 0, 2, 4, 6, 8, 10, 1, 3, 5, 7, 9, 11)
GROUPS = ((0, 8), (8, 8), (16, 8), (24, 8), (32, 4), (36, 6), (42, 6))
FF_BLOCKS = 32
PARTS = 3
PER = 6 // PARTS


def backward_kernel(
    gates,
    heads,
    order,
    small_in,
    segs,
    lse,
    g_in,
    joined_in,
    ctx_in,
    ctxT_in,
    tokT_in,
    sgrad_in,
    wq_in,
    wo_in,
    o_igrad,
    o_full,
    small_out,
    joined,
    ctx,
    ctxT,
    tokT,
    sgrad,
    wq,
    wo,
    outb,
    cgrad,
    igrad,
    half,
    ga,
    got1,
    got2,
    got3,
    part,
    gotz,
    total,
    slots,
    gz,
    gfull,
    sm,
    gots,
    segcol,
    hrow,
    hcol,
    load_sem,
    half_sem,
    send_sem,
    recv_sem,
    z_send,
    z_recv,
    a_send,
    a_recv,
    f_send,
    f_recv,
    s_send,
    s_recv,
    out_sem,
):
    z, x, y, c = coords()
    g0 = gates[0]
    sib = at(z, x, y, 1 - c)
    ypeer = at(z, x, 1 - y, c)
    xpeer = at(z, 1 - x, y, c)
    diag = at(z, 1 - x, 1 - y, c)
    zpeers = [at((z + k) % 4, x, y, c) for k in (1, 2, 3)]

    loads = [
        pltpu.make_async_copy(src, dst, load_sem.at[i])
        for i, (src, dst) in enumerate(
            (
                (sgrad_in, sgrad),
                (wo_in, wo),
                (ctx_in, ctx),
                (ctxT_in, ctxT),
                (joined_in, joined),
                (tokT_in, tokT),
                (wq_in, wq),
            )
        )
    ]
    halves_in = [
        pltpu.make_async_copy(
            g_in.at[pl.ds(8 * g, 8), c], half.at[pl.ds(8 * g, 8)], half_sem.at[g]
        )
        for g in range(4)
    ]
    for copy in loads[:4]:
        copy.start()

    barrier = pltpu.get_barrier_semaphore()
    for peer in [sib, ypeer, xpeer, diag] + zpeers:
        pl.semaphore_signal(barrier, inc=1, device_id=peer, device_id_type=MESH)
    pl.semaphore_wait(barrier, 7)

    def remote(src, dst, sems, dev):
        return pltpu.make_async_remote_copy(
            src_ref=src,
            dst_ref=dst,
            send_sem=sems[0],
            recv_sem=sems[1],
            device_id=dev,
            device_id_type=MESH,
        )

    def pair(g, k):
        return send_sem.at[g, k], recv_sem.at[g, k]

    def block(n):
        def ref(i):
            return half.at[i] if n < FF_BLOCKS else ga.at[i - FF_BLOCKS, c]

        return ref

    def mine(g, first, count):
        base = GROUPS[g][0] + first
        if base < FF_BLOCKS:
            return half.at[pl.ds(base, count)]
        return ga.at[pl.ds(base - FF_BLOCKS, count), c]

    def swap1(g):
        base, count = GROUPS[g]
        if base < FF_BLOCKS:
            src = g_in.at[pl.ds(base, count), 1 - c]
        else:
            src = ga.at[pl.ds(base - FF_BLOCKS, count), 1 - c]
        return remote(src, got1.at[pl.ds(base, count)], pair(g, 0), sib)

    def swap2(g):
        base, count = GROUPS[g]
        n = count // 2
        return (
            remote(mine(g, 0, n).at[:, 1 - y], got2.at[pl.ds(base, n)], pair(g, 1), ypeer),
            remote(
                mine(g, n, n).at[:, :, 1 - x], got2.at[pl.ds(base + n, n)], pair(g, 2), xpeer
            ),
        )

    def swap3(g):
        base, count = GROUPS[g]
        n = count // 2
        return (
            remote(mine(g, 0, n).at[:, y, 1 - x], got3.at[pl.ds(base, n)], pair(g, 3), xpeer),
            remote(
                mine(g, n, n).at[:, 1 - y, x], got3.at[pl.ds(base + n, n)], pair(g, 4), ypeer
            ),
        )

    def plus(left, right):
        return (left.astype(F32) + right.astype(F32)).astype(BF)

    def step1(g):
        base, count = GROUPS[g]
        if g < 4:
            halves_in[g].wait()
        swap1(g).wait_recv()

        @pl.loop(base, base + count)
        def _(i):
            ref = block(base)(i)
            ref[...] = plus(ref[...], got1[i])

        for copy in swap2(g):
            copy.start()

    def step2(g):
        base, count = GROUPS[g]
        n = count // 2
        for copy in swap2(g):
            copy.wait_recv()

        @pl.loop(base, base + n)
        def _(i):
            ref = block(base)(i)
            ref[y] = plus(ref[y], got2[i])

        @pl.loop(base + n, base + count)
        def _(i):
            ref = block(base)(i)
            ref[0, x] = plus(ref[0, x], got2[i, 0])
            ref[1, x] = plus(ref[1, x], got2[i, 1])

        for copy in swap3(g):
            copy.start()

    spare = 1 + c

    def unit(zz):
        return zz - (zz + 3 - spare) // 4

    def swapz(g, k):
        base, count = GROUPS[g]
        return remote(
            part.at[pl.ds(base, count), unit((z + k) % 4)],
            gotz.at[k - 1, pl.ds(base, count)],
            (z_send.at[g, k - 1], z_recv.at[g, k - 1]),
            zpeers[k - 1],
        )

    def step3(g):
        base, count = GROUPS[g]
        for copy in swap3(g):
            copy.wait_recv()

        @pl.loop(base, base + count)
        def _(i):
            part[i] = plus(block(base)(i)[y, x], got3[i]).reshape(3, 16, SB)

        for k in (1, 2, 3):

            @pl.when((z + k) % 4 != spare)
            def _(k=k):
                swapz(g, k).start()

    def step4(g):
        base, count = GROUPS[g]

        @pl.when(z != spare)
        def _():
            for k in (1, 2, 3):
                swapz(g, k).wait_recv()

            @pl.loop(base, base + count)
            def _(i):
                value = part[i, unit(z)].astype(F32)
                for k in range(3):
                    value = value + gotz[k, i].astype(F32)
                total[i] = value.astype(BF)

    small_peers = [sib, ypeer, xpeer, diag] + zpeers
    small_stage = ((0,), (1, 2, 3), (4, 5, 6))

    def small_copy(k):
        stage = 0 if k == 0 else 1 if k < 4 else 2
        return remote(sm.at[stage], gots.at[k], (s_send.at[k], s_recv.at[k]), small_peers[k])

    def small_send(stage):
        for k in small_stage[stage]:
            small_copy(k).start()

    def small_take(stage):
        value = sm[stage]
        for k in small_stage[stage]:
            small_copy(k).wait_recv()
            value = value + gots[k]
        if stage < 2:
            sm[stage + 1] = value
            small_send(stage + 1)
        else:
            small_out[...] = value

    for g in range(4):
        swap1(g).start()
        halves_in[g].start()
    for copy in loads[4:]:
        copy.start()

    columns_of(segs, segcol)
    hrow[...] = head_lanes(heads)
    hcol[...] = jnp.broadcast_to(hrow[...], (8, D)).T[:, 0:1]
    hgate = hrow
    sm[0] = small_in[...]
    step1(0)
    loads[0].wait()
    loads[1].wait()
    loads[2].wait()

    @pl.loop(0, 4)
    def _(r):
        rows = pl.ds(pl.multiple_of(r * 256, 256), 256)
        low = (g0 * sgrad[rows, :]).astype(BF)
        outb[rows, :] = low
        grad = nt(low, wo[...].reshape(D, D)).astype(BF)
        sm[0, 9:10, :] += colsum(ctx[rows, :].astype(F32) * grad.astype(F32))
        cgrad[rows, :] = grad * hgate[...].astype(BF)

    small_send(0)
    step1(1)
    loads[3].wait()

    def weight_tiles(left, right, lane, rowgate, places):
        @pl.loop(0, 2)
        def _(r):
            rr = pl.ds(pl.multiple_of(r * SB, 128), SB)
            g = nn(left[rr, :], right[:, pl.ds(lane, SB)])
            if rowgate is not None:
                g = g * rowgate[rr, :]
            ga[places[0] + r * (places[1] - places[0])] = g.astype(BF).reshape(2, 2, 2, 48, SB)

    for j in range(2):
        weight_tiles(ctxT, outb, SB * j, hcol, (SENT.index(12 + j), SENT.index(14 + j)))

    swap1(4).start()
    step1(2)
    step1(3)
    loads[4].wait()

    scale = LOG2E / math.sqrt(HD)
    factor = 1.0 / math.sqrt(HD)
    half_iota = lax.broadcasted_iota(jnp.int32, (1, 128), 1) // HD
    halves = [(half_iota == e).astype(F32).astype(BF) for e in range(2)]

    def attend_back(i):
        p = i // 2
        b = i % 2
        rows = pl.ds(pl.multiple_of(b * BLK, BLK), BLK)
        lane = pl.multiple_of(p * 128, 128)
        q = joined[rows, pl.ds(lane, 128)]
        k = joined[rows, pl.ds(D + lane, 128)]
        v = joined[rows, pl.ds(2 * D + lane, 128)]
        do = cgrad[rows, pl.ds(lane, 128)]
        sc = segcol[b]
        sr = segs[pl.ds(b, 1), :]
        dv = None
        dk = None
        for qt in range(2):
            cols = slice(qt * 256, qt * 256 + 256)
            allowed = sc == sr[:, cols]
            dqT = None
            for e in range(2):
                ke = k * halves[e]
                s = nt(ke, q[cols])
                s = jnp.where(allowed, s * scale, MASKED)
                pr = jnp.exp2(s - lse[2 * (b * 6 + p) + e, :, pl.ds(qt * 256, 256)])
                dp = nt(v * halves[e], do[cols])
                delta = jnp.sum(pr * dp, axis=0, keepdims=True)
                ds = (pr * (dp - delta)).astype(BF)
                dv_part = nn(pr.astype(BF), do[cols] * halves[e])
                dk_part = nn(ds, q[cols] * halves[e])
                dq_part = nn(ke.T, ds)
                dv = dv_part if dv is None else dv + dv_part
                dk = dk_part if dk is None else dk + dk_part
                dqT = dq_part if dqT is None else dqT + dq_part
            qrows = pl.ds(pl.multiple_of(b * BLK + qt * 256, 256), 256)
            joined[qrows, pl.ds(lane, 128)] = (dqT * factor).T.astype(BF)
        joined[rows, pl.ds(D + lane, 128)] = (dk * factor).astype(BF)
        joined[rows, pl.ds(2 * D + lane, 128)] = dv.astype(BF)

    def qkv_tiles(h):
        for j in (h, 2 + h, 4 + h):
            weight_tiles(tokT, joined, SB * j, None, (SENT.index(j), SENT.index(6 + j)))

    def middle():
        loads[5].wait()
        qkv_tiles(0)
        swap1(5).start()

    plan = {
        0: [lambda: small_take(0)],
        1: [lambda: step1(4)],
        2: [lambda: step2(0)],
        4: [lambda: step2(1)],
        5: [middle],
        6: [lambda: step1(5), lambda: step2(2)],
        7: [lambda: small_take(1)],
        8: [lambda: step2(3)],
        9: [lambda: step3(0), lambda: step2(4)],
        11: [lambda: small_take(2), lambda: step3(1)],
    }

    @pl.loop(0, 12)
    def _(i):
        attend_back(i)
        for at_step, todo in plan.items():

            @pl.when(i == at_step)
            def _(todo=todo):
                for f in todo:
                    f()

    qkv_tiles(1)
    swap1(6).start()
    loads[6].wait()

    def input_rows(lo, hi):
        @pl.loop(lo, hi)
        def _(r):
            rows = pl.ds(pl.multiple_of(r * 256, 256), 256)
            igrad[rows, :] = sgrad[rows, :] + nt(joined[rows, :], wq[...].reshape(D, 3 * D))

    step3(2)
    step2(5)
    step1(6)
    input_rows(0, 1)
    step4(0)
    step3(3)
    input_rows(1, 2)
    step4(1)
    step3(4)
    input_rows(2, 3)
    step4(2)
    step3(5)
    input_rows(3, 4)
    igrad_copy = pltpu.make_async_copy(igrad, o_igrad, out_sem.at[0])
    igrad_copy.start()
    step2(6)
    step4(3)
    step4(4)
    step4(5)
    step3(6)
    step4(6)

    def deal(n, k, to, u):
        return remote(
            slots.at[to, :, n],
            gz.at[:, n, :, u],
            (a_send.at[n, k - 1], a_recv.at[n, k - 1]),
            zpeers[k - 1],
        )

    @pl.when(z != spare)
    def _():
        @pl.loop(0, 48)
        def _(s):
            slots[s // 12, s // 6 % 2, s // PER % PARTS, s % PER] = total[order[s]]

        for n in range(PARTS):
            for k in (1, 2, 3):
                deal(n, k, (z + k) % 4, unit(z)).start()
            gz[:, n, :, unit(z)] = slots[z, :, n]

    def piece(n, cc, yy, xx):
        return gfull.at[n, :, 4 * cc + 2 * yy + xx]

    others = ((y, 1 - x), (1 - y, x), (1 - y, 1 - x))

    def near(n, k):
        src = gz.at[1 - x if k in (0, 2) else x, n]
        sems = (f_send.at[n, k], f_recv.at[n, k])
        return remote(src, piece(n, c, y, x), sems, (xpeer, ypeer, diag, sib)[k])

    def onward(n, k):
        yy, xx = others[k]
        to = piece(n, c, yy, xx)
        return remote(to, to, (f_send.at[n, 4 + k], f_recv.at[n, 4 + k]), sib)

    def pass_on(n):
        for k in range(3):
            near(n, k).wait_recv()
            onward(n, k).start()

    for n in range(PARTS):
        for k in (1, 2, 3):
            sender = (z + 4 - k) % 4

            @pl.when(sender != spare)
            def _(n=n, k=k, sender=sender):
                deal(n, k, z, unit(sender)).wait_recv()

        for k in range(4):
            near(n, k).start()
        gfull[n, :, 4 * c + 2 * y + x] = gz[x, n]
        if n:
            pass_on(n - 1)
    pass_on(PARTS - 1)
    for n in range(PARTS):
        near(n, 3).wait_recv()
        for k in range(3):
            onward(n, k).wait_recv()
    full_copy = pltpu.make_async_copy(gfull, o_full, out_sem.at[2])
    full_copy.start()
    for n in range(PARTS):
        for k in range(4):
            near(n, k).wait_send()
        for k in range(3):
            onward(n, k).wait_send()

        @pl.when(z != spare)
        def _(n=n):
            for k in (1, 2, 3):
                deal(n, k, (z + k) % 4, unit(z)).wait_send()

    for g in range(len(GROUPS)):
        for k in (1, 2, 3):

            @pl.when((z + k) % 4 != spare)
            def _(g=g, k=k):
                swapz(g, k).wait_send()

    for k in range(7):
        small_copy(k).wait_send()
    for g in range(len(GROUPS)):
        for copy in (swap1(g),) + swap2(g) + swap3(g):
            copy.wait_send()
    igrad_copy.wait()
    full_copy.wait()


def run_backward(*arrays):
    sds = jax.ShapeDtypeStruct
    outs = (sds((ROWS, D), F32), sds((PARTS, PER, 8, 3, 16, SB), BF), sds((16, D), F32))
    any_ = pl.BlockSpec(memory_space=pl.ANY)
    vm = pl.BlockSpec(memory_space=pltpu.VMEM)
    sm = pl.BlockSpec(memory_space=pltpu.SMEM)
    dma = pltpu.SemaphoreType.DMA
    return pl.pallas_call(
        backward_kernel,
        out_shape=outs,
        in_specs=[sm] * 3 + [vm] * 3 + [any_] * 8,
        out_specs=[any_] * 2 + [vm],
        scratch_shapes=[
            pltpu.VMEM((ROWS, 3 * D), BF),
            pltpu.VMEM((ROWS, D), BF),
            pltpu.VMEM((D, ROWS), BF),
            pltpu.VMEM((D, ROWS), BF),
            pltpu.VMEM((ROWS, D), F32),
            pltpu.VMEM((4, 192, 3 * D), BF),
            pltpu.VMEM((4, 192, D), BF),
            pltpu.VMEM((ROWS, D), BF),
            pltpu.VMEM((ROWS, D), BF),
            pltpu.VMEM((ROWS, D), F32),
            pltpu.VMEM((32, 2, 2, 48, SB), BF),
            pltpu.VMEM((16, 2, 2, 2, 48, SB), BF),
            pltpu.VMEM((48, 2, 2, 48, SB), BF),
            pltpu.VMEM((48, 2, 48, SB), BF),
            pltpu.VMEM((48, 48, SB), BF),
            pltpu.VMEM((48, 3, 16, SB), BF),
            pltpu.VMEM((3, 48, 16, SB), BF),
            pltpu.VMEM((48, 16, SB), BF),
            pltpu.VMEM((4, 2, PARTS, PER, 16, SB), BF),
            pltpu.VMEM((2, PARTS, PER, 3, 16, SB), BF),
            pltpu.VMEM((PARTS, PER, 8, 3, 16, SB), BF),
            pltpu.VMEM((3, 16, D), F32),
            pltpu.VMEM((7, 16, D), F32),
            pltpu.VMEM((2, BLK, 1), jnp.int32),
            pltpu.VMEM((1, D), F32),
            pltpu.VMEM((D, 1), F32),
            dma((7,)),
            dma((4,)),
            dma((7, 5)),
            dma((7, 5)),
            dma((7, 3)),
            dma((7, 3)),
            dma((PARTS, 3)),
            dma((PARTS, 3)),
            dma((PARTS, 7)),
            dma((PARTS, 7)),
            dma((7,)),
            dma((7,)),
            dma((3,)),
        ],
        compiler_params=pltpu.CompilerParams(
            collective_id=2, has_side_effects=True, vmem_limit_bytes=64 << 20
        ),
    )(*arrays)


def split(value):
    high = value.astype(BF)
    return high, (value - high.astype(F32)).astype(BF)


def update_kernel(
    small,
    gain,
    bias,
    full,
    master,
    left_stats,
    right_stats,
    left_root,
    right_root,
    out_in,
    igrad_in,
    o_grad,
    o_left,
    o_right,
    o_new,
    o_copy,
    o_unit,
    o_hidden,
    o_head,
    o_layer,
    o_norm,
    o_norm_new,
    o_out,
    o_igrad,
    turned,
    stage_out,
    stage_igrad,
    sem,
):
    slot = pl.program_id(0)
    moves_in = (
        pltpu.make_async_copy(out_in, stage_out, sem.at[0]),
        pltpu.make_async_copy(igrad_in, stage_igrad, sem.at[1]),
    )
    moves = (
        pltpu.make_async_copy(stage_out, o_out, sem.at[2]),
        pltpu.make_async_copy(stage_igrad, o_igrad, sem.at[3]),
    )

    @pl.when(slot == 0)
    def _():
        for move in moves_in:
            move.start()
        for i in range(4):
            o_unit[6 * i : 6 * i + 6, :] = many_rows(small[i : i + 1, :])
        o_hidden[...] = many_rows(small[6:7, :])
        o_norm[...] = small[4:6, :]
        rate = 0.2 / math.sqrt(ROWS * 32)
        o_norm_new[0:1, :] = one_row(gain[...]) - rate * small[4:5, :]
        o_norm_new[1:2, :] = one_row(bias[...]) - rate * small[5:6, :]
        lane = lax.broadcasted_iota(jnp.int32, (16, D), 1) // HD
        row = lax.broadcasted_iota(jnp.int32, (16, D), 0)
        by_head = jnp.sum(jnp.where(lane == row, small[9:10, :], 0.0), axis=1, keepdims=True)
        square = lax.broadcasted_iota(jnp.int32, (16, 128), 1)
        diagonal = square == lax.broadcasted_iota(jnp.int32, (16, 128), 0)
        o_head[...] = jnp.sum(jnp.where(diagonal, by_head, 0.0), axis=0, keepdims=True)[:, :12]
        pair = jnp.sum(small[7:9, :], axis=1, keepdims=True)
        first = lax.broadcasted_iota(jnp.int32, (1, 2), 1) == 0
        o_layer[...] = jnp.where(first, pair[0:1], pair[1:2])

    start = pl.multiple_of(lax.axis_index("mp") * 96, 16)
    own = full[0, pl.ds(start, 96), :]
    whole = full[0]
    o_grad[0] = own.astype(F32)
    o_left[0] = BETA * left_stats[0] + (1.0 - BETA) * nt(own, whole)
    turned[...] = whole.T
    o_right[0] = BETA * right_stats[0] + (1.0 - BETA) * nn(turned[pl.ds(start, 96), :], whole)
    root_high, root_low = split(left_root[0])
    left_part = nn(root_high, whole) + nn(root_low, whole)
    part_high, part_low = split(left_part)
    right_high, right_low = split(right_root[0])
    update = nn(part_high, right_high) + nn(part_low, right_high) + nn(part_high, right_low)
    new = master[0] - RATE * update
    o_new[0] = new
    o_copy[0] = new.astype(BF)

    @pl.when(slot == 2)
    def _():
        for first, then in zip(moves_in, moves):
            first.wait()
            then.start()

    @pl.when(slot == 5)
    def _():
        for move in moves:
            move.wait()


def run_update(*arrays):
    sds = jax.ShapeDtypeStruct
    whole = pl.BlockSpec((1, SB, SB), lambda s: (s, 0, 0))
    rows = pl.BlockSpec((1, 96, SB), lambda s: (s, 0, 0))
    any_ = pl.BlockSpec(memory_space=pl.ANY)

    def const(*shape):
        return pl.BlockSpec(shape, lambda s: (0, 0))

    flat = const(6, 128)
    return pl.pallas_call(
        update_kernel,
        grid=(6,),
        out_shape=(sds((6, 96, SB), F32),) * 4
        + (
            sds((6, 96, SB), BF),
            sds((24, 128), F32),
            sds((6, 128), F32),
            sds((1, 12), F32),
            sds((1, 2), F32),
            sds((2, D), F32),
            sds((2, D), F32),
            sds((ROWS, D), BF),
            sds((ROWS, D), F32),
        ),
        in_specs=[const(16, D), flat, flat, whole] + [rows] * 4 + [whole] + [any_] * 2,
        out_specs=[rows] * 5
        + [const(24, 128), flat, const(1, 12), const(1, 2), const(2, D), const(2, D), any_, any_],
        scratch_shapes=[
            pltpu.VMEM((SB, SB), BF),
            pltpu.VMEM((ROWS, D), BF),
            pltpu.VMEM((ROWS, D), F32),
            pltpu.SemaphoreType.DMA((4,)),
        ],
        compiler_params=pltpu.CompilerParams(vmem_limit_bytes=64 << 20),
    )(*arrays)


PLACE = tuple(FF_BLOCKS + SENT.index(b) for b in range(16)) + tuple(range(32))


def fast_body(
    tokens,
    segments,
    head_mask,
    unit_mask,
    hidden_mask,
    layer_gates,
    qkv_weight,
    out_weight,
    norm_gain,
    norm_bias,
    up_weight,
    down_weight,
    cotangent,
    owner_slot,
    master,
    left_stats,
    right_stats,
    left_root,
    right_root,
):
    gain = norm_gain.reshape(6, 128)
    bias = norm_bias.reshape(6, 128)
    (output, joined, ctx, ctxT, tokT, summed_grad, ff_grad, wq, wo, lse, small) = run_forward(
        layer_gates,
        head_mask,
        tokens,
        cotangent,
        segments,
        unit_mask.reshape(24, 128),
        hidden_mask.reshape(6, 128),
        gain,
        bias,
        qkv_weight,
        out_weight,
        up_weight,
        down_weight,
    )
    slot_order = jnp.sum(
        jnp.where(owner_slot[None, :] == jnp.arange(48)[:, None], jnp.asarray(PLACE)[None, :], 0), axis=1
    )
    input_grad, full, small = run_backward(
        layer_gates,
        head_mask,
        slot_order,
        small,
        segments,
        lse,
        ff_grad.reshape(32, 2, 2, 2, 48, SB),
        joined,
        ctx,
        ctxT,
        tokT,
        summed_grad,
        wq,
        wo,
    )
    (
        owned,
        left_new,
        right_new,
        weight_new,
        weight_copy,
        unit_grad,
        hidden_grad,
        head_grad,
        layer_grad,
        norm_grad,
        norm_new,
        output,
        input_grad,
    ) = run_update(
        small,
        gain,
        bias,
        full.reshape(6, SB, SB),
        master,
        left_stats,
        right_stats,
        left_root,
        right_root,
        output,
        input_grad,
    )
    return (
        output,
        input_grad,
        head_grad.reshape(12),
        unit_grad.reshape(FF),
        hidden_grad.reshape(D),
        layer_grad.reshape(2),
        norm_grad,
        norm_new,
        owned,
        left_new,
        right_new,
        weight_new,
        weight_copy,
    )


def solution(mesh):
    return jax.shard_map(
        fast_body if dict(mesh.shape) == {"dp": 8, "mp": 4} else body,
        mesh=mesh,
        in_specs=(
            P(("dp", "mp"), None),
            P(("dp", "mp"), None),
            P(),
            P(),
            P(),
            P(),
            P("mp", None),
            P("mp", None),
            P(),
            P(),
            P(None, "mp"),
            P(None, "mp"),
            P(("dp", "mp"), None),
            P(),
            P("dp", "mp", None),
            P("dp", "mp", None),
            P("dp", "mp", None),
            P("dp", "mp", None),
            P("dp", None, None),
        ),
        out_specs=(
            P(("dp", "mp"), None),
            P(("dp", "mp"), None),
            P(),
            P(),
            P(),
            P(),
            P(),
            P(),
            P("dp", "mp", None),
            P("dp", "mp", None),
            P("dp", "mp", None),
            P("dp", "mp", None),
            P("dp", "mp", None),
        ),
        check_vma=False,
    )
```

```python
from functools import partial
import math

import jax
import jax.numpy as jnp
from jax import lax
from jax.experimental import pallas as pl
from jax.experimental.pallas import tpu as pltpu
from jax.sharding import PartitionSpec as P

FF = 3072
SB = 384


HIGH = lax.Precision.HIGHEST
BETA = 0.5
RATE = 0.5
EPS = 1e-12
MASKED = -1e30


def gelu_exact(values):
    return jax.nn.gelu(values, approximate=False)


def normalize(summed, gain_in, offset, hidden_gate):
    centre = summed - jnp.mean(summed, axis=-1, keepdims=True)
    spread = jnp.mean(centre * centre, axis=-1, keepdims=True)
    return (centre * lax.rsqrt(spread + EPS) * gain_in + offset) * hidden_gate


def split_heads(block_joined, head_count):
    pieces = block_joined.reshape(block_joined.shape[0], 3, head_count, -1)
    return (pieces[:, 0], pieces[:, 1], pieces[:, 2])


def masked_scores(queries, keys_in, labels, factor):
    scores = (
        jnp.einsum("qhd,khd->hqk", queries, keys_in, preferred_element_type=jnp.float32) * factor
    )
    allowed = labels[:, None] == labels[None, :]
    return jnp.where(allowed[None], scores, MASKED)


def attend_forward(packed, head_count, factor):
    block_joined, labels = packed
    queries, keys_in, values_in = split_heads(block_joined, head_count)
    scores = masked_scores(queries, keys_in, labels, factor)
    highest = jnp.max(scores, axis=-1, keepdims=True)
    raised = jnp.exp(scores - highest)
    totals = jnp.sum(raised, axis=-1, keepdims=True)
    weights_low = (raised / totals).astype(jnp.bfloat16)
    context = jnp.einsum("hqk,khd->qhd", weights_low, values_in, preferred_element_type=jnp.float32)
    return (context, (highest + jnp.log(totals))[:, :, 0])


def attend_backward(packed, head_count, factor):
    block_joined, log_totals, context_grad, labels = packed
    queries, keys_in, values_in = split_heads(block_joined, head_count)
    scores = masked_scores(queries, keys_in, labels, factor)
    weights_full = jnp.exp(scores - log_totals[:, :, None])
    weights_low = weights_full.astype(jnp.bfloat16)
    values_grad = jnp.einsum(
        "hqk,qhd->khd", weights_low, context_grad, preferred_element_type=jnp.float32
    )
    weights_grad = jnp.einsum(
        "qhd,khd->hqk", context_grad, values_in, preferred_element_type=jnp.float32
    )
    inner_sum = jnp.sum(weights_full * weights_grad, axis=-1, keepdims=True)
    scores_grad = (weights_full * (weights_grad - inner_sum)).astype(jnp.bfloat16)
    queries_grad = (
        jnp.einsum("hqk,khd->qhd", scores_grad, keys_in, preferred_element_type=jnp.float32)
        * factor
    )
    keys_grad = (
        jnp.einsum("hqk,qhd->khd", scores_grad, queries, preferred_element_type=jnp.float32)
        * factor
    )
    merged = jnp.concatenate([queries_grad, keys_grad, values_grad], axis=1)
    return merged.reshape(merged.shape[0], -1).astype(jnp.bfloat16)


def contract_rows(left, right):
    return lax.dot_general(
        left, right, (((0,), (0,)), ((), ())), preferred_element_type=jnp.float32
    )


def contract_cols(left, right):
    return lax.dot_general(
        left, right, (((1,), (1,)), ((), ())), preferred_element_type=jnp.float32
    )


def body(
    tokens,
    segments,
    head_mask,
    unit_mask,
    hidden_mask,
    layer_gates,
    qkv_weight,
    out_weight,
    norm_gain,
    norm_bias,
    up_weight,
    down_weight,
    cotangent,
    owner_slot,
    master,
    left_stats,
    right_stats,
    left_root,
    right_root,
):
    row_count = tokens.shape[0]
    width = tokens.shape[1]
    head_count = head_mask.shape[0]
    head_width = width // head_count
    block_rows = segments.shape[1]
    block_count = segments.shape[0]
    factor = 1.0 / math.sqrt(head_width)
    model_size = lax.axis_size("mp")
    share = FF // model_size
    part_rows = SB // model_size
    total_tokens = row_count * lax.axis_size("dp") * model_size
    head_gate = head_mask.astype(jnp.float32)
    unit_gate = unit_mask.astype(jnp.float32)
    hidden_gate = hidden_mask.astype(jnp.float32)
    inputs = tokens.astype(jnp.float32)
    back_full = cotangent.astype(jnp.float32)
    qkv_full, out_full, up_full, down_full = (
        lax.all_gather(qkv_weight, "mp", axis=0, tiled=True),
        lax.all_gather(out_weight, "mp", axis=0, tiled=True),
        lax.all_gather(up_weight, "mp", axis=1, tiled=True),
        lax.all_gather(down_weight, "mp", axis=1, tiled=True),
    )
    joined_qkv = jnp.dot(tokens, qkv_full, preferred_element_type=jnp.float32).astype(jnp.bfloat16)
    joined_blocks = joined_qkv.reshape(block_count, block_rows, 3 * width)
    context, log_totals = lax.map(
        partial(attend_forward, head_count=head_count, factor=factor), (joined_blocks, segments)
    )
    context = context.reshape(row_count, head_count, head_width)
    gated_low = (context * head_gate[None, :, None]).reshape(row_count, width).astype(jnp.bfloat16)
    attn_out = jnp.dot(gated_low, out_full, preferred_element_type=jnp.float32)
    summed = inputs + layer_gates[0] * attn_out
    hidden, norm_pull = jax.vjp(normalize, summed, norm_gain, norm_bias, hidden_gate)
    hidden_low = hidden.astype(jnp.bfloat16)
    pre_act = jnp.dot(hidden_low, up_full, preferred_element_type=jnp.float32)
    active, gelu_pull = jax.vjp(gelu_exact, pre_act)
    active_low = (active * unit_gate).astype(jnp.bfloat16)
    branch = contract_cols(active_low, down_full)
    output = (hidden + layer_gates[1] * branch).astype(jnp.bfloat16)
    back_rounded = (layer_gates[1] * back_full).astype(jnp.bfloat16)
    qkv_full, out_full, up_full, down_full = (
        lax.all_gather(qkv_weight, "mp", axis=0, tiled=True),
        lax.all_gather(out_weight, "mp", axis=0, tiled=True),
        lax.all_gather(up_weight, "mp", axis=1, tiled=True),
        lax.all_gather(down_weight, "mp", axis=1, tiled=True),
    )
    grad_active = jnp.dot(back_rounded, down_full, preferred_element_type=jnp.float32)
    unit_grad = jnp.sum(grad_active * active, axis=0)
    grad_inner = gelu_pull(grad_active * unit_gate)[0].astype(jnp.bfloat16)
    hidden_back = contract_cols(grad_inner, up_full)
    up_term = contract_rows(grad_inner, hidden_low)
    down_term = contract_rows(active_low, back_rounded)
    unit_local = (
        lax.psum_scatter(
            jnp.stack([up_term, down_term], axis=1).astype(jnp.bfloat16),
            "mp",
            scatter_dimension=0,
            tiled=True,
        )
        .astype(jnp.float32)
        .transpose(1, 2, 0)
    )
    summed_grad, gain_grad, bias_grad, mask_grad = norm_pull(back_full + hidden_back)
    layer_grad = jnp.stack([jnp.sum(summed_grad * attn_out), jnp.sum(back_full * branch)])
    out_back = (layer_gates[0] * summed_grad).astype(jnp.bfloat16)
    gated_grad = contract_cols(out_back, out_full).astype(jnp.bfloat16)
    gated_heads = gated_grad.reshape(row_count, head_count, head_width)
    head_grad = jnp.sum(context * gated_heads.astype(jnp.float32), axis=(0, 2))
    context_grad = gated_heads * head_mask.astype(jnp.bfloat16)[None, :, None]
    joined_grad = lax.map(
        partial(attend_backward, head_count=head_count, factor=factor),
        (
            joined_blocks,
            log_totals,
            context_grad.reshape(block_count, block_rows, head_count, head_width),
            segments,
        ),
    )
    joined_grad = joined_grad.reshape(row_count, 3 * width)
    input_grad = summed_grad + contract_cols(joined_grad, qkv_full)
    tiles = width // SB
    qkv_term = jnp.einsum(
        "tri,tcj->rcij",
        tokens.reshape(row_count, tiles, SB),
        joined_grad.reshape(row_count, 3 * tiles, SB),
        preferred_element_type=jnp.float32,
    )
    out_term = jnp.einsum(
        "tri,tcj->rcij",
        gated_low.reshape(row_count, tiles, SB),
        out_back.reshape(row_count, tiles, SB),
        preferred_element_type=jnp.float32,
    )
    attn_terms = jnp.concatenate(
        [
            qkv_term.reshape(-1, model_size, part_rows, SB),
            out_term.reshape(-1, model_size, part_rows, SB),
        ],
        axis=0,
    )
    attn_rows = (
        lax.psum_scatter(attn_terms.astype(jnp.bfloat16), "mp", scatter_dimension=1, tiled=True)
        .astype(jnp.float32)
        .reshape(-1, part_rows, SB)
    )
    unit_split = unit_local.reshape(2, tiles, model_size, part_rows, share)
    unit_rows = lax.all_to_all(
        unit_split.astype(jnp.bfloat16), "mp", split_axis=2, concat_axis=4, tiled=True
    ).astype(unit_split.dtype)
    unit_rows = (
        unit_rows.reshape(2, tiles, part_rows, FF // SB, SB)
        .transpose(0, 1, 3, 2, 4)
        .reshape(-1, part_rows, SB)
    )
    all_rows = jnp.concatenate([attn_rows, unit_rows], axis=0)
    slot_count = owner_slot.shape[0]
    pick = (owner_slot[None, :] == jnp.arange(slot_count)[:, None]).astype(jnp.bfloat16)
    flat_rows = all_rows.astype(jnp.bfloat16).reshape(slot_count, -1)
    slotted = jnp.dot(pick, flat_rows, preferred_element_type=jnp.float32).reshape(all_rows.shape)
    owned = lax.psum_scatter(
        slotted.astype(jnp.bfloat16), "dp", scatter_dimension=0, tiled=True
    ).astype(jnp.float32)
    full_grad = lax.all_gather(owned.astype(jnp.bfloat16), "mp", axis=1, tiled=True).astype(
        owned.dtype
    )
    row_start = lax.axis_index("mp") * part_rows
    columns = lax.dynamic_slice_in_dim(full_grad, row_start, part_rows, 2)
    left_new = BETA * left_stats + (1.0 - BETA) * jnp.einsum(
        "srj,skj->srk", owned, full_grad, precision=HIGH
    )
    right_new = BETA * right_stats + (1.0 - BETA) * jnp.einsum(
        "sjr,sjk->srk", columns, full_grad, precision=HIGH
    )
    left_part = jnp.einsum("sri,sij->srj", left_root, full_grad, precision=HIGH)
    update = jnp.einsum("srj,sjk->srk", left_part, right_root, precision=HIGH)
    weight_new = master - RATE * update
    norm_grad = jnp.stack([gain_grad, bias_grad])
    norm_grad, mask_grad, head_grad, layer_grad, unit_grad = lax.psum(
        (norm_grad, mask_grad, head_grad, layer_grad, unit_grad), ("dp", "mp")
    )
    norm_new = jnp.stack([norm_gain, norm_bias]) - 0.2 / math.sqrt(total_tokens) * norm_grad
    return (
        output,
        input_grad,
        head_grad,
        unit_grad,
        mask_grad,
        layer_grad,
        norm_grad,
        norm_new,
        owned,
        left_new,
        right_new,
        weight_new,
        weight_new.astype(jnp.bfloat16),
    )


F32 = jnp.float32
BF = jnp.bfloat16
MESH = pl.DeviceIdType.MESH
LOG2E = 1.4426950408889634
ROWS = 1024
D = 768
HD = 64
BLK = 512
NT_DIMS = (((1,), (1,)), ((), ()))
NN_DIMS = (((1,), (0,)), ((), ()))


def nn(left, right):
    return lax.dot_general(left, right, NN_DIMS, preferred_element_type=F32)


def nt(left, right):
    return lax.dot_general(left, right, NT_DIMS, preferred_element_type=F32)


def coords():
    d = lax.axis_index("dp")
    m = lax.axis_index("mp")
    return d // 2, d % 2, m // 2, m % 2


def at(z, x, y, c):
    return (2 * z + x, 2 * y + c)


def gelu_parts(x):
    ax = jnp.abs(x)
    e = jnp.exp2(x * x * (-0.5 * LOG2E))
    t = 1.0 / (1.0 + (0.3275911 * math.sqrt(0.5)) * ax)
    poly = t * (
        0.5 * 0.254829592
        + t
        * (
            -0.5 * 0.284496736
            + t * (0.5 * 1.421413741 + t * (-0.5 * 1.453152027 + t * (0.5 * 1.061405429)))
        )
    )
    tail = poly * e
    cdf = jnp.where(x < 0, tail, 1.0 - tail)
    active = x * cdf
    return active, cdf + x * (e * (1.0 / math.sqrt(2.0 * math.pi)))


def colsum(v):
    return jnp.sum(v, axis=0, keepdims=True)


def row_norm(summed):
    centre = summed - jnp.mean(summed, axis=-1, keepdims=True)
    spread = jnp.mean(centre * centre, axis=-1, keepdims=True)
    inv = lax.rsqrt(spread + EPS)
    return centre * inv, inv


def one_row(v):
    return jnp.concatenate([v[i : i + 1] for i in range(v.shape[0])], axis=1)


def many_rows(v):
    return jnp.concatenate([v[:, 128 * i : 128 * i + 128] for i in range(v.shape[1] // 128)], axis=0)


def head_lanes(heads):
    which = lax.broadcasted_iota(jnp.int32, (1, D), 1) // HD
    row = jnp.zeros((1, D), F32)
    for h in range(12):
        row = row + jnp.where(which == h, heads[h].astype(F32), 0.0)
    return row


HALF = BLK // 2


def first_rows(segs):
    values = segs[...].astype(F32)
    begin = jnp.zeros((2, 1), F32)
    for item in range(6):
        count = jnp.sum(jnp.where(values == item, 1.0, 0.0), axis=1, keepdims=True)
        before = jnp.sum(jnp.where(values < item, 1.0, 0.0), axis=1, keepdims=True)
        begin = begin + jnp.where(count == HALF, before, 0.0)
    return begin


def turning(begin, sign):
    row = lax.broadcasted_iota(jnp.int32, (BLK, BLK), 0).astype(F32)
    col = lax.broadcasted_iota(jnp.int32, (BLK, BLK), 1).astype(F32)
    off = sign * (col - row) - begin
    return jnp.where((off == 0) | (off == -BLK), 1.0, 0.0)


def turn_labels(segs, begin, segcol, segrow):
    for b in range(2):
        hot = turning(begin[b : b + 1], 1)[HALF:, :]
        column = jnp.sum(hot * segs[b : b + 1, :].astype(F32), axis=1, keepdims=True)
        segcol[b] = column
        segrow[b] = jnp.broadcast_to(column, (HALF, 128)).T[0:1, :]


MOVED = (8, 8, 4)
LEFT = 8 - MOVED[2]
NPIECE = 8


def forward_kernel(
    gates,
    heads,
    tokens_in,
    cot_in,
    segs,
    units,
    hidden,
    gain_in,
    bias_in,
    qkv_in,
    out_in,
    up_in,
    down_in,
    o_out,
    o_joined,
    o_ctx,
    o_ctxT,
    o_tokT,
    o_sgrad,
    o_sums,
    o_far,
    o_wq,
    o_wo,
    lse,
    small,
    wq,
    wo,
    wu,
    wd,
    joined,
    ctx,
    ctxT,
    tokT,
    attn,
    blow,
    bT,
    branch,
    hback,
    grads,
    got1,
    got2,
    tokens,
    cot,
    segcol,
    segrow,
    ugate,
    vec,
    send_sem,
    recv_sem,
    loc_sem,
    out_sem,
    c_send,
    c_recv,
    x_send,
    x_recv,
):
    z, x, y, c = coords()
    hT = tokT
    hlow = ctx
    act, inner, outv = (joined.at[:, pl.ds(D * i, D)] for i in range(3))
    m = 2 * y + c
    ms = 2 * y + 1 - c
    my = 2 * (1 - y) + c
    mys = 2 * (1 - y) + 1 - c
    sib = at(z, x, y, 1 - c)
    ypeer = at(z, x, 1 - y, c)
    xpeer = at(z, 1 - x, y, c)
    zpeer = at(z + 1 - 2 * (z % 2), x, y, c)
    g0 = gates[0]
    g1 = gates[1]

    barrier = pltpu.get_barrier_semaphore()
    for peer in (sib, ypeer, xpeer, zpeer):
        pl.semaphore_signal(barrier, inc=1, device_id=peer, device_id_type=MESH)
    pl.semaphore_wait(barrier, 4)

    def spot(j):
        if j < 3:
            return 0, 192, pl.ds(768 * j, 768)
        if j == 3:
            return 1, 192, slice(None)
        return 2 + (j - 4) // 2, 768, pl.ds(384 * (j % 2), 384)

    def full(j, i, h=None):
        which, n, cols = spot(j)
        ref = (wq, wo, wu, wd)[which]
        if h is None:
            return ref.at[i, :, cols]
        return ref.at[i, pl.ds(pl.multiple_of(h * (n // 2), 16), n // 2), cols]

    def own(j, h=None):
        which, n, cols = spot(j)
        ref = (qkv_in, out_in, up_in, down_in)[which]
        if h is None:
            return ref.at[:, cols]
        return ref.at[pl.ds(pl.multiple_of(h * (n // 2), 16), n // 2), cols]

    def remote(src, dst, j, k, dev):
        return pltpu.make_async_remote_copy(
            src_ref=src,
            dst_ref=dst,
            send_sem=send_sem.at[j, k],
            recv_sem=recv_sem.at[j, k],
            device_id=dev,
            device_id_type=MESH,
        )

    def s1(j):
        return remote(own(j), full(j, m), j, 0, sib)

    def half_of(j):
        return (x, xpeer) if j < 4 else (z % 2, zpeer)

    def s2(j):
        h, _ = half_of(j)
        return remote(own(j, h), full(j, m, h), j, 1, ypeer)

    def s3(j):
        h, peer = half_of(j)
        return remote(full(j, my, h), full(j, my, h), j, 2, peer)

    def s4(j):
        h, _ = half_of(j)
        return remote(full(j, my, h), full(j, my, h), j, 3, sib)

    def s5(j):
        h, _ = half_of(j)
        return remote(full(j, my, 1 - h), full(j, my, 1 - h), j, 4, sib)

    def local(j):
        return pltpu.make_async_copy(own(j), full(j, m), loc_sem.at[j])

    def first(j):
        s2(j).start()
        s1(j).start()
        local(j).start()

    def second(j):
        s2(j).wait_recv()
        s3(j).start()
        s4(j).start()

    def third(j):
        s3(j).wait_recv()
        s5(j).start()

    def finish_near(j):
        local(j).wait()
        s1(j).wait_recv()

    def finish_far(j):
        s4(j).wait_recv()
        s5(j).wait_recv()

    def finish_sends(j):
        for s in (s1, s2, s3, s4, s5):
            s(j).wait_send()

    loads = (
        pltpu.make_async_copy(tokens_in, blow, out_sem.at[6]),
        pltpu.make_async_copy(cot_in, ctx, out_sem.at[7]),
    )
    for j in range(3):
        first(j)
    for copy in loads:
        copy.start()

    begin = first_rows(segs)
    turn_labels(segs, begin, segcol, segrow)
    for copy in loads:
        copy.wait()
    def turn(src, dst):
        for b in range(2):
            hot = turning(begin[b : b + 1], 1).astype(BF)
            rows = slice(b * BLK, b * BLK + BLK)
            dst[rows, :] = nn(hot, src[rows, :]).astype(BF)

    def backs(lo, hi):
        @pl.loop(lo, hi)
        def _(r):
            rows = pl.ds(pl.multiple_of(r * 256, 256), 256)
            low = (g1 * cot[rows, :].astype(F32)).astype(BF)
            blow[rows, :] = low
            bT[:, rows] = low.T

    turn(blow, tokens)

    near_sum = (attn, branch, hback)

    def project(j, near):
        yy = y if near else 1 - y

        @pl.loop(0, 2)
        def _(r):
            rows = pl.ds(pl.multiple_of(r * 512, 512), 512)
            w = wq[pl.ds(2 * yy, 2), :, pl.ds(768 * j, 768)].reshape(SB, D)
            one = nn(tokens[rows, pl.ds(pl.multiple_of(SB * yy, 128), SB)], w)
            if near:
                near_sum[j][rows, :] = one
            else:
                joined[rows, pl.ds(768 * j, 768)] = (near_sum[j][rows, :] + one).astype(BF)

    for j in range(3):
        finish_near(j)
    project(0, True)
    second(0)
    turn(ctx, cot)
    for i in range(4):
        ugate[i] = one_row(units[6 * i : 6 * i + 6, :].astype(F32))
    vec[0:1, :] = head_lanes(heads)
    vec[1:2, :] = one_row(hidden[...].astype(F32))
    vec[2:3, :] = one_row(gain_in[...])
    vec[3:4, :] = one_row(bias_in[...])
    hgate, mgate, gain, bias = (vec.at[i : i + 1] for i in range(4))
    project(1, True)
    second(1)
    project(2, True)
    third(0)
    backs(0, 2)
    second(2)
    for j in range(3, NPIECE):
        first(j)
    tokT[...] = tokens[...].T
    tok_copy = pltpu.make_async_copy(tokT, o_tokT, out_sem.at[0])
    tok_copy.start()
    third(1)
    backs(2, 4)
    finish_far(0)
    project(0, False)
    third(2)
    finish_far(1)
    project(1, False)
    finish_far(2)
    wq_copy = pltpu.make_async_copy(wq, o_wq, out_sem.at[1])
    wq_copy.start()
    project(2, False)
    joined_copy = pltpu.make_async_copy(joined, o_joined, out_sem.at[2])
    joined_copy.start()

    scale = LOG2E / math.sqrt(HD)
    half_iota = lax.broadcasted_iota(jnp.int32, (1, 128), 1) // HD
    halves = [(half_iota == e).astype(F32).astype(BF) for e in range(2)]

    def attend(i):
        b = i // 6
        p = i % 6
        lane = pl.multiple_of(p * 128, 128)
        for part in range(2):
            rows = pl.ds(pl.multiple_of(b * BLK + part * HALF, HALF), HALF)
            q = joined[rows, pl.ds(lane, 128)]
            k = joined[rows, pl.ds(D + lane, 128)]
            v = joined[rows, pl.ds(2 * D + lane, 128)]
            total = None
            for e in range(2):
                s = nt(k * halves[e], q) * scale
                if part:
                    s = jnp.where(segcol[b] == segrow[b], s, MASKED)
                top = jnp.max(s, axis=0, keepdims=True)
                pr = jnp.exp2(s - top)
                tot = jnp.sum(pr, axis=0, keepdims=True)
                low = (pr * (1.0 / tot)).astype(BF)
                lse[2 * i + e, :, part * HALF : part * HALF + HALF] = top + jnp.log(tot) * LOG2E
                one = nn((v * halves[e]).T, low)
                total = one if total is None else total + one
            ctxT[pl.ds(lane, 128), rows] = total.astype(BF)
            ctx[rows, pl.ds(lane, 128)] = total.T.astype(BF)

    plan = {
        0: [lambda: second(3)],
        5: [lambda: second(4), lambda: third(3)],
    }

    @pl.loop(0, 12)
    def _(i):
        attend(i)
        for at_step, todo in plan.items():

            @pl.when(i == at_step)
            def _(todo=todo):
                for f in todo:
                    f()

    ctx_copy = pltpu.make_async_copy(ctx, o_ctx, out_sem.at[3])
    ctx_copy.start()
    ctxT_copy = pltpu.make_async_copy(ctxT, o_ctxT, out_sem.at[4])
    ctxT_copy.start()
    finish_near(3)
    finish_far(3)
    wo_copy = pltpu.make_async_copy(wo, o_wo, out_sem.at[5])
    wo_copy.start()

    joined_copy.wait()
    tok_copy.wait()
    ctx_copy.wait()

    @pl.loop(0, 4)
    def _(r):
        rows = pl.ds(pl.multiple_of(r * 256, 256), 256)
        gated = ctx[rows, :] * hgate[...].astype(BF)
        a = nn(gated, wo[...].reshape(D, D))
        attn[rows, :] = a
        normed, _ = row_norm(tokens[rows, :].astype(F32) + g0 * a)
        low = ((normed * gain[...] + bias[...]) * mgate[...]).astype(BF)
        hlow[rows, :] = low
        hT[:, rows] = low.T

    second(5)

    small[...] = jnp.zeros_like(small)

    def feed(f, between={}):
        u = 2 * ((y + f // 2) % 2) + f % 2
        begin = f == 0
        w_up = wu.at[u]
        w_down = wd.at[u]

        @pl.loop(0, 2)
        def _(r):
            rows = pl.ds(pl.multiple_of(r * 512, 512), 512)
            pre = nn(hlow[rows, :], w_up[...])
            back = nn(blow[rows, :], w_down[...])
            active, slope = gelu_parts(pre)
            gate = ugate[u]
            small[pl.ds(u, 1), :] += colsum(back * active)
            a_low = (active * gate).astype(BF)
            i_low = (back * gate * slope).astype(BF)
            act[rows, :] = a_low
            inner[rows, :] = i_low
            up_part = nt(a_low, w_down[...])
            back_part = nt(i_low, w_up[...])
            if begin:
                branch[rows, :] = up_part
                hback[rows, :] = back_part
            else:
                branch[rows, :] += up_part
                hback[rows, :] += back_part
            for at_row, todo in between.items():
                pl.when(r == at_row)(todo)

        for which, (left, right) in enumerate(((hT, inner), (bT, act))):

            @pl.loop(0, 2)
            def _(r, which=which, left=left, right=right):
                rr = pl.ds(pl.multiple_of(r * SB, 128), SB)
                g = nn(left[rr, :], right[...]).astype(BF)
                for j in range(2):
                    grads[f, 4 * which + 2 * r + j] = g[:, SB * j : SB * j + SB].reshape(
                        2, 2, 2, 48, SB
                    )

    def swap1(f):
        return pltpu.make_async_remote_copy(
            src_ref=grads.at[f, :, 1 - c],
            dst_ref=got1.at[f],
            send_sem=c_send.at[f],
            recv_sem=c_recv.at[f],
            device_id=sib,
            device_id_type=MESH,
        )

    def swap2(f):
        return pltpu.make_async_remote_copy(
            src_ref=grads.at[f, pl.ds(0, MOVED[f]), c, :, 1 - x],
            dst_ref=got2.at[f, pl.ds(0, MOVED[f])],
            send_sem=x_send.at[f],
            recv_sem=x_recv.at[f],
            device_id=xpeer,
            device_id_type=MESH,
        )

    def plus(left, right):
        return (left.astype(F32) + right.astype(F32)).astype(BF)

    def sum1(f):
        swap1(f).wait_recv()

        @pl.loop(0, 8)
        def _(i):
            grads[f, i, c] = plus(grads[f, i, c], got1[f, i])

    for j in range(4, NPIECE):
        finish_near(j)

    def spread(f):
        sum1(f)
        swap2(f).start()

    def rest(j, i):
        second(j)
        third(i)

    feed(0, {0: lambda: rest(6, 4)})
    swap1(0).start()
    rest(7, 5)

    def near_first():
        third(6)
        spread(0)

    feed(1, {0: near_first, 1: lambda: third(7)})
    swap1(1).start()
    for j in range(4, NPIECE):
        finish_far(j)
    feed(2, {0: lambda: spread(1)})
    swap1(2).start()
    feed(3, {0: lambda: spread(2)})
    swap1(3).start()

    lane = lax.broadcasted_iota(jnp.int32, (1, D), 1)

    @pl.loop(0, 4)
    def _(r):
        rows = pl.ds(pl.multiple_of(r * 256, 256), 256)
        a = attn[rows, :]
        normed, inv = row_norm(tokens[rows, :].astype(F32) + g0 * a)
        plain = normed * gain[...] + bias[...]
        back = cot[rows, :].astype(F32)
        br = branch[rows, :]
        outv[rows, :] = (plain * mgate[...] + g1 * br).astype(BF)
        total = back + hback[rows, :]
        masked = total * mgate[...]
        small[4:5, :] += colsum(masked * normed)
        small[5:6, :] += colsum(masked)
        small[6:7, :] += colsum(total * plain)
        n = masked * gain[...]
        grad = (
            n
            - jnp.mean(n, axis=-1, keepdims=True)
            - normed * jnp.mean(n * normed, axis=-1, keepdims=True)
        ) * inv
        hback[rows, :] = grad
        small[7:8, :] += colsum(grad * a)
        small[8:9, :] += colsum(back * br)

    out_copy = pltpu.make_async_copy(outv, o_out, out_sem.at[6])
    out_copy.start()
    sgrad_copy = pltpu.make_async_copy(hback, o_sgrad, out_sem.at[7])
    sgrad_copy.start()
    sum1(3)
    grad_copies = [
        pltpu.make_async_copy(
            grads.at[2, pl.ds(MOVED[2], LEFT), c], o_far.at[pl.ds(0, LEFT)], out_sem.at[8]
        ),
        pltpu.make_async_copy(grads.at[3, :, c], o_far.at[pl.ds(LEFT, 8)], out_sem.at[12]),
    ]
    for copy in grad_copies:
        copy.start()
    for f in range(3):
        swap2(f).wait_recv()

        @pl.loop(0, MOVED[f])
        def _(i, f=f):
            for yy in range(2):
                grads[f, i, c, yy, x] = plus(grads[f, i, c, yy, x], got2[f, i, yy])

        copy = pltpu.make_async_copy(
            grads.at[f, pl.ds(0, MOVED[f]), c, :, x],
            o_sums.at[f, pl.ds(0, MOVED[f])],
            out_sem.at[9 + f],
        )
        copy.start()
        grad_copies.append(copy)
    for copy in grad_copies:
        copy.wait()
    for copy in (wq_copy, ctxT_copy, wo_copy, out_copy, sgrad_copy):
        copy.wait()
    for f in range(4):
        swap1(f).wait_send()
    for f in range(3):
        swap2(f).wait_send()
    for j in range(NPIECE):
        finish_sends(j)


def run_forward(*arrays):
    sds = jax.ShapeDtypeStruct
    outs = (
        sds((ROWS, D), BF),
        sds((ROWS, 3 * D), BF),
        sds((ROWS, D), BF),
        sds((D, ROWS), BF),
        sds((D, ROWS), BF),
        sds((ROWS, D), F32),
        sds((3, 8, 2, 48, SB), BF),
        sds((LEFT + 8, 2, 2, 48, SB), BF),
        sds((4, 192, 3 * D), BF),
        sds((4, 192, D), BF),
        sds((24, 1, BLK), F32),
        sds((16, D), F32),
    )
    any_ = pl.BlockSpec(memory_space=pl.ANY)
    vm = pl.BlockSpec(memory_space=pltpu.VMEM)
    sm = pl.BlockSpec(memory_space=pltpu.SMEM)
    return pl.pallas_call(
        forward_kernel,
        out_shape=outs,
        in_specs=[sm] * 2 + [any_] * 2 + [vm] * 5 + [any_] * 4,
        out_specs=[any_] * 10 + [vm] * 2,
        scratch_shapes=[
            pltpu.VMEM((4, 192, 3 * D), BF),
            pltpu.VMEM((4, 192, D), BF),
            pltpu.VMEM((4, D, D), BF),
            pltpu.VMEM((4, D, D), BF),
            pltpu.VMEM((ROWS, 3 * D), BF),
            pltpu.VMEM((ROWS, D), BF),
            pltpu.VMEM((D, ROWS), BF),
            pltpu.VMEM((D, ROWS), BF),
            pltpu.VMEM((ROWS, D), F32),
            pltpu.VMEM((ROWS, D), BF),
            pltpu.VMEM((D, ROWS), BF),
            pltpu.VMEM((ROWS, D), F32),
            pltpu.VMEM((ROWS, D), F32),
            pltpu.VMEM((4, 8, 2, 2, 2, 48, SB), BF),
            pltpu.VMEM((4, 8, 2, 2, 48, SB), BF),
            pltpu.VMEM((3, 8, 2, 48, SB), BF),
            pltpu.VMEM((ROWS, D), BF),
            pltpu.VMEM((ROWS, D), BF),
            pltpu.VMEM((2, HALF, 1), F32),
            pltpu.VMEM((2, 1, HALF), F32),
            pltpu.VMEM((4, 1, D), F32),
            pltpu.VMEM((8, D), F32),
            pltpu.SemaphoreType.DMA((NPIECE, 5)),
            pltpu.SemaphoreType.DMA((NPIECE, 5)),
            pltpu.SemaphoreType.DMA((NPIECE,)),
            pltpu.SemaphoreType.DMA((13,)),
            pltpu.SemaphoreType.DMA((4,)),
            pltpu.SemaphoreType.DMA((4,)),
            pltpu.SemaphoreType.DMA((3,)),
            pltpu.SemaphoreType.DMA((3,)),
        ],
        compiler_params=pltpu.CompilerParams(
            collective_id=1, has_side_effects=True, vmem_limit_bytes=64 << 20
        ),
    )(*arrays)


SENT = (12, 13, 14, 15, 0, 2, 4, 6, 8, 10, 1, 3, 5, 7, 9, 11)
GROUPS = (None,) * 4 + ((32, 4, 0), (36, 6, 0), (42, 6, 3))
FF_BLOCKS = 32
PARTS = 3
PER = 6 // PARTS


def backward_kernel(
    gates,
    heads,
    order,
    small_in,
    segs,
    lse,
    sums_in,
    far_in,
    joined_in,
    ctx_in,
    ctxT_in,
    tokT_in,
    sgrad_in,
    wq_in,
    wo_in,
    out_in,
    o_out,
    o_igrad,
    o_full,
    small_out,
    joined,
    ctx,
    ctxT,
    tokT,
    sgrad,
    wq,
    wo,
    outb,
    cgrad,
    igrad,
    ownv,
    farv,
    gotx,
    goty,
    ga,
    got1,
    got2,
    got3,
    part,
    gotz,
    total,
    slots,
    gz,
    gfull,
    sm_all,
    sm_rows,
    sm_lanes,
    sm_z,
    sm_back,
    sm_got1,
    sm_got2,
    sm_got3,
    segcol,
    segrow,
    hrow,
    hcol,
    load_sem,
    half_sem,
    ff_send,
    ff_recv,
    send_sem,
    recv_sem,
    z_send,
    z_recv,
    a_send,
    a_recv,
    f_send,
    f_recv,
    s_send,
    s_recv,
    out_sem,
):
    z, x, y, c = coords()
    g0 = gates[0]
    sib = at(z, x, y, 1 - c)
    ypeer = at(z, x, 1 - y, c)
    xpeer = at(z, 1 - x, y, c)
    diag = at(z, 1 - x, 1 - y, c)
    zpeers = [at((z + k) % 4, x, y, c) for k in (1, 2, 3)]

    loads = [
        pltpu.make_async_copy(src, dst, load_sem.at[i])
        for i, (src, dst) in enumerate(
            (
                (sgrad_in, sgrad),
                (wo_in, wo),
                (ctx_in, ctx),
                (ctxT_in, ctxT),
                (joined_in, joined),
                (tokT_in, tokT),
                (wq_in, wq),
                (out_in, ctx),
            )
        )
    ]
    halves_in = [
        pltpu.make_async_copy(sums_in.at[pl.ds(0, 2), :, y], ownv.at[pl.ds(0, 2)], half_sem.at[0]),
        pltpu.make_async_copy(far_in.at[:, :, x], farv, half_sem.at[1]),
        pltpu.make_async_copy(
            sums_in.at[2, pl.ds(0, MOVED[2]), y], ownv.at[2, pl.ds(0, MOVED[2])], half_sem.at[2]
        ),
    ]
    for copy in loads[:4]:
        copy.start()

    barrier = pltpu.get_barrier_semaphore()
    for peer in [sib, ypeer, xpeer, diag] + zpeers:
        pl.semaphore_signal(barrier, inc=1, device_id=peer, device_id_type=MESH)
    pl.semaphore_wait(barrier, 7)

    def remote(src, dst, sems, dev):
        return pltpu.make_async_remote_copy(
            src_ref=src,
            dst_ref=dst,
            send_sem=sems[0],
            recv_sem=sems[1],
            device_id=dev,
            device_id_type=MESH,
        )

    def pair(g, k):
        return send_sem.at[g, k], recv_sem.at[g, k]

    def first_block(f):
        return 8 * (2 * ((y + f // 2) % 2) + f % 2)

    def span(g):
        return (first_block(g), 8) if g < 4 else GROUPS[g][:2]

    def over_y(i):
        src, to = (
            (lambda: sums_in.at[0, :, 1 - y], goty.at[2]),
            (lambda: sums_in.at[1, :, 1 - y], goty.at[3]),
            (lambda: sums_in.at[2, pl.ds(0, MOVED[2]), 1 - y], goty.at[0, pl.ds(0, MOVED[2])]),
            (lambda: farv.at[pl.ds(0, LEFT), 1 - y], goty.at[0, pl.ds(MOVED[2], LEFT)]),
            (lambda: farv.at[pl.ds(LEFT, 8), 1 - y], goty.at[1]),
        )[i]
        return remote(src(), to, (ff_send.at[i], ff_recv.at[i]), ypeer)

    def over_x(i):
        part = (pl.ds(0, LEFT), pl.ds(LEFT, 8))[i]
        return remote(
            far_in.at[part, :, 1 - x], gotx.at[part], (ff_send.at[5 + i], ff_recv.at[5 + i]), xpeer
        )

    def mine(g, first, count):
        return ga.at[pl.ds(GROUPS[g][0] + first - FF_BLOCKS, count), c]

    def swap1(g):
        base, count, _ = GROUPS[g]
        src = ga.at[pl.ds(base - FF_BLOCKS, count), 1 - c]
        return remote(src, got1.at[pl.ds(base - FF_BLOCKS, count)], pair(g, 0), sib)

    def swap2(g):
        base, count, n = GROUPS[g]
        rest = count - n
        to = base - FF_BLOCKS
        found = [
            remote(mine(g, n, rest).at[:, :, 1 - x], got2.at[pl.ds(to + n, rest)], pair(g, 2), xpeer)
        ]
        if n:
            found.append(remote(mine(g, 0, n).at[:, 1 - y], got2.at[pl.ds(to, n)], pair(g, 1), ypeer))
        return found

    def swap3(g):
        base, count, n = GROUPS[g]
        rest = count - n
        to = base - FF_BLOCKS
        found = [
            remote(mine(g, n, rest).at[:, 1 - y, x], got3.at[pl.ds(to + n, rest)], pair(g, 4), ypeer)
        ]
        if n:
            found.append(remote(mine(g, 0, n).at[:, y, 1 - x], got3.at[pl.ds(to, n)], pair(g, 3), xpeer))
        return found

    def plus(left, right):
        return (left.astype(F32) + right.astype(F32)).astype(BF)

    def step1(g):
        base, count, _ = GROUPS[g]
        swap1(g).wait_recv()

        @pl.loop(base - FF_BLOCKS, base - FF_BLOCKS + count)
        def _(i):
            ga[i, c] = plus(ga[i, c], got1[i])

        for copy in swap2(g):
            copy.start()

    def step2(g):
        base, count, n = GROUPS[g]
        for copy in swap2(g):
            copy.wait_recv()

        @pl.loop(base - FF_BLOCKS, base - FF_BLOCKS + n)
        def _(i):
            ga[i, c, y] = plus(ga[i, c, y], got2[i])

        @pl.loop(base - FF_BLOCKS + n, base - FF_BLOCKS + count)
        def _(i):
            for yy in range(2):
                ga[i, c, yy, x] = plus(ga[i, c, yy, x], got2[i, yy])

        for copy in swap3(g):
            copy.start()

    def feed_far(n):
        over_x(n).wait_recv()

        @pl.loop(*((0, LEFT), (LEFT, LEFT + 8))[n])
        def _(i):
            farv[i] = plus(farv[i], gotx[i])

        over_y(3 + n).start()

    spare = 1 + c

    def unit(zz):
        return zz - (zz + 3 - spare) // 4

    def swapz(g, k):
        base, count = span(g)
        return remote(
            part.at[pl.ds(base, count), unit((z + k) % 4)],
            gotz.at[k - 1, pl.ds(base, count)],
            (z_send.at[g, k - 1], z_recv.at[g, k - 1]),
            zpeers[k - 1],
        )

    def step3(g):
        base, count = span(g)
        if g < 4:
            for i in ((2, 3), (4,), (0,), (1,))[g]:
                over_y(i).wait_recv()
        else:
            for copy in swap3(g):
                copy.wait_recv()
        moved = (8, 8, MOVED[2], 0)[g] if g < 4 else 0

        if moved:

            @pl.loop(0, moved)
            def _(i):
                part[base + i] = plus(ownv[g, i], goty[g, i]).reshape(3, 16, SB)

        @pl.loop(moved, count)
        def _(i):
            if g < 4:
                value = plus(farv[i - (8 - LEFT) if g == 2 else LEFT + i, y], goty[g, i])
            else:
                value = plus(ga[base - FF_BLOCKS + i, c, y, x], got3[base - FF_BLOCKS + i])
            part[base + i] = value.reshape(3, 16, SB)

        for k in (1, 2, 3):

            @pl.when((z + k) % 4 != spare)
            def _(k=k):
                swapz(g, k).start()

    def step4(g):
        base, count = span(g)

        @pl.when(z != spare)
        def _():
            for k in (1, 2, 3):
                swapz(g, k).wait_recv()

            @pl.loop(0, count)
            def _(i):
                value = part[base + i, unit(z)].astype(F32)
                for k in range(3):
                    value = value + gotz[k, base + i].astype(F32)
                total[base + i] = value.astype(BF)

    def small_copy(k):
        rows = pl.ds(pl.multiple_of(8 * c, 8), 8)
        away = pl.ds(pl.multiple_of(8 * (1 - c), 8), 8)
        lanes = pl.ds(pl.multiple_of(SB * y, 128), SB)
        other = pl.ds(pl.multiple_of(SB * (1 - y), 128), SB)
        src, dst, dev = (
            (sm_all.at[away], sm_got1, sib),
            (sm_rows.at[:, other], sm_got2, ypeer),
            (sm_lanes, sm_got3, xpeer),
            (sm_z.at[z], sm_z.at[z], zpeers[0]),
            (sm_z.at[z], sm_z.at[z], zpeers[1]),
            (sm_z.at[z], sm_z.at[z], zpeers[2]),
            (sm_back.at[rows, lanes], sm_back.at[rows, lanes], ypeer),
            (sm_back.at[rows], sm_back.at[rows], sib),
        )[k]
        return remote(src, dst, (s_send.at[k], s_recv.at[k]), dev)

    def small_take(stage):
        rows = pl.ds(pl.multiple_of(8 * c, 8), 8)
        away = pl.ds(pl.multiple_of(8 * (1 - c), 8), 8)
        lanes = pl.ds(pl.multiple_of(SB * y, 128), SB)
        other = pl.ds(pl.multiple_of(SB * (1 - y), 128), SB)
        if stage == 0:
            small_copy(0).wait_recv()
            sm_rows[...] = sm_all[rows, :] + sm_got1[...]
            small_copy(1).start()
        elif stage == 1:
            small_copy(1).wait_recv()
            sm_lanes[...] = sm_rows[:, lanes] + sm_got2[...]
            small_copy(2).start()
        elif stage == 2:
            small_copy(2).wait_recv()
            sm_z[z] = sm_lanes[...] + sm_got3[...]
            for k in (3, 4, 5):
                small_copy(k).start()
        elif stage == 3:
            for k in (1, 2, 3):
                sender = (z + 4 - k) % 4
                remote(
                    sm_z.at[sender], sm_z.at[sender], (s_send.at[2 + k], s_recv.at[2 + k]), zpeers[k - 1]
                ).wait_recv()
            sm_back[rows, lanes] = sm_z[0] + sm_z[1] + sm_z[2] + sm_z[3]
            small_copy(6).start()
        elif stage == 4:
            remote(
                sm_back.at[rows, other], sm_back.at[rows, other], (s_send.at[6], s_recv.at[6]), ypeer
            ).wait_recv()
            small_copy(7).start()
        else:
            remote(sm_back.at[away], sm_back.at[away], (s_send.at[7], s_recv.at[7]), sib).wait_recv()
            small_out[...] = sm_back[...]

    for n in range(2):
        over_x(n).start()
    for i in range(3):
        over_y(i).start()
    for copy in [loads[4]] + halves_in + loads[5:7]:
        copy.start()

    begin = first_rows(segs)
    turn_labels(segs, begin, segcol, segrow)
    hrow[...] = head_lanes(heads)
    hcol[...] = jnp.broadcast_to(hrow[...], (8, D)).T[:, 0:1]
    hgate = hrow
    sm_all[...] = small_in[...]
    loads[0].wait()
    loads[1].wait()
    loads[2].wait()

    @pl.loop(0, 4)
    def _(r):
        rows = pl.ds(pl.multiple_of(r * 256, 256), 256)
        low = (g0 * sgrad[rows, :]).astype(BF)
        outb[rows, :] = low
        grad = nt(low, wo[...].reshape(D, D)).astype(BF)
        sm_all[9:10, :] += colsum(ctx[rows, :].astype(F32) * grad.astype(F32))
        cgrad[rows, :] = grad * hgate[...].astype(BF)

    small_copy(0).start()
    loads[7].start()
    loads[3].wait()

    def weight_tiles(left, right, lane, rowgate, places):
        @pl.loop(0, 2)
        def _(r):
            rr = pl.ds(pl.multiple_of(r * SB, 128), SB)
            g = nn(left[rr, :], right[:, pl.ds(lane, SB)])
            if rowgate is not None:
                g = g * rowgate[rr, :]
            ga[places[0] + r * (places[1] - places[0])] = g.astype(BF).reshape(2, 2, 2, 48, SB)

    for j in range(2):
        weight_tiles(ctxT, outb, SB * j, hcol, (SENT.index(12 + j), SENT.index(14 + j)))

    swap1(4).start()
    loads[4].wait()

    scale = LOG2E / math.sqrt(HD)
    factor = 1.0 / math.sqrt(HD)
    half_iota = lax.broadcasted_iota(jnp.int32, (1, 128), 1) // HD
    halves = [(half_iota == e).astype(F32).astype(BF) for e in range(2)]

    def attend_back(i):
        p = i // 2
        b = i % 2
        lane = pl.multiple_of(p * 128, 128)
        for part in range(2):
            rows = pl.ds(pl.multiple_of(b * BLK + part * HALF, HALF), HALF)
            q = joined[rows, pl.ds(lane, 128)]
            k = joined[rows, pl.ds(D + lane, 128)]
            v = joined[rows, pl.ds(2 * D + lane, 128)]
            do = cgrad[rows, pl.ds(lane, 128)]
            parts = []
            for e in range(2):
                ke = k * halves[e]
                s = nt(ke, q) * scale
                if part:
                    s = jnp.where(segcol[b] == segrow[b], s, MASKED)
                total = lse[2 * (b * 6 + p) + e, :, part * HALF : part * HALF + HALF]
                pr = jnp.exp2(s - total)
                dp = nt(v * halves[e], do)
                delta = jnp.sum(pr * dp, axis=0, keepdims=True)
                ds = (pr * (dp - delta)).astype(BF)
                parts.append(
                    (nn(ke.T, ds), nn(ds, q * halves[e]), nn(pr.astype(BF), do * halves[e]))
                )
            dqT, dk, dv = (one + two for one, two in zip(*parts))
            joined[rows, pl.ds(lane, 128)] = (dqT * factor).T.astype(BF)
            joined[rows, pl.ds(D + lane, 128)] = (dk * factor).astype(BF)
            joined[rows, pl.ds(2 * D + lane, 128)] = dv.astype(BF)

    def qkv_tiles(h):
        for j in (h, 2 + h, 4 + h):
            weight_tiles(tokT, joined, SB * j, None, (SENT.index(j), SENT.index(6 + j)))

    def middle():
        loads[5].wait()
        qkv_tiles(0)
        swap1(5).start()

    def first_sums():
        halves_in[0].wait()
        halves_in[2].wait()
        halves_in[1].wait()
        feed_far(0)
        step3(2)

    plan = {
        0: [lambda: small_take(0)],
        1: [lambda: step1(4), first_sums],
        5: [middle],
        6: [lambda: step1(5), lambda: small_take(1)],
        7: [lambda: feed_far(1), lambda: step3(3)],
        9: [lambda: step3(0)],
        11: [lambda: step2(4)],
    }

    @pl.loop(0, 12)
    def _(i):
        attend_back(i)
        for at_step, todo in plan.items():

            @pl.when(i == at_step)
            def _(todo=todo):
                for f in todo:
                    f()

    qkv_tiles(1)
    swap1(6).start()
    loads[6].wait()

    def input_rows(lo, hi):
        @pl.loop(lo, hi)
        def _(r):
            rows = pl.ds(pl.multiple_of(r * 256, 256), 256)
            igrad[rows, :] = sgrad[rows, :] + nt(joined[rows, :], wq[...].reshape(D, 3 * D))

    step3(1)
    step1(6)
    small_take(2)
    input_rows(0, 1)
    step4(2)
    step3(4)
    input_rows(1, 2)
    step2(5)
    step4(3)
    input_rows(2, 4)
    def turn_back():
        loads[7].wait()
        for b in range(2):
            hot = turning(begin[b : b + 1], -1).astype(BF)
            rows = slice(b * BLK, b * BLK + BLK)
            cgrad[rows, :] = nn(hot, ctx[rows, :]).astype(BF)
            for j in range(3):
                cols = slice(256 * j, 256 * j + 256)
                rest = igrad[rows, cols]
                value = None
                for _ in range(3):
                    high = rest.astype(BF)
                    rest = rest - high.astype(F32)
                    one = nn(hot, high)
                    value = one if value is None else value + one
                igrad[rows, cols] = value

    step2(6)
    step3(5)
    turn_back()
    igrad_copy = pltpu.make_async_copy(igrad, o_igrad, out_sem.at[0])
    igrad_copy.start()
    out_copy = pltpu.make_async_copy(cgrad, o_out, out_sem.at[1])
    out_copy.start()
    step4(0)
    step3(6)
    step4(1)
    step4(4)
    small_take(3)
    step4(5)
    step4(6)

    def deal(n, k, to, u):
        return remote(
            slots.at[to, :, n],
            gz.at[:, n, :, u],
            (a_send.at[n, k - 1], a_recv.at[n, k - 1]),
            zpeers[k - 1],
        )

    @pl.when(z != spare)
    def _():
        @pl.loop(0, 48)
        def _(s):
            slots[s // 12, s // 6 % 2, s // PER % PARTS, s % PER] = total[order[s]]

        for n in range(PARTS):
            for k in (1, 2, 3):
                deal(n, k, (z + k) % 4, unit(z)).start()
            gz[:, n, :, unit(z)] = slots[z, :, n]

    def piece(n, cc, yy, xx):
        return gfull.at[n, :, 4 * cc + 2 * yy + xx]

    others = ((y, 1 - x), (1 - y, x), (1 - y, 1 - x))

    def near(n, k):
        src = gz.at[1 - x if k in (0, 2) else x, n]
        sems = (f_send.at[n, k], f_recv.at[n, k])
        return remote(src, piece(n, c, y, x), sems, (xpeer, ypeer, diag, sib)[k])

    def onward(n, k):
        yy, xx = others[k]
        to = piece(n, c, yy, xx)
        return remote(to, to, (f_send.at[n, 4 + k], f_recv.at[n, 4 + k]), sib)

    def pass_on(n):
        for k in range(3):
            near(n, k).wait_recv()
            onward(n, k).start()

    for n in range(PARTS):
        for k in (1, 2, 3):
            sender = (z + 4 - k) % 4

            @pl.when(sender != spare)
            def _(n=n, k=k, sender=sender):
                deal(n, k, z, unit(sender)).wait_recv()

        for k in range(4):
            near(n, k).start()
        gfull[n, :, 4 * c + 2 * y + x] = gz[x, n]
        if n:
            pass_on(n - 1)
    small_take(4)
    pass_on(PARTS - 1)
    small_take(5)
    for n in range(PARTS):
        near(n, 3).wait_recv()
        for k in range(3):
            onward(n, k).wait_recv()
    full_copy = pltpu.make_async_copy(gfull, o_full, out_sem.at[2])
    full_copy.start()
    for n in range(PARTS):
        for k in range(4):
            near(n, k).wait_send()
        for k in range(3):
            onward(n, k).wait_send()

        @pl.when(z != spare)
        def _(n=n):
            for k in (1, 2, 3):
                deal(n, k, (z + k) % 4, unit(z)).wait_send()

    for g in range(len(GROUPS)):
        for k in (1, 2, 3):

            @pl.when((z + k) % 4 != spare)
            def _(g=g, k=k):
                swapz(g, k).wait_send()

    for k in range(8):
        small_copy(k).wait_send()
    for g in range(4, len(GROUPS)):
        for copy in [swap1(g)] + swap2(g) + swap3(g):
            copy.wait_send()
    for i in range(5):
        over_y(i).wait_send()
    for n in range(2):
        over_x(n).wait_send()
    igrad_copy.wait()
    out_copy.wait()
    full_copy.wait()


def run_backward(*arrays):
    sds = jax.ShapeDtypeStruct
    outs = (sds((ROWS, D), BF), sds((ROWS, D), F32), sds((PARTS, PER, 8, 3, 16, SB), BF), sds((16, D), F32))
    any_ = pl.BlockSpec(memory_space=pl.ANY)
    vm = pl.BlockSpec(memory_space=pltpu.VMEM)
    sm = pl.BlockSpec(memory_space=pltpu.SMEM)
    dma = pltpu.SemaphoreType.DMA
    return pl.pallas_call(
        backward_kernel,
        out_shape=outs,
        in_specs=[sm] * 3 + [vm] * 3 + [any_] * 10,
        out_specs=[any_] * 3 + [vm],
        scratch_shapes=[
            pltpu.VMEM((ROWS, 3 * D), BF),
            pltpu.VMEM((ROWS, D), BF),
            pltpu.VMEM((D, ROWS), BF),
            pltpu.VMEM((D, ROWS), BF),
            pltpu.VMEM((ROWS, D), F32),
            pltpu.VMEM((4, 192, 3 * D), BF),
            pltpu.VMEM((4, 192, D), BF),
            pltpu.VMEM((ROWS, D), BF),
            pltpu.VMEM((ROWS, D), BF),
            pltpu.VMEM((ROWS, D), F32),
            pltpu.VMEM((3, 8, 48, SB), BF),
            pltpu.VMEM((LEFT + 8, 2, 48, SB), BF),
            pltpu.VMEM((LEFT + 8, 2, 48, SB), BF),
            pltpu.VMEM((4, 8, 48, SB), BF),
            pltpu.VMEM((16, 2, 2, 2, 48, SB), BF),
            pltpu.VMEM((16, 2, 2, 48, SB), BF),
            pltpu.VMEM((16, 2, 48, SB), BF),
            pltpu.VMEM((16, 48, SB), BF),
            pltpu.VMEM((48, 3, 16, SB), BF),
            pltpu.VMEM((3, 48, 16, SB), BF),
            pltpu.VMEM((48, 16, SB), BF),
            pltpu.VMEM((4, 2, PARTS, PER, 16, SB), BF),
            pltpu.VMEM((2, PARTS, PER, 3, 16, SB), BF),
            pltpu.VMEM((PARTS, PER, 8, 3, 16, SB), BF),
            pltpu.VMEM((16, D), F32),
            pltpu.VMEM((8, D), F32),
            pltpu.VMEM((8, SB), F32),
            pltpu.VMEM((4, 8, SB), F32),
            pltpu.VMEM((16, D), F32),
            pltpu.VMEM((8, D), F32),
            pltpu.VMEM((8, SB), F32),
            pltpu.VMEM((8, SB), F32),
            pltpu.VMEM((2, HALF, 1), F32),
            pltpu.VMEM((2, 1, HALF), F32),
            pltpu.VMEM((1, D), F32),
            pltpu.VMEM((D, 1), F32),
            dma((8,)),
            dma((3,)),
            dma((7,)),
            dma((7,)),
            dma((7, 5)),
            dma((7, 5)),
            dma((7, 3)),
            dma((7, 3)),
            dma((PARTS, 3)),
            dma((PARTS, 3)),
            dma((PARTS, 7)),
            dma((PARTS, 7)),
            dma((8,)),
            dma((8,)),
            dma((3,)),
        ],
        compiler_params=pltpu.CompilerParams(
            collective_id=2, has_side_effects=True, vmem_limit_bytes=64 << 20
        ),
    )(*arrays)


def split(value):
    high = value.astype(BF)
    return high, (value - high.astype(F32)).astype(BF)


def update_kernel(
    small,
    gain,
    bias,
    full,
    master,
    left_stats,
    right_stats,
    left_root,
    right_root,
    out_in,
    igrad_in,
    o_grad,
    o_left,
    o_right,
    o_new,
    o_copy,
    o_unit,
    o_hidden,
    o_head,
    o_layer,
    o_norm,
    o_norm_new,
    o_out,
    o_igrad,
    turned,
    stage_out,
    stage_igrad,
    sem,
):
    slot = pl.program_id(0)
    moves_in = (
        pltpu.make_async_copy(out_in, stage_out, sem.at[0]),
        pltpu.make_async_copy(igrad_in, stage_igrad, sem.at[1]),
    )
    moves = (
        pltpu.make_async_copy(stage_out, o_out, sem.at[2]),
        pltpu.make_async_copy(stage_igrad, o_igrad, sem.at[3]),
    )

    @pl.when(slot == 0)
    def _():
        for move in moves_in:
            move.start()
        for i in range(4):
            o_unit[6 * i : 6 * i + 6, :] = many_rows(small[i : i + 1, :])
        o_hidden[...] = many_rows(small[6:7, :])
        o_norm[...] = small[4:6, :]
        rate = 0.2 / math.sqrt(ROWS * 32)
        o_norm_new[0:1, :] = one_row(gain[...]) - rate * small[4:5, :]
        o_norm_new[1:2, :] = one_row(bias[...]) - rate * small[5:6, :]
        lane = lax.broadcasted_iota(jnp.int32, (16, D), 1) // HD
        row = lax.broadcasted_iota(jnp.int32, (16, D), 0)
        by_head = jnp.sum(jnp.where(lane == row, small[9:10, :], 0.0), axis=1, keepdims=True)
        square = lax.broadcasted_iota(jnp.int32, (16, 128), 1)
        diagonal = square == lax.broadcasted_iota(jnp.int32, (16, 128), 0)
        o_head[...] = jnp.sum(jnp.where(diagonal, by_head, 0.0), axis=0, keepdims=True)[:, :12]
        pair = jnp.sum(small[7:9, :], axis=1, keepdims=True)
        first = lax.broadcasted_iota(jnp.int32, (1, 2), 1) == 0
        o_layer[...] = jnp.where(first, pair[0:1], pair[1:2])

    start = pl.multiple_of(lax.axis_index("mp") * 96, 16)
    own = full[0, pl.ds(start, 96), :]
    whole = full[0]
    o_grad[0] = own.astype(F32)
    o_left[0] = BETA * left_stats[0] + (1.0 - BETA) * nt(own, whole)
    turned[...] = whole.T
    o_right[0] = BETA * right_stats[0] + (1.0 - BETA) * nn(turned[pl.ds(start, 96), :], whole)
    root_high, root_low = split(left_root[0])
    left_part = nn(root_high, whole) + nn(root_low, whole)
    part_high, part_low = split(left_part)
    right_high, right_low = split(right_root[0])
    update = nn(part_high, right_high) + nn(part_low, right_high) + nn(part_high, right_low)
    new = master[0] - RATE * update
    o_new[0] = new
    o_copy[0] = new.astype(BF)

    @pl.when(slot == 2)
    def _():
        for first, then in zip(moves_in, moves):
            first.wait()
            then.start()

    @pl.when(slot == 5)
    def _():
        for move in moves:
            move.wait()


def run_update(*arrays):
    sds = jax.ShapeDtypeStruct
    whole = pl.BlockSpec((1, SB, SB), lambda s: (s, 0, 0))
    rows = pl.BlockSpec((1, 96, SB), lambda s: (s, 0, 0))
    any_ = pl.BlockSpec(memory_space=pl.ANY)

    def const(*shape):
        return pl.BlockSpec(shape, lambda s: (0, 0))

    flat = const(6, 128)
    return pl.pallas_call(
        update_kernel,
        grid=(6,),
        out_shape=(sds((6, 96, SB), F32),) * 4
        + (
            sds((6, 96, SB), BF),
            sds((24, 128), F32),
            sds((6, 128), F32),
            sds((1, 12), F32),
            sds((1, 2), F32),
            sds((2, D), F32),
            sds((2, D), F32),
            sds((ROWS, D), BF),
            sds((ROWS, D), F32),
        ),
        in_specs=[const(16, D), flat, flat, whole] + [rows] * 4 + [whole] + [any_] * 2,
        out_specs=[rows] * 5
        + [const(24, 128), flat, const(1, 12), const(1, 2), const(2, D), const(2, D), any_, any_],
        scratch_shapes=[
            pltpu.VMEM((SB, SB), BF),
            pltpu.VMEM((ROWS, D), BF),
            pltpu.VMEM((ROWS, D), F32),
            pltpu.SemaphoreType.DMA((4,)),
        ],
        compiler_params=pltpu.CompilerParams(vmem_limit_bytes=64 << 20),
    )(*arrays)


PLACE = tuple(FF_BLOCKS + SENT.index(b) for b in range(16)) + tuple(
    8 * (col // 2) + 4 * which + 2 * row + col % 2 for which in range(2) for row in range(2) for col in range(8)
)


def fast_body(
    tokens,
    segments,
    head_mask,
    unit_mask,
    hidden_mask,
    layer_gates,
    qkv_weight,
    out_weight,
    norm_gain,
    norm_bias,
    up_weight,
    down_weight,
    cotangent,
    owner_slot,
    master,
    left_stats,
    right_stats,
    left_root,
    right_root,
):
    gain = norm_gain.reshape(6, 128)
    bias = norm_bias.reshape(6, 128)
    (output, joined, ctx, ctxT, tokT, summed_grad, sums, far, wq, wo, lse, small) = run_forward(
        layer_gates,
        head_mask,
        tokens,
        cotangent,
        segments,
        unit_mask.reshape(24, 128),
        hidden_mask.reshape(6, 128),
        gain,
        bias,
        qkv_weight,
        out_weight,
        up_weight,
        down_weight,
    )
    slot_order = jnp.sum(
        jnp.where(owner_slot[None, :] == jnp.arange(48)[:, None], jnp.asarray(PLACE)[None, :], 0), axis=1
    )
    output, input_grad, full, small = run_backward(
        layer_gates,
        head_mask,
        slot_order,
        small,
        segments,
        lse,
        sums,
        far,
        joined,
        ctx,
        ctxT,
        tokT,
        summed_grad,
        wq,
        wo,
        output,
    )
    (
        owned,
        left_new,
        right_new,
        weight_new,
        weight_copy,
        unit_grad,
        hidden_grad,
        head_grad,
        layer_grad,
        norm_grad,
        norm_new,
        output,
        input_grad,
    ) = run_update(
        small,
        gain,
        bias,
        full.reshape(6, SB, SB),
        master,
        left_stats,
        right_stats,
        left_root,
        right_root,
        output,
        input_grad,
    )
    return (
        output,
        input_grad,
        head_grad.reshape(12),
        unit_grad.reshape(FF),
        hidden_grad.reshape(D),
        layer_grad.reshape(2),
        norm_grad,
        norm_new,
        owned,
        left_new,
        right_new,
        weight_new,
        weight_copy,
    )


def solution(mesh):
    return jax.shard_map(
        fast_body if dict(mesh.shape) == {"dp": 8, "mp": 4} else body,
        mesh=mesh,
        in_specs=(
            P(("dp", "mp"), None),
            P(("dp", "mp"), None),
            P(),
            P(),
            P(),
            P(),
            P("mp", None),
            P("mp", None),
            P(),
            P(),
            P(None, "mp"),
            P(None, "mp"),
            P(("dp", "mp"), None),
            P(),
            P("dp", "mp", None),
            P("dp", "mp", None),
            P("dp", "mp", None),
            P("dp", "mp", None),
            P("dp", None, None),
        ),
        out_specs=(
            P(("dp", "mp"), None),
            P(("dp", "mp"), None),
            P(),
            P(),
            P(),
            P(),
            P(),
            P(),
            P("dp", "mp", None),
            P("dp", "mp", None),
            P("dp", "mp", None),
            P("dp", "mp", None),
            P("dp", "mp", None),
        ),
        check_vma=False,
    )
```

```python
from functools import partial
import math

import jax
import jax.numpy as jnp
from jax import lax
from jax.experimental import pallas as pl
from jax.experimental.pallas import tpu as pltpu
from jax.sharding import PartitionSpec as P

FF = 3072
SB = 384


HIGH = lax.Precision.HIGHEST
BETA = 0.5
RATE = 0.5
EPS = 1e-12
MASKED = -1e30


def gelu_exact(values):
    return jax.nn.gelu(values, approximate=False)


def normalize(summed, gain_in, offset, hidden_gate):
    centre = summed - jnp.mean(summed, axis=-1, keepdims=True)
    spread = jnp.mean(centre * centre, axis=-1, keepdims=True)
    return (centre * lax.rsqrt(spread + EPS) * gain_in + offset) * hidden_gate


def split_heads(block_joined, head_count):
    pieces = block_joined.reshape(block_joined.shape[0], 3, head_count, -1)
    return (pieces[:, 0], pieces[:, 1], pieces[:, 2])


def masked_scores(queries, keys_in, labels, factor):
    scores = (
        jnp.einsum("qhd,khd->hqk", queries, keys_in, preferred_element_type=jnp.float32) * factor
    )
    allowed = labels[:, None] == labels[None, :]
    return jnp.where(allowed[None], scores, MASKED)


def attend_forward(packed, head_count, factor):
    block_joined, labels = packed
    queries, keys_in, values_in = split_heads(block_joined, head_count)
    scores = masked_scores(queries, keys_in, labels, factor)
    highest = jnp.max(scores, axis=-1, keepdims=True)
    raised = jnp.exp(scores - highest)
    totals = jnp.sum(raised, axis=-1, keepdims=True)
    weights_low = (raised / totals).astype(jnp.bfloat16)
    context = jnp.einsum("hqk,khd->qhd", weights_low, values_in, preferred_element_type=jnp.float32)
    return (context, (highest + jnp.log(totals))[:, :, 0])


def attend_backward(packed, head_count, factor):
    block_joined, log_totals, context_grad, labels = packed
    queries, keys_in, values_in = split_heads(block_joined, head_count)
    scores = masked_scores(queries, keys_in, labels, factor)
    weights_full = jnp.exp(scores - log_totals[:, :, None])
    weights_low = weights_full.astype(jnp.bfloat16)
    values_grad = jnp.einsum(
        "hqk,qhd->khd", weights_low, context_grad, preferred_element_type=jnp.float32
    )
    weights_grad = jnp.einsum(
        "qhd,khd->hqk", context_grad, values_in, preferred_element_type=jnp.float32
    )
    inner_sum = jnp.sum(weights_full * weights_grad, axis=-1, keepdims=True)
    scores_grad = (weights_full * (weights_grad - inner_sum)).astype(jnp.bfloat16)
    queries_grad = (
        jnp.einsum("hqk,khd->qhd", scores_grad, keys_in, preferred_element_type=jnp.float32)
        * factor
    )
    keys_grad = (
        jnp.einsum("hqk,qhd->khd", scores_grad, queries, preferred_element_type=jnp.float32)
        * factor
    )
    merged = jnp.concatenate([queries_grad, keys_grad, values_grad], axis=1)
    return merged.reshape(merged.shape[0], -1).astype(jnp.bfloat16)


def contract_rows(left, right):
    return lax.dot_general(
        left, right, (((0,), (0,)), ((), ())), preferred_element_type=jnp.float32
    )


def contract_cols(left, right):
    return lax.dot_general(
        left, right, (((1,), (1,)), ((), ())), preferred_element_type=jnp.float32
    )


def body(
    tokens,
    segments,
    head_mask,
    unit_mask,
    hidden_mask,
    layer_gates,
    qkv_weight,
    out_weight,
    norm_gain,
    norm_bias,
    up_weight,
    down_weight,
    cotangent,
    owner_slot,
    master,
    left_stats,
    right_stats,
    left_root,
    right_root,
):
    row_count = tokens.shape[0]
    width = tokens.shape[1]
    head_count = head_mask.shape[0]
    head_width = width // head_count
    block_rows = segments.shape[1]
    block_count = segments.shape[0]
    factor = 1.0 / math.sqrt(head_width)
    model_size = lax.axis_size("mp")
    share = FF // model_size
    part_rows = SB // model_size
    total_tokens = row_count * lax.axis_size("dp") * model_size
    head_gate = head_mask.astype(jnp.float32)
    unit_gate = unit_mask.astype(jnp.float32)
    hidden_gate = hidden_mask.astype(jnp.float32)
    inputs = tokens.astype(jnp.float32)
    back_full = cotangent.astype(jnp.float32)
    qkv_full, out_full, up_full, down_full = (
        lax.all_gather(qkv_weight, "mp", axis=0, tiled=True),
        lax.all_gather(out_weight, "mp", axis=0, tiled=True),
        lax.all_gather(up_weight, "mp", axis=1, tiled=True),
        lax.all_gather(down_weight, "mp", axis=1, tiled=True),
    )
    joined_qkv = jnp.dot(tokens, qkv_full, preferred_element_type=jnp.float32).astype(jnp.bfloat16)
    joined_blocks = joined_qkv.reshape(block_count, block_rows, 3 * width)
    context, log_totals = lax.map(
        partial(attend_forward, head_count=head_count, factor=factor), (joined_blocks, segments)
    )
    context = context.reshape(row_count, head_count, head_width)
    gated_low = (context * head_gate[None, :, None]).reshape(row_count, width).astype(jnp.bfloat16)
    attn_out = jnp.dot(gated_low, out_full, preferred_element_type=jnp.float32)
    summed = inputs + layer_gates[0] * attn_out
    hidden, norm_pull = jax.vjp(normalize, summed, norm_gain, norm_bias, hidden_gate)
    hidden_low = hidden.astype(jnp.bfloat16)
    pre_act = jnp.dot(hidden_low, up_full, preferred_element_type=jnp.float32)
    active, gelu_pull = jax.vjp(gelu_exact, pre_act)
    active_low = (active * unit_gate).astype(jnp.bfloat16)
    branch = contract_cols(active_low, down_full)
    output = (hidden + layer_gates[1] * branch).astype(jnp.bfloat16)
    back_rounded = (layer_gates[1] * back_full).astype(jnp.bfloat16)
    qkv_full, out_full, up_full, down_full = (
        lax.all_gather(qkv_weight, "mp", axis=0, tiled=True),
        lax.all_gather(out_weight, "mp", axis=0, tiled=True),
        lax.all_gather(up_weight, "mp", axis=1, tiled=True),
        lax.all_gather(down_weight, "mp", axis=1, tiled=True),
    )
    grad_active = jnp.dot(back_rounded, down_full, preferred_element_type=jnp.float32)
    unit_grad = jnp.sum(grad_active * active, axis=0)
    grad_inner = gelu_pull(grad_active * unit_gate)[0].astype(jnp.bfloat16)
    hidden_back = contract_cols(grad_inner, up_full)
    up_term = contract_rows(grad_inner, hidden_low)
    down_term = contract_rows(active_low, back_rounded)
    unit_local = (
        lax.psum_scatter(
            jnp.stack([up_term, down_term], axis=1).astype(jnp.bfloat16),
            "mp",
            scatter_dimension=0,
            tiled=True,
        )
        .astype(jnp.float32)
        .transpose(1, 2, 0)
    )
    summed_grad, gain_grad, bias_grad, mask_grad = norm_pull(back_full + hidden_back)
    layer_grad = jnp.stack([jnp.sum(summed_grad * attn_out), jnp.sum(back_full * branch)])
    out_back = (layer_gates[0] * summed_grad).astype(jnp.bfloat16)
    gated_grad = contract_cols(out_back, out_full).astype(jnp.bfloat16)
    gated_heads = gated_grad.reshape(row_count, head_count, head_width)
    head_grad = jnp.sum(context * gated_heads.astype(jnp.float32), axis=(0, 2))
    context_grad = gated_heads * head_mask.astype(jnp.bfloat16)[None, :, None]
    joined_grad = lax.map(
        partial(attend_backward, head_count=head_count, factor=factor),
        (
            joined_blocks,
            log_totals,
            context_grad.reshape(block_count, block_rows, head_count, head_width),
            segments,
        ),
    )
    joined_grad = joined_grad.reshape(row_count, 3 * width)
    input_grad = summed_grad + contract_cols(joined_grad, qkv_full)
    tiles = width // SB
    qkv_term = jnp.einsum(
        "tri,tcj->rcij",
        tokens.reshape(row_count, tiles, SB),
        joined_grad.reshape(row_count, 3 * tiles, SB),
        preferred_element_type=jnp.float32,
    )
    out_term = jnp.einsum(
        "tri,tcj->rcij",
        gated_low.reshape(row_count, tiles, SB),
        out_back.reshape(row_count, tiles, SB),
        preferred_element_type=jnp.float32,
    )
    attn_terms = jnp.concatenate(
        [
            qkv_term.reshape(-1, model_size, part_rows, SB),
            out_term.reshape(-1, model_size, part_rows, SB),
        ],
        axis=0,
    )
    attn_rows = (
        lax.psum_scatter(attn_terms.astype(jnp.bfloat16), "mp", scatter_dimension=1, tiled=True)
        .astype(jnp.float32)
        .reshape(-1, part_rows, SB)
    )
    unit_split = unit_local.reshape(2, tiles, model_size, part_rows, share)
    unit_rows = lax.all_to_all(
        unit_split.astype(jnp.bfloat16), "mp", split_axis=2, concat_axis=4, tiled=True
    ).astype(unit_split.dtype)
    unit_rows = (
        unit_rows.reshape(2, tiles, part_rows, FF // SB, SB)
        .transpose(0, 1, 3, 2, 4)
        .reshape(-1, part_rows, SB)
    )
    all_rows = jnp.concatenate([attn_rows, unit_rows], axis=0)
    slot_count = owner_slot.shape[0]
    pick = (owner_slot[None, :] == jnp.arange(slot_count)[:, None]).astype(jnp.bfloat16)
    flat_rows = all_rows.astype(jnp.bfloat16).reshape(slot_count, -1)
    slotted = jnp.dot(pick, flat_rows, preferred_element_type=jnp.float32).reshape(all_rows.shape)
    owned = lax.psum_scatter(
        slotted.astype(jnp.bfloat16), "dp", scatter_dimension=0, tiled=True
    ).astype(jnp.float32)
    full_grad = lax.all_gather(owned.astype(jnp.bfloat16), "mp", axis=1, tiled=True).astype(
        owned.dtype
    )
    row_start = lax.axis_index("mp") * part_rows
    columns = lax.dynamic_slice_in_dim(full_grad, row_start, part_rows, 2)
    left_new = BETA * left_stats + (1.0 - BETA) * jnp.einsum(
        "srj,skj->srk", owned, full_grad, precision=HIGH
    )
    right_new = BETA * right_stats + (1.0 - BETA) * jnp.einsum(
        "sjr,sjk->srk", columns, full_grad, precision=HIGH
    )
    left_part = jnp.einsum("sri,sij->srj", left_root, full_grad, precision=HIGH)
    update = jnp.einsum("srj,sjk->srk", left_part, right_root, precision=HIGH)
    weight_new = master - RATE * update
    norm_grad = jnp.stack([gain_grad, bias_grad])
    norm_grad, mask_grad, head_grad, layer_grad, unit_grad = lax.psum(
        (norm_grad, mask_grad, head_grad, layer_grad, unit_grad), ("dp", "mp")
    )
    norm_new = jnp.stack([norm_gain, norm_bias]) - 0.2 / math.sqrt(total_tokens) * norm_grad
    return (
        output,
        input_grad,
        head_grad,
        unit_grad,
        mask_grad,
        layer_grad,
        norm_grad,
        norm_new,
        owned,
        left_new,
        right_new,
        weight_new,
        weight_new.astype(jnp.bfloat16),
    )


F32 = jnp.float32
BF = jnp.bfloat16
MESH = pl.DeviceIdType.MESH
LOG2E = 1.4426950408889634
ROWS = 1024
D = 768
HD = 64
BLK = 512
NT_DIMS = (((1,), (1,)), ((), ()))
NN_DIMS = (((1,), (0,)), ((), ()))


def nn(left, right):
    return lax.dot_general(left, right, NN_DIMS, preferred_element_type=F32)


def nt(left, right):
    return lax.dot_general(left, right, NT_DIMS, preferred_element_type=F32)


def coords():
    d = lax.axis_index("dp")
    m = lax.axis_index("mp")
    return d // 2, d % 2, m // 2, m % 2


def at(z, x, y, c):
    return (2 * z + x, 2 * y + c)


def gelu_parts(x):
    ax = jnp.abs(x)
    e = jnp.exp2(x * x * (-0.5 * LOG2E))
    t = 1.0 / (1.0 + (0.3275911 * math.sqrt(0.5)) * ax)
    poly = t * (
        0.5 * 0.254829592
        + t
        * (
            -0.5 * 0.284496736
            + t * (0.5 * 1.421413741 + t * (-0.5 * 1.453152027 + t * (0.5 * 1.061405429)))
        )
    )
    tail = poly * e
    cdf = jnp.where(x < 0, tail, 1.0 - tail)
    active = x * cdf
    return active, cdf + x * (e * (1.0 / math.sqrt(2.0 * math.pi)))


def colsum(v):
    return jnp.sum(v, axis=0, keepdims=True)


def row_norm(summed):
    centre = summed - jnp.mean(summed, axis=-1, keepdims=True)
    spread = jnp.mean(centre * centre, axis=-1, keepdims=True)
    inv = lax.rsqrt(spread + EPS)
    return centre * inv, inv


def one_row(v):
    return jnp.concatenate([v[i : i + 1] for i in range(v.shape[0])], axis=1)


def many_rows(v):
    return jnp.concatenate([v[:, 128 * i : 128 * i + 128] for i in range(v.shape[1] // 128)], axis=0)


def head_lanes(heads):
    which = lax.broadcasted_iota(jnp.int32, (1, D), 1) // HD
    row = jnp.zeros((1, D), F32)
    for h in range(12):
        row = row + jnp.where(which == h, heads[h].astype(F32), 0.0)
    return row


HALF = BLK // 2


def first_rows(segs):
    values = segs[...].astype(F32)
    begin = jnp.zeros((2, 1), F32)
    for item in range(6):
        count = jnp.sum(jnp.where(values == item, 1.0, 0.0), axis=1, keepdims=True)
        before = jnp.sum(jnp.where(values < item, 1.0, 0.0), axis=1, keepdims=True)
        begin = begin + jnp.where(count == HALF, before, 0.0)
    return begin


def turning(begin, sign):
    row = lax.broadcasted_iota(jnp.int32, (BLK, BLK), 0).astype(F32)
    col = lax.broadcasted_iota(jnp.int32, (BLK, BLK), 1).astype(F32)
    off = sign * (col - row) - begin
    return jnp.where((off == 0) | (off == -BLK), 1.0, 0.0)


def turn_labels(segs, begin, segcol, segrow):
    for b in range(2):
        hot = turning(begin[b : b + 1], 1)[HALF:, :]
        column = jnp.sum(hot * segs[b : b + 1, :].astype(F32), axis=1, keepdims=True)
        segcol[b] = column
        segrow[b] = jnp.broadcast_to(column, (HALF, 128)).T[0:1, :]


MOVED = (8, 8, 4)
LEFT = 8 - MOVED[2]
NPIECE = 8


def forward_kernel(
    gates,
    heads,
    tokens_in,
    cot_in,
    segs,
    units,
    hidden,
    gain_in,
    bias_in,
    qkv_in,
    out_in,
    up_in,
    down_in,
    o_out,
    o_joined,
    o_ctx,
    o_ctxT,
    o_tokT,
    o_sgrad,
    o_sums,
    o_far,
    o_wq,
    o_wo,
    lse,
    small,
    wq,
    wo,
    wu,
    wd,
    joined,
    ctx,
    ctxT,
    tokT,
    attn,
    blow,
    bT,
    branch,
    hback,
    grads,
    got1,
    got2,
    tokens,
    cot,
    segcol,
    segrow,
    ugate,
    vec,
    send_sem,
    recv_sem,
    loc_sem,
    out_sem,
    c_send,
    c_recv,
    x_send,
    x_recv,
):
    z, x, y, c = coords()
    hT = tokT
    hlow = ctx
    act, inner, outv = (joined.at[:, pl.ds(D * i, D)] for i in range(3))
    m = 2 * y + c
    ms = 2 * y + 1 - c
    my = 2 * (1 - y) + c
    mys = 2 * (1 - y) + 1 - c
    sib = at(z, x, y, 1 - c)
    ypeer = at(z, x, 1 - y, c)
    xpeer = at(z, 1 - x, y, c)
    zpeer = at(z + 1 - 2 * (z % 2), x, y, c)
    g0 = gates[0]
    g1 = gates[1]

    barrier = pltpu.get_barrier_semaphore()
    for peer in (sib, ypeer, xpeer, zpeer):
        pl.semaphore_signal(barrier, inc=1, device_id=peer, device_id_type=MESH)
    loads = (
        pltpu.make_async_copy(tokens_in, blow, out_sem.at[6]),
        pltpu.make_async_copy(cot_in, ctx, out_sem.at[7]),
    )
    for copy in loads:
        copy.start()
    begin = first_rows(segs)
    pl.semaphore_wait(barrier, 4)

    def spot(j):
        if j < 3:
            return 0, 192, pl.ds(768 * j, 768)
        if j == 3:
            return 1, 192, slice(None)
        return 2 + (j - 4) // 2, 768, pl.ds(384 * (j % 2), 384)

    def full(j, i, h=None):
        which, n, cols = spot(j)
        ref = (wq, wo, wu, wd)[which]
        if h is None:
            return ref.at[i, :, cols]
        return ref.at[i, pl.ds(pl.multiple_of(h * (n // 2), 16), n // 2), cols]

    def own(j, h=None):
        which, n, cols = spot(j)
        ref = (qkv_in, out_in, up_in, down_in)[which]
        if h is None:
            return ref.at[:, cols]
        return ref.at[pl.ds(pl.multiple_of(h * (n // 2), 16), n // 2), cols]

    def remote(src, dst, j, k, dev):
        return pltpu.make_async_remote_copy(
            src_ref=src,
            dst_ref=dst,
            send_sem=send_sem.at[j, k],
            recv_sem=recv_sem.at[j, k],
            device_id=dev,
            device_id_type=MESH,
        )

    def s1(j):
        return remote(own(j), full(j, m), j, 0, sib)

    def half_of(j):
        return (x, xpeer) if j < 4 else (z % 2, zpeer)

    def s2(j):
        h, _ = half_of(j)
        return remote(own(j, h), full(j, m, h), j, 1, ypeer)

    def s3(j):
        h, peer = half_of(j)
        return remote(full(j, my, h), full(j, my, h), j, 2, peer)

    def s4(j):
        h, _ = half_of(j)
        return remote(full(j, my, h), full(j, my, h), j, 3, sib)

    def s5(j):
        h, _ = half_of(j)
        return remote(full(j, my, 1 - h), full(j, my, 1 - h), j, 4, sib)

    def local(j):
        return pltpu.make_async_copy(own(j), full(j, m), loc_sem.at[j])

    def first(j):
        s2(j).start()
        s1(j).start()
        local(j).start()

    def second(j):
        s2(j).wait_recv()
        s3(j).start()
        s4(j).start()

    def third(j):
        s3(j).wait_recv()
        s5(j).start()

    def finish_near(j):
        local(j).wait()
        s1(j).wait_recv()

    def finish_far(j):
        s4(j).wait_recv()
        s5(j).wait_recv()

    def finish_sends(j):
        for s in (s1, s2, s3, s4, s5):
            s(j).wait_send()

    for j in range(3):
        first(j)

    turn_labels(segs, begin, segcol, segrow)
    for copy in loads:
        copy.wait()
    def turn(src, dst):
        @pl.loop(0, 2)
        def _(b):
            hot = turning(jnp.where(b == 0, begin[0:1], begin[1:2]), 1).astype(BF)
            rows = pl.ds(pl.multiple_of(b * BLK, BLK), BLK)
            dst[rows, :] = nn(hot, src[rows, :]).astype(BF)

    def backs(lo, hi):
        @pl.loop(lo, hi)
        def _(r):
            rows = pl.ds(pl.multiple_of(r * 256, 256), 256)
            low = (g1 * cot[rows, :].astype(F32)).astype(BF)
            blow[rows, :] = low
            bT[:, rows] = low.T

    turn(blow, tokens)

    near_sum = (attn, branch, hback)

    def project(j, near):
        yy = y if near else 1 - y

        @pl.loop(0, 2)
        def _(r):
            rows = pl.ds(pl.multiple_of(r * 512, 512), 512)
            w = wq[pl.ds(2 * yy, 2), :, pl.ds(768 * j, 768)].reshape(SB, D)
            one = nn(tokens[rows, pl.ds(pl.multiple_of(SB * yy, 128), SB)], w)
            if near:
                near_sum[j][rows, :] = one
            else:
                joined[rows, pl.ds(768 * j, 768)] = (near_sum[j][rows, :] + one).astype(BF)

    for j in range(3):
        finish_near(j)
    project(0, True)
    second(0)
    turn(ctx, cot)
    for i in range(4):
        ugate[i] = one_row(units[6 * i : 6 * i + 6, :].astype(F32))
    vec[0:1, :] = head_lanes(heads)
    vec[1:2, :] = one_row(hidden[...].astype(F32))
    vec[2:3, :] = one_row(gain_in[...])
    vec[3:4, :] = one_row(bias_in[...])
    hgate, mgate, gain, bias = (vec.at[i : i + 1] for i in range(4))
    project(1, True)
    second(1)
    project(2, True)
    third(0)
    backs(0, 2)
    second(2)
    for j in range(3, NPIECE):
        first(j)
    tokT[...] = tokens[...].T
    tok_copy = pltpu.make_async_copy(tokT, o_tokT, out_sem.at[0])
    tok_copy.start()
    third(1)
    backs(2, 4)
    finish_far(0)
    project(0, False)
    third(2)
    finish_far(1)
    project(1, False)
    finish_far(2)
    wq_copy = pltpu.make_async_copy(wq, o_wq, out_sem.at[1])
    wq_copy.start()
    project(2, False)
    joined_copy = pltpu.make_async_copy(joined, o_joined, out_sem.at[2])
    joined_copy.start()

    scale = LOG2E / math.sqrt(HD)
    half_iota = lax.broadcasted_iota(jnp.int32, (1, 128), 1) // HD
    halves = [(half_iota == e).astype(F32).astype(BF) for e in range(2)]

    def by_head(v):
        return jnp.concatenate([v * halves[0], v * halves[1]], axis=0)

    def attend(i):
        b = i // 6
        p = i % 6
        lane = pl.multiple_of(p * 128, 128)
        for part in range(2):
            rows = pl.ds(pl.multiple_of(b * BLK + part * HALF, HALF), HALF)
            q = joined[rows, pl.ds(lane, 128)]
            k = joined[rows, pl.ds(D + lane, 128)]
            v = joined[rows, pl.ds(2 * D + lane, 128)]
            s = nt(by_head(k), q).reshape(2, HALF, HALF) * scale
            if part:
                s = jnp.where(segcol[b] == segrow[b], s, MASKED)
            top = jnp.max(s, axis=1, keepdims=True)
            pr = jnp.exp2(s - top)
            tot = jnp.sum(pr, axis=1, keepdims=True)
            low = (pr * (1.0 / tot)).astype(BF).reshape(BLK, HALF)
            lse[pl.ds(2 * i, 2), :, part * HALF : part * HALF + HALF] = top + jnp.log(tot) * LOG2E
            total = nn(by_head(v).T, low)
            ctxT[pl.ds(lane, 128), rows] = total.astype(BF)
            ctx[rows, pl.ds(lane, 128)] = total.T.astype(BF)

    plan = {
        0: [lambda: second(3)],
        5: [lambda: second(4), lambda: third(3)],
    }

    @pl.loop(0, 12)
    def _(i):
        attend(i)
        for at_step, todo in plan.items():

            @pl.when(i == at_step)
            def _(todo=todo):
                for f in todo:
                    f()

    ctx_copy = pltpu.make_async_copy(ctx, o_ctx, out_sem.at[3])
    ctx_copy.start()
    ctxT_copy = pltpu.make_async_copy(ctxT, o_ctxT, out_sem.at[4])
    ctxT_copy.start()
    finish_near(3)
    finish_far(3)
    wo_copy = pltpu.make_async_copy(wo, o_wo, out_sem.at[5])
    wo_copy.start()

    joined_copy.wait()
    tok_copy.wait()
    ctx_copy.wait()

    @pl.loop(0, 4)
    def _(r):
        rows = pl.ds(pl.multiple_of(r * 256, 256), 256)
        gated = ctx[rows, :] * hgate[...].astype(BF)
        a = nn(gated, wo[...].reshape(D, D))
        attn[rows, :] = a
        normed, _ = row_norm(tokens[rows, :].astype(F32) + g0 * a)
        low = ((normed * gain[...] + bias[...]) * mgate[...]).astype(BF)
        hlow[rows, :] = low
        hT[:, rows] = low.T

    small[...] = jnp.zeros_like(small)

    def feed(f, between={}):
        u = 2 * ((y + f // 2) % 2) + f % 2
        begin = f == 0
        w_up = wu.at[u]
        w_down = wd.at[u]

        @pl.loop(0, 2)
        def _(r):
            rows = pl.ds(pl.multiple_of(r * 512, 512), 512)
            pre = nn(hlow[rows, :], w_up[...])
            back = nn(blow[rows, :], w_down[...])
            active, slope = gelu_parts(pre)
            gate = ugate[u]
            small[pl.ds(u, 1), :] += colsum(back * active)
            a_low = (active * gate).astype(BF)
            i_low = (back * gate * slope).astype(BF)
            act[rows, :] = a_low
            inner[rows, :] = i_low
            up_part = nt(a_low, w_down[...])
            back_part = nt(i_low, w_up[...])
            if begin:
                branch[rows, :] = up_part
                hback[rows, :] = back_part
            else:
                branch[rows, :] += up_part
                hback[rows, :] += back_part
            for at_row, todo in between.items():
                pl.when(r == at_row)(todo)

        for which, (left, right) in enumerate(((hT, inner), (bT, act))):

            @pl.loop(0, 2)
            def _(r, which=which, left=left, right=right):
                rr = pl.ds(pl.multiple_of(r * SB, 128), SB)
                g = nn(left[rr, :], right[...]).astype(BF)
                for j in range(2):
                    grads[f, 4 * which + 2 * r + j] = g[:, SB * j : SB * j + SB].reshape(
                        2, 2, 2, 48, SB
                    )

    def swap1(f):
        return pltpu.make_async_remote_copy(
            src_ref=grads.at[f, :, 1 - c],
            dst_ref=got1.at[f],
            send_sem=c_send.at[f],
            recv_sem=c_recv.at[f],
            device_id=sib,
            device_id_type=MESH,
        )

    def swap2(f):
        return pltpu.make_async_remote_copy(
            src_ref=grads.at[f, pl.ds(0, MOVED[f]), c, :, 1 - x],
            dst_ref=got2.at[f, pl.ds(0, MOVED[f])],
            send_sem=x_send.at[f],
            recv_sem=x_recv.at[f],
            device_id=xpeer,
            device_id_type=MESH,
        )

    def plus(left, right):
        return (left.astype(F32) + right.astype(F32)).astype(BF)

    def sum1(f):
        swap1(f).wait_recv()

        @pl.loop(0, 8)
        def _(i):
            grads[f, i, c] = plus(grads[f, i, c], got1[f, i])

    for j in range(4, NPIECE):
        finish_near(j)

    def spread(f):
        sum1(f)
        swap2(f).start()

    def finish(f):
        swap2(f).wait_recv()

        @pl.loop(0, MOVED[f])
        def _(i):
            for yy in range(2):
                grads[f, i, c, yy, x] = plus(grads[f, i, c, yy, x], got2[f, i, yy])

        sums_copy(f).start()

    def sums_copy(f):
        return pltpu.make_async_copy(
            grads.at[f, pl.ds(0, MOVED[f]), c, :, x],
            o_sums.at[f, pl.ds(0, MOVED[f])],
            out_sem.at[9 + f],
        )

    def in_turn(*steps):
        def run():
            for step, i in steps:
                step(i)

        return run

    feed(0, {0: in_turn((second, 5), (third, 4)), 1: in_turn((second, 6))})
    swap1(0).start()
    feed(1, {0: in_turn((second, 7), (third, 5), (spread, 0)), 1: in_turn((third, 6))})
    swap1(1).start()
    third(7)
    for j in range(4, NPIECE):
        finish_far(j)
    feed(2, {0: in_turn((spread, 1))})
    swap1(2).start()
    feed(3, {0: in_turn((spread, 2)), 1: in_turn((finish, 0))})
    swap1(3).start()

    lane = lax.broadcasted_iota(jnp.int32, (1, D), 1)

    @pl.loop(0, 4)
    def _(r):
        rows = pl.ds(pl.multiple_of(r * 256, 256), 256)
        a = attn[rows, :]
        normed, inv = row_norm(tokens[rows, :].astype(F32) + g0 * a)
        plain = normed * gain[...] + bias[...]
        back = cot[rows, :].astype(F32)
        br = branch[rows, :]
        outv[rows, :] = (plain * mgate[...] + g1 * br).astype(BF)
        total = back + hback[rows, :]
        masked = total * mgate[...]
        small[4:5, :] += colsum(masked * normed)
        small[5:6, :] += colsum(masked)
        small[6:7, :] += colsum(total * plain)
        n = masked * gain[...]
        grad = (
            n
            - jnp.mean(n, axis=-1, keepdims=True)
            - normed * jnp.mean(n * normed, axis=-1, keepdims=True)
        ) * inv
        hback[rows, :] = grad
        small[7:8, :] += colsum(grad * a)
        small[8:9, :] += colsum(back * br)

    out_copy = pltpu.make_async_copy(outv, o_out, out_sem.at[6])
    out_copy.start()
    sgrad_copy = pltpu.make_async_copy(hback, o_sgrad, out_sem.at[7])
    sgrad_copy.start()
    sum1(3)
    grad_copies = [
        pltpu.make_async_copy(
            grads.at[2, pl.ds(MOVED[2], LEFT), c], o_far.at[pl.ds(0, LEFT)], out_sem.at[8]
        ),
        pltpu.make_async_copy(grads.at[3, :, c], o_far.at[pl.ds(LEFT, 8)], out_sem.at[12]),
    ]
    for copy in grad_copies:
        copy.start()
    finish(1)
    finish(2)
    for f in range(3):
        sums_copy(f).wait()
    for copy in grad_copies:
        copy.wait()
    for copy in (wq_copy, ctxT_copy, wo_copy, out_copy, sgrad_copy):
        copy.wait()
    for f in range(4):
        swap1(f).wait_send()
    for f in range(3):
        swap2(f).wait_send()
    for j in range(NPIECE):
        finish_sends(j)


def run_forward(*arrays):
    sds = jax.ShapeDtypeStruct
    outs = (
        sds((ROWS, D), BF),
        sds((ROWS, 3 * D), BF),
        sds((ROWS, D), BF),
        sds((D, ROWS), BF),
        sds((D, ROWS), BF),
        sds((ROWS, D), F32),
        sds((3, 8, 2, 48, SB), BF),
        sds((LEFT + 8, 2, 2, 48, SB), BF),
        sds((4, 192, 3 * D), BF),
        sds((4, 192, D), BF),
        sds((24, 1, BLK), F32),
        sds((16, D), F32),
    )
    any_ = pl.BlockSpec(memory_space=pl.ANY)
    vm = pl.BlockSpec(memory_space=pltpu.VMEM)
    sm = pl.BlockSpec(memory_space=pltpu.SMEM)
    return pl.pallas_call(
        forward_kernel,
        out_shape=outs,
        in_specs=[sm] * 2 + [any_] * 2 + [vm] * 5 + [any_] * 4,
        out_specs=[any_] * 10 + [vm] * 2,
        scratch_shapes=[
            pltpu.VMEM((4, 192, 3 * D), BF),
            pltpu.VMEM((4, 192, D), BF),
            pltpu.VMEM((4, D, D), BF),
            pltpu.VMEM((4, D, D), BF),
            pltpu.VMEM((ROWS, 3 * D), BF),
            pltpu.VMEM((ROWS, D), BF),
            pltpu.VMEM((D, ROWS), BF),
            pltpu.VMEM((D, ROWS), BF),
            pltpu.VMEM((ROWS, D), F32),
            pltpu.VMEM((ROWS, D), BF),
            pltpu.VMEM((D, ROWS), BF),
            pltpu.VMEM((ROWS, D), F32),
            pltpu.VMEM((ROWS, D), F32),
            pltpu.VMEM((4, 8, 2, 2, 2, 48, SB), BF),
            pltpu.VMEM((4, 8, 2, 2, 48, SB), BF),
            pltpu.VMEM((3, 8, 2, 48, SB), BF),
            pltpu.VMEM((ROWS, D), BF),
            pltpu.VMEM((ROWS, D), BF),
            pltpu.VMEM((2, HALF, 1), F32),
            pltpu.VMEM((2, 1, HALF), F32),
            pltpu.VMEM((4, 1, D), F32),
            pltpu.VMEM((8, D), F32),
            pltpu.SemaphoreType.DMA((NPIECE, 5)),
            pltpu.SemaphoreType.DMA((NPIECE, 5)),
            pltpu.SemaphoreType.DMA((NPIECE,)),
            pltpu.SemaphoreType.DMA((13,)),
            pltpu.SemaphoreType.DMA((4,)),
            pltpu.SemaphoreType.DMA((4,)),
            pltpu.SemaphoreType.DMA((3,)),
            pltpu.SemaphoreType.DMA((3,)),
        ],
        compiler_params=pltpu.CompilerParams(
            collective_id=1, has_side_effects=True, vmem_limit_bytes=64 << 20
        ),
    )(*arrays)


SENT = (12, 13, 14, 15, 0, 2, 4, 6, 8, 10, 1, 3, 5, 7, 9, 11)
GROUPS = (None,) * 4 + ((32, 4, 2), (36, 6, 3), (42, 6, 3))
FF_BLOCKS = 32
PARTS = 3
PER = 6 // PARTS


def backward_kernel(
    gates,
    heads,
    order,
    small_in,
    segs,
    lse,
    sums_in,
    far_in,
    joined_in,
    ctx_in,
    ctxT_in,
    tokT_in,
    sgrad_in,
    wq_in,
    wo_in,
    out_in,
    o_out,
    o_igrad,
    o_full,
    small_out,
    joined,
    ctx,
    ctxT,
    tokT,
    sgrad,
    wq,
    wo,
    outb,
    cgrad,
    igrad,
    ownv,
    farv,
    gotx,
    goty,
    ga,
    got1,
    got2,
    got3,
    part,
    gotz,
    total,
    slots,
    gz,
    gfull,
    sm_all,
    sm_rows,
    sm_lanes,
    sm_z,
    sm_back,
    sm_got1,
    sm_got2,
    sm_got3,
    segcol,
    segrow,
    hrow,
    hcol,
    load_sem,
    half_sem,
    ff_send,
    ff_recv,
    send_sem,
    recv_sem,
    z_send,
    z_recv,
    a_send,
    a_recv,
    f_send,
    f_recv,
    s_send,
    s_recv,
    out_sem,
):
    z, x, y, c = coords()
    g0 = gates[0]
    sib = at(z, x, y, 1 - c)
    ypeer = at(z, x, 1 - y, c)
    xpeer = at(z, 1 - x, y, c)
    diag = at(z, 1 - x, 1 - y, c)
    zpeers = [at((z + k) % 4, x, y, c) for k in (1, 2, 3)]

    loads = [
        pltpu.make_async_copy(src, dst, load_sem.at[i])
        for i, (src, dst) in enumerate(
            (
                (sgrad_in, sgrad),
                (wo_in, wo),
                (ctx_in, ctx),
                (ctxT_in, ctxT),
                (joined_in, joined),
                (tokT_in, tokT),
                (wq_in, wq),
                (out_in, ctx),
            )
        )
    ]
    halves_in = [
        pltpu.make_async_copy(sums_in.at[pl.ds(0, 2), :, y], ownv.at[pl.ds(0, 2)], half_sem.at[0]),
        pltpu.make_async_copy(far_in.at[:, :, x], farv, half_sem.at[1]),
        pltpu.make_async_copy(
            sums_in.at[2, pl.ds(0, MOVED[2]), y], ownv.at[2, pl.ds(0, MOVED[2])], half_sem.at[2]
        ),
    ]
    for copy in loads[:4]:
        copy.start()

    barrier = pltpu.get_barrier_semaphore()
    for peer in [sib, ypeer, xpeer, diag] + zpeers:
        pl.semaphore_signal(barrier, inc=1, device_id=peer, device_id_type=MESH)
    pl.semaphore_wait(barrier, 7)

    def remote(src, dst, sems, dev):
        return pltpu.make_async_remote_copy(
            src_ref=src,
            dst_ref=dst,
            send_sem=sems[0],
            recv_sem=sems[1],
            device_id=dev,
            device_id_type=MESH,
        )

    def pair(g, k):
        return send_sem.at[g, k], recv_sem.at[g, k]

    def first_block(f):
        return 8 * (2 * ((y + f // 2) % 2) + f % 2)

    def span(g):
        return (first_block(g), 8) if g < 4 else GROUPS[g][:2]

    def over_y(i):
        src, to = (
            (lambda: sums_in.at[0, :, 1 - y], goty.at[2]),
            (lambda: sums_in.at[1, :, 1 - y], goty.at[3]),
            (lambda: sums_in.at[2, pl.ds(0, MOVED[2]), 1 - y], goty.at[0, pl.ds(0, MOVED[2])]),
            (lambda: farv.at[pl.ds(0, LEFT), 1 - y], goty.at[0, pl.ds(MOVED[2], LEFT)]),
            (lambda: farv.at[pl.ds(LEFT, 8), 1 - y], goty.at[1]),
        )[i]
        return remote(src(), to, (ff_send.at[i], ff_recv.at[i]), ypeer)

    def over_x(i):
        part = (pl.ds(0, LEFT), pl.ds(LEFT, 8))[i]
        return remote(
            far_in.at[part, :, 1 - x], gotx.at[part], (ff_send.at[5 + i], ff_recv.at[5 + i]), xpeer
        )

    def mine(g, first, count):
        return ga.at[pl.ds(GROUPS[g][0] + first - FF_BLOCKS, count), c]

    def swap1(g):
        base, count, _ = GROUPS[g]
        src = ga.at[pl.ds(base - FF_BLOCKS, count), 1 - c]
        return remote(src, got1.at[pl.ds(base - FF_BLOCKS, count)], pair(g, 0), sib)

    def swap2(g):
        base, count, n = GROUPS[g]
        rest = count - n
        to = base - FF_BLOCKS
        found = [
            remote(mine(g, n, rest).at[:, :, 1 - x], got2.at[pl.ds(to + n, rest)], pair(g, 2), xpeer)
        ]
        if n:
            found.append(remote(mine(g, 0, n).at[:, 1 - y], got2.at[pl.ds(to, n)], pair(g, 1), ypeer))
        return found

    def swap3(g):
        base, count, n = GROUPS[g]
        rest = count - n
        to = base - FF_BLOCKS
        found = [
            remote(mine(g, n, rest).at[:, 1 - y, x], got3.at[pl.ds(to + n, rest)], pair(g, 4), ypeer)
        ]
        if n:
            found.append(remote(mine(g, 0, n).at[:, y, 1 - x], got3.at[pl.ds(to, n)], pair(g, 3), xpeer))
        return found

    def plus(left, right):
        return (left.astype(F32) + right.astype(F32)).astype(BF)

    def step1(g):
        base, count, _ = GROUPS[g]
        swap1(g).wait_recv()

        @pl.loop(base - FF_BLOCKS, base - FF_BLOCKS + count)
        def _(i):
            ga[i, c] = plus(ga[i, c], got1[i])

        for copy in swap2(g):
            copy.start()

    def step2(g):
        base, count, n = GROUPS[g]
        for copy in swap2(g):
            copy.wait_recv()

        @pl.loop(base - FF_BLOCKS, base - FF_BLOCKS + n)
        def _(i):
            ga[i, c, y] = plus(ga[i, c, y], got2[i])

        @pl.loop(base - FF_BLOCKS + n, base - FF_BLOCKS + count)
        def _(i):
            for yy in range(2):
                ga[i, c, yy, x] = plus(ga[i, c, yy, x], got2[i, yy])

        for copy in swap3(g):
            copy.start()

    def feed_far(n):
        over_x(n).wait_recv()

        @pl.loop(*((0, LEFT), (LEFT, LEFT + 8))[n])
        def _(i):
            farv[i] = plus(farv[i], gotx[i])

        over_y(3 + n).start()

    spare = 1 + c

    def unit(zz):
        return zz - (zz + 3 - spare) // 4

    def swapz(g, k):
        base, count = span(g)
        return remote(
            part.at[pl.ds(base, count), unit((z + k) % 4)],
            gotz.at[k - 1, pl.ds(base, count)],
            (z_send.at[g, k - 1], z_recv.at[g, k - 1]),
            zpeers[k - 1],
        )

    def step3(g):
        base, count = span(g)
        if g < 4:
            for i in ((2, 3), (4,), (0,), (1,))[g]:
                over_y(i).wait_recv()
        else:
            for copy in swap3(g):
                copy.wait_recv()
        moved = (8, 8, MOVED[2], 0)[g] if g < 4 else 0

        if moved:

            @pl.loop(0, moved)
            def _(i):
                part[base + i] = plus(ownv[g, i], goty[g, i]).reshape(3, 16, SB)

        @pl.loop(moved, count)
        def _(i):
            if g < 4:
                value = plus(farv[i - (8 - LEFT) if g == 2 else LEFT + i, y], goty[g, i])
            else:
                value = plus(ga[base - FF_BLOCKS + i, c, y, x], got3[base - FF_BLOCKS + i])
            part[base + i] = value.reshape(3, 16, SB)

        for k in (1, 2, 3):

            @pl.when((z + k) % 4 != spare)
            def _(k=k):
                swapz(g, k).start()

    def step4(g):
        base, count = span(g)

        @pl.when(z != spare)
        def _():
            for k in (1, 2, 3):
                swapz(g, k).wait_recv()

            @pl.loop(0, count)
            def _(i):
                value = part[base + i, unit(z)].astype(F32)
                for k in range(3):
                    value = value + gotz[k, base + i].astype(F32)
                total[base + i] = value.astype(BF)

    def small_copy(k):
        rows = pl.ds(pl.multiple_of(8 * c, 8), 8)
        away = pl.ds(pl.multiple_of(8 * (1 - c), 8), 8)
        lanes = pl.ds(pl.multiple_of(SB * y, 128), SB)
        other = pl.ds(pl.multiple_of(SB * (1 - y), 128), SB)
        src, dst, dev = (
            (sm_all.at[away], sm_got1, sib),
            (sm_rows.at[:, other], sm_got2, ypeer),
            (sm_lanes, sm_got3, xpeer),
            (sm_z.at[z], sm_z.at[z], zpeers[0]),
            (sm_z.at[z], sm_z.at[z], zpeers[1]),
            (sm_z.at[z], sm_z.at[z], zpeers[2]),
            (sm_back.at[rows, lanes], sm_back.at[rows, lanes], ypeer),
            (sm_back.at[rows], sm_back.at[rows], sib),
        )[k]
        return remote(src, dst, (s_send.at[k], s_recv.at[k]), dev)

    def small_take(stage):
        rows = pl.ds(pl.multiple_of(8 * c, 8), 8)
        away = pl.ds(pl.multiple_of(8 * (1 - c), 8), 8)
        lanes = pl.ds(pl.multiple_of(SB * y, 128), SB)
        other = pl.ds(pl.multiple_of(SB * (1 - y), 128), SB)
        if stage == 0:
            small_copy(0).wait_recv()
            sm_rows[...] = sm_all[rows, :] + sm_got1[...]
            small_copy(1).start()
        elif stage == 1:
            small_copy(1).wait_recv()
            sm_lanes[...] = sm_rows[:, lanes] + sm_got2[...]
            small_copy(2).start()
        elif stage == 2:
            small_copy(2).wait_recv()
            sm_z[z] = sm_lanes[...] + sm_got3[...]
            for k in (3, 4, 5):
                small_copy(k).start()
        elif stage == 3:
            for k in (1, 2, 3):
                sender = (z + 4 - k) % 4
                remote(
                    sm_z.at[sender], sm_z.at[sender], (s_send.at[2 + k], s_recv.at[2 + k]), zpeers[k - 1]
                ).wait_recv()
            sm_back[rows, lanes] = sm_z[0] + sm_z[1] + sm_z[2] + sm_z[3]
            small_copy(6).start()
        elif stage == 4:
            remote(
                sm_back.at[rows, other], sm_back.at[rows, other], (s_send.at[6], s_recv.at[6]), ypeer
            ).wait_recv()
            small_copy(7).start()
        else:
            remote(sm_back.at[away], sm_back.at[away], (s_send.at[7], s_recv.at[7]), sib).wait_recv()
            small_out[...] = sm_back[...]

    for n in range(2):
        over_x(n).start()
    for i in range(3):
        over_y(i).start()
    for copy in [loads[4]] + halves_in + loads[5:7]:
        copy.start()

    begin = first_rows(segs)
    turn_labels(segs, begin, segcol, segrow)
    hrow[...] = head_lanes(heads)
    hcol[...] = jnp.broadcast_to(hrow[...], (8, D)).T[:, 0:1]
    hgate = hrow
    sm_all[...] = small_in[...]
    loads[0].wait()
    loads[1].wait()
    loads[2].wait()

    @pl.loop(0, 4)
    def _(r):
        rows = pl.ds(pl.multiple_of(r * 256, 256), 256)
        low = (g0 * sgrad[rows, :]).astype(BF)
        outb[rows, :] = low
        grad = nt(low, wo[...].reshape(D, D)).astype(BF)
        sm_all[9:10, :] += colsum(ctx[rows, :].astype(F32) * grad.astype(F32))
        cgrad[rows, :] = grad * hgate[...].astype(BF)

    small_copy(0).start()
    loads[7].start()
    loads[3].wait()

    def weight_tiles(left, right, lane, rowgate, places):
        @pl.loop(0, 2)
        def _(r):
            rr = pl.ds(pl.multiple_of(r * SB, 128), SB)
            g = nn(left[rr, :], right[:, pl.ds(lane, SB)])
            if rowgate is not None:
                g = g * rowgate[rr, :]
            ga[places[0] + r * (places[1] - places[0])] = g.astype(BF).reshape(2, 2, 2, 48, SB)

    for j in range(2):
        weight_tiles(ctxT, outb, SB * j, hcol, (SENT.index(12 + j), SENT.index(14 + j)))

    swap1(4).start()
    loads[4].wait()

    scale = LOG2E / math.sqrt(HD)
    factor = 1.0 / math.sqrt(HD)
    half_iota = lax.broadcasted_iota(jnp.int32, (1, 128), 1) // HD
    halves = [(half_iota == e).astype(F32).astype(BF) for e in range(2)]

    def by_head(v):
        return jnp.concatenate([v * halves[0], v * halves[1]], axis=0)

    def of_head(v):
        return jnp.where(half_iota == 0, v[:HALF], v[HALF:])

    def attend_back(i):
        p = i // 2
        b = i % 2
        lane = pl.multiple_of(p * 128, 128)
        for part in range(2):
            rows = pl.ds(pl.multiple_of(b * BLK + part * HALF, HALF), HALF)
            q = joined[rows, pl.ds(lane, 128)]
            k = joined[rows, pl.ds(D + lane, 128)]
            v = joined[rows, pl.ds(2 * D + lane, 128)]
            do = cgrad[rows, pl.ds(lane, 128)]
            k2 = by_head(k)
            s = nt(k2, q).reshape(2, HALF, HALF) * scale
            if part:
                s = jnp.where(segcol[b] == segrow[b], s, MASKED)
            first = 2 * (b * 6 + p)
            pr = jnp.exp2(s - lse[pl.ds(first, 2), :, part * HALF : part * HALF + HALF])
            dp = nt(by_head(v), do).reshape(2, HALF, HALF)
            delta = jnp.sum(pr * dp, axis=1, keepdims=True)
            ds = (pr * (dp - delta)).astype(BF).reshape(BLK, HALF)
            dqT = nn(k2.T, ds)
            dk = of_head(nn(ds, q))
            dv = of_head(nn(pr.astype(BF).reshape(BLK, HALF), do))
            joined[rows, pl.ds(lane, 128)] = (dqT * factor).T.astype(BF)
            joined[rows, pl.ds(D + lane, 128)] = (dk * factor).astype(BF)
            joined[rows, pl.ds(2 * D + lane, 128)] = dv.astype(BF)

    def qkv_tiles(h):
        for j in (h, 2 + h, 4 + h):
            weight_tiles(tokT, joined, SB * j, None, (SENT.index(j), SENT.index(6 + j)))

    def middle():
        loads[5].wait()
        qkv_tiles(0)
        swap1(5).start()

    def first_sums():
        halves_in[0].wait()
        halves_in[2].wait()
        halves_in[1].wait()
        feed_far(0)
        step3(2)

    plan = {
        0: [lambda: small_take(0)],
        1: [lambda: step1(4), first_sums],
        5: [middle],
        6: [lambda: step1(5), lambda: small_take(1)],
        7: [lambda: feed_far(1), lambda: step3(3)],
        9: [lambda: step3(0)],
        11: [lambda: step2(4)],
    }

    @pl.loop(0, 12)
    def _(i):
        attend_back(i)
        for at_step, todo in plan.items():

            @pl.when(i == at_step)
            def _(todo=todo):
                for f in todo:
                    f()

    qkv_tiles(1)
    swap1(6).start()
    loads[6].wait()

    def input_rows(lo, hi):
        @pl.loop(lo, hi)
        def _(r):
            rows = pl.ds(pl.multiple_of(r * 512, 512), 512)
            igrad[rows, :] = sgrad[rows, :] + nt(joined[rows, :], wq[...].reshape(D, 3 * D))

    step3(1)
    step1(6)
    small_take(2)
    input_rows(0, 1)
    step4(2)
    step3(4)
    step2(5)
    step4(3)
    input_rows(1, 2)
    def turn_back():
        loads[7].wait()

        @pl.loop(0, 6)
        def _(t):
            b = t // 3
            hot = turning(jnp.where(b == 0, begin[0:1], begin[1:2]), -1).astype(BF)
            rows = pl.ds(pl.multiple_of(b * BLK, BLK), BLK)
            cols = pl.ds(pl.multiple_of(t % 3 * 256, 256), 256)
            cgrad[rows, cols] = nn(hot, ctx[rows, cols]).astype(BF)
            rest = igrad[rows, cols]
            value = None
            for _ in range(3):
                high = rest.astype(BF)
                rest = rest - high.astype(F32)
                one = nn(hot, high)
                value = one if value is None else value + one
            igrad[rows, cols] = value

    step2(6)
    step3(5)
    turn_back()
    igrad_copy = pltpu.make_async_copy(igrad, o_igrad, out_sem.at[0])
    igrad_copy.start()
    out_copy = pltpu.make_async_copy(cgrad, o_out, out_sem.at[1])
    out_copy.start()
    step4(0)
    step3(6)
    step4(1)
    step4(4)
    small_take(3)
    step4(5)
    step4(6)

    def deal(n, k, to, u):
        return remote(
            slots.at[to, :, n],
            gz.at[:, n, :, u],
            (a_send.at[n, k - 1], a_recv.at[n, k - 1]),
            zpeers[k - 1],
        )

    @pl.when(z != spare)
    def _():
        @pl.loop(0, 48)
        def _(s):
            slots[s // 12, s // 6 % 2, s // PER % PARTS, s % PER] = total[order[s]]

        for n in range(PARTS):
            for k in (1, 2, 3):
                deal(n, k, (z + k) % 4, unit(z)).start()
            gz[:, n, :, unit(z)] = slots[z, :, n]

    def piece(n, cc, yy, xx):
        return gfull.at[n, :, 4 * cc + 2 * yy + xx]

    others = ((y, 1 - x), (1 - y, x), (1 - y, 1 - x))

    def near(n, k):
        src = gz.at[1 - x if k in (0, 2) else x, n]
        sems = (f_send.at[n, k], f_recv.at[n, k])
        return remote(src, piece(n, c, y, x), sems, (xpeer, ypeer, diag, sib)[k])

    def onward(n, k):
        yy, xx = others[k]
        to = piece(n, c, yy, xx)
        return remote(to, to, (f_send.at[n, 4 + k], f_recv.at[n, 4 + k]), sib)

    def pass_on(n):
        for k in range(3):
            near(n, k).wait_recv()
            onward(n, k).start()

    for n in range(PARTS):
        for k in (1, 2, 3):
            sender = (z + 4 - k) % 4

            @pl.when(sender != spare)
            def _(n=n, k=k, sender=sender):
                deal(n, k, z, unit(sender)).wait_recv()

        for k in range(4):
            near(n, k).start()
        gfull[n, :, 4 * c + 2 * y + x] = gz[x, n]
        if n:
            pass_on(n - 1)
    small_take(4)
    pass_on(PARTS - 1)
    small_take(5)
    for n in range(PARTS):
        near(n, 3).wait_recv()
        for k in range(3):
            onward(n, k).wait_recv()
    full_copy = pltpu.make_async_copy(gfull, o_full, out_sem.at[2])
    full_copy.start()
    for n in range(PARTS):
        for k in range(4):
            near(n, k).wait_send()
        for k in range(3):
            onward(n, k).wait_send()

        @pl.when(z != spare)
        def _(n=n):
            for k in (1, 2, 3):
                deal(n, k, (z + k) % 4, unit(z)).wait_send()

    for g in range(len(GROUPS)):
        for k in (1, 2, 3):

            @pl.when((z + k) % 4 != spare)
            def _(g=g, k=k):
                swapz(g, k).wait_send()

    for k in range(8):
        small_copy(k).wait_send()
    for g in range(4, len(GROUPS)):
        for copy in [swap1(g)] + swap2(g) + swap3(g):
            copy.wait_send()
    for i in range(5):
        over_y(i).wait_send()
    for n in range(2):
        over_x(n).wait_send()
    igrad_copy.wait()
    out_copy.wait()
    full_copy.wait()


def run_backward(*arrays):
    sds = jax.ShapeDtypeStruct
    outs = (sds((ROWS, D), BF), sds((ROWS, D), F32), sds((PARTS, PER, 8, 3, 16, SB), BF), sds((16, D), F32))
    any_ = pl.BlockSpec(memory_space=pl.ANY)
    vm = pl.BlockSpec(memory_space=pltpu.VMEM)
    sm = pl.BlockSpec(memory_space=pltpu.SMEM)
    dma = pltpu.SemaphoreType.DMA
    return pl.pallas_call(
        backward_kernel,
        out_shape=outs,
        in_specs=[sm] * 3 + [vm] * 3 + [any_] * 10,
        out_specs=[any_] * 3 + [vm],
        scratch_shapes=[
            pltpu.VMEM((ROWS, 3 * D), BF),
            pltpu.VMEM((ROWS, D), BF),
            pltpu.VMEM((D, ROWS), BF),
            pltpu.VMEM((D, ROWS), BF),
            pltpu.VMEM((ROWS, D), F32),
            pltpu.VMEM((4, 192, 3 * D), BF),
            pltpu.VMEM((4, 192, D), BF),
            pltpu.VMEM((ROWS, D), BF),
            pltpu.VMEM((ROWS, D), BF),
            pltpu.VMEM((ROWS, D), F32),
            pltpu.VMEM((3, 8, 48, SB), BF),
            pltpu.VMEM((LEFT + 8, 2, 48, SB), BF),
            pltpu.VMEM((LEFT + 8, 2, 48, SB), BF),
            pltpu.VMEM((4, 8, 48, SB), BF),
            pltpu.VMEM((16, 2, 2, 2, 48, SB), BF),
            pltpu.VMEM((16, 2, 2, 48, SB), BF),
            pltpu.VMEM((16, 2, 48, SB), BF),
            pltpu.VMEM((16, 48, SB), BF),
            pltpu.VMEM((48, 3, 16, SB), BF),
            pltpu.VMEM((3, 48, 16, SB), BF),
            pltpu.VMEM((48, 16, SB), BF),
            pltpu.VMEM((4, 2, PARTS, PER, 16, SB), BF),
            pltpu.VMEM((2, PARTS, PER, 3, 16, SB), BF),
            pltpu.VMEM((PARTS, PER, 8, 3, 16, SB), BF),
            pltpu.VMEM((16, D), F32),
            pltpu.VMEM((8, D), F32),
            pltpu.VMEM((8, SB), F32),
            pltpu.VMEM((4, 8, SB), F32),
            pltpu.VMEM((16, D), F32),
            pltpu.VMEM((8, D), F32),
            pltpu.VMEM((8, SB), F32),
            pltpu.VMEM((8, SB), F32),
            pltpu.VMEM((2, HALF, 1), F32),
            pltpu.VMEM((2, 1, HALF), F32),
            pltpu.VMEM((1, D), F32),
            pltpu.VMEM((D, 1), F32),
            dma((8,)),
            dma((3,)),
            dma((7,)),
            dma((7,)),
            dma((7, 5)),
            dma((7, 5)),
            dma((7, 3)),
            dma((7, 3)),
            dma((PARTS, 3)),
            dma((PARTS, 3)),
            dma((PARTS, 7)),
            dma((PARTS, 7)),
            dma((8,)),
            dma((8,)),
            dma((3,)),
        ],
        compiler_params=pltpu.CompilerParams(
            collective_id=2, has_side_effects=True, vmem_limit_bytes=64 << 20
        ),
    )(*arrays)


def split(value):
    high = value.astype(BF)
    return high, (value - high.astype(F32)).astype(BF)


def update_kernel(
    small,
    gain,
    bias,
    full,
    master,
    left_stats,
    right_stats,
    left_root,
    right_root,
    out_in,
    igrad_in,
    o_grad,
    o_left,
    o_right,
    o_new,
    o_copy,
    o_unit,
    o_hidden,
    o_head,
    o_layer,
    o_norm,
    o_norm_new,
    o_out,
    o_igrad,
    turned,
    stage_out,
    stage_igrad,
    sem,
):
    slot = pl.program_id(0)
    moves_in = (
        pltpu.make_async_copy(out_in, stage_out, sem.at[0]),
        pltpu.make_async_copy(igrad_in, stage_igrad, sem.at[1]),
    )
    moves = (
        pltpu.make_async_copy(stage_out, o_out, sem.at[2]),
        pltpu.make_async_copy(stage_igrad, o_igrad, sem.at[3]),
    )

    @pl.when(slot == 0)
    def _():
        for move in moves_in:
            move.start()
        for i in range(4):
            o_unit[6 * i : 6 * i + 6, :] = many_rows(small[i : i + 1, :])
        o_hidden[...] = many_rows(small[6:7, :])
        o_norm[...] = small[4:6, :]
        rate = 0.2 / math.sqrt(ROWS * 32)
        o_norm_new[0:1, :] = one_row(gain[...]) - rate * small[4:5, :]
        o_norm_new[1:2, :] = one_row(bias[...]) - rate * small[5:6, :]
        lane = lax.broadcasted_iota(jnp.int32, (16, D), 1) // HD
        row = lax.broadcasted_iota(jnp.int32, (16, D), 0)
        by_head = jnp.sum(jnp.where(lane == row, small[9:10, :], 0.0), axis=1, keepdims=True)
        square = lax.broadcasted_iota(jnp.int32, (16, 128), 1)
        diagonal = square == lax.broadcasted_iota(jnp.int32, (16, 128), 0)
        o_head[...] = jnp.sum(jnp.where(diagonal, by_head, 0.0), axis=0, keepdims=True)[:, :12]
        pair = jnp.sum(small[7:9, :], axis=1, keepdims=True)
        first = lax.broadcasted_iota(jnp.int32, (1, 2), 1) == 0
        o_layer[...] = jnp.where(first, pair[0:1], pair[1:2])

    start = pl.multiple_of(lax.axis_index("mp") * 96, 16)
    own = full[0, pl.ds(start, 96), :]
    whole = full[0]
    o_grad[0] = own.astype(F32)
    o_left[0] = BETA * left_stats[0] + (1.0 - BETA) * nt(own, whole)
    turned[...] = whole.T
    root_high, root_low = split(left_root[0])
    stack = nn(jnp.concatenate([turned[pl.ds(start, 96), :], root_high, root_low], axis=0), whole)
    o_right[0] = BETA * right_stats[0] + (1.0 - BETA) * stack[:96]
    part_high, part_low = split(stack[96:192] + stack[192:])
    right_high, right_low = split(right_root[0])
    pair = nn(jnp.concatenate([part_high, part_low], axis=0), right_high)
    update = pair[:96] + pair[96:] + nn(part_high, right_low)
    new = master[0] - RATE * update
    o_new[0] = new
    o_copy[0] = new.astype(BF)

    @pl.when(slot == 2)
    def _():
        for first, then in zip(moves_in, moves):
            first.wait()
            then.start()

    @pl.when(slot == 5)
    def _():
        for move in moves:
            move.wait()


def run_update(*arrays):
    sds = jax.ShapeDtypeStruct
    whole = pl.BlockSpec((1, SB, SB), lambda s: (s, 0, 0))
    rows = pl.BlockSpec((1, 96, SB), lambda s: (s, 0, 0))
    any_ = pl.BlockSpec(memory_space=pl.ANY)

    def const(*shape):
        return pl.BlockSpec(shape, lambda s: (0, 0))

    flat = const(6, 128)
    return pl.pallas_call(
        update_kernel,
        grid=(6,),
        out_shape=(sds((6, 96, SB), F32),) * 4
        + (
            sds((6, 96, SB), BF),
            sds((24, 128), F32),
            sds((6, 128), F32),
            sds((1, 12), F32),
            sds((1, 2), F32),
            sds((2, D), F32),
            sds((2, D), F32),
            sds((ROWS, D), BF),
            sds((ROWS, D), F32),
        ),
        in_specs=[const(16, D), flat, flat, whole] + [rows] * 4 + [whole] + [any_] * 2,
        out_specs=[rows] * 5
        + [const(24, 128), flat, const(1, 12), const(1, 2), const(2, D), const(2, D), any_, any_],
        scratch_shapes=[
            pltpu.VMEM((SB, SB), BF),
            pltpu.VMEM((ROWS, D), BF),
            pltpu.VMEM((ROWS, D), F32),
            pltpu.SemaphoreType.DMA((4,)),
        ],
        compiler_params=pltpu.CompilerParams(vmem_limit_bytes=64 << 20),
    )(*arrays)


PLACE = tuple(FF_BLOCKS + SENT.index(b) for b in range(16)) + tuple(
    8 * (col // 2) + 4 * which + 2 * row + col % 2 for which in range(2) for row in range(2) for col in range(8)
)


def fast_body(
    tokens,
    segments,
    head_mask,
    unit_mask,
    hidden_mask,
    layer_gates,
    qkv_weight,
    out_weight,
    norm_gain,
    norm_bias,
    up_weight,
    down_weight,
    cotangent,
    owner_slot,
    master,
    left_stats,
    right_stats,
    left_root,
    right_root,
):
    gain = norm_gain.reshape(6, 128)
    bias = norm_bias.reshape(6, 128)
    (output, joined, ctx, ctxT, tokT, summed_grad, sums, far, wq, wo, lse, small) = run_forward(
        layer_gates,
        head_mask,
        tokens,
        cotangent,
        segments,
        unit_mask.reshape(24, 128),
        hidden_mask.reshape(6, 128),
        gain,
        bias,
        qkv_weight,
        out_weight,
        up_weight,
        down_weight,
    )
    slot_order = jnp.sum(
        jnp.where(owner_slot[None, :] == jnp.arange(48)[:, None], jnp.asarray(PLACE)[None, :], 0), axis=1
    )
    output, input_grad, full, small = run_backward(
        layer_gates,
        head_mask,
        slot_order,
        small,
        segments,
        lse,
        sums,
        far,
        joined,
        ctx,
        ctxT,
        tokT,
        summed_grad,
        wq,
        wo,
        output,
    )
    (
        owned,
        left_new,
        right_new,
        weight_new,
        weight_copy,
        unit_grad,
        hidden_grad,
        head_grad,
        layer_grad,
        norm_grad,
        norm_new,
        output,
        input_grad,
    ) = run_update(
        small,
        gain,
        bias,
        full.reshape(6, SB, SB),
        master,
        left_stats,
        right_stats,
        left_root,
        right_root,
        output,
        input_grad,
    )
    return (
        output,
        input_grad,
        head_grad.reshape(12),
        unit_grad.reshape(FF),
        hidden_grad.reshape(D),
        layer_grad.reshape(2),
        norm_grad,
        norm_new,
        owned,
        left_new,
        right_new,
        weight_new,
        weight_copy,
    )


def solution(mesh):
    return jax.shard_map(
        fast_body if dict(mesh.shape) == {"dp": 8, "mp": 4} else body,
        mesh=mesh,
        in_specs=(
            P(("dp", "mp"), None),
            P(("dp", "mp"), None),
            P(),
            P(),
            P(),
            P(),
            P("mp", None),
            P("mp", None),
            P(),
            P(),
            P(None, "mp"),
            P(None, "mp"),
            P(("dp", "mp"), None),
            P(),
            P("dp", "mp", None),
            P("dp", "mp", None),
            P("dp", "mp", None),
            P("dp", "mp", None),
            P("dp", None, None),
        ),
        out_specs=(
            P(("dp", "mp"), None),
            P(("dp", "mp"), None),
            P(),
            P(),
            P(),
            P(),
            P(),
            P(),
            P("dp", "mp", None),
            P("dp", "mp", None),
            P("dp", "mp", None),
            P("dp", "mp", None),
            P("dp", "mp", None),
        ),
        check_vma=False,
    )
```

```python
from functools import partial
import math

import jax
import jax.numpy as jnp
from jax import lax
from jax.experimental import pallas as pl
from jax.experimental.pallas import tpu as pltpu
from jax.sharding import PartitionSpec as P

FF = 3072
SB = 384


HIGH = lax.Precision.HIGHEST
BETA = 0.5
RATE = 0.5
EPS = 1e-12
MASKED = -1e30


def gelu_exact(values):
    return jax.nn.gelu(values, approximate=False)


def normalize(summed, gain_in, offset, hidden_gate):
    centre = summed - jnp.mean(summed, axis=-1, keepdims=True)
    spread = jnp.mean(centre * centre, axis=-1, keepdims=True)
    return (centre * lax.rsqrt(spread + EPS) * gain_in + offset) * hidden_gate


def split_heads(block_joined, head_count):
    pieces = block_joined.reshape(block_joined.shape[0], 3, head_count, -1)
    return (pieces[:, 0], pieces[:, 1], pieces[:, 2])


def masked_scores(queries, keys_in, labels, factor):
    scores = (
        jnp.einsum("qhd,khd->hqk", queries, keys_in, preferred_element_type=jnp.float32) * factor
    )
    allowed = labels[:, None] == labels[None, :]
    return jnp.where(allowed[None], scores, MASKED)


def attend_forward(packed, head_count, factor):
    block_joined, labels = packed
    queries, keys_in, values_in = split_heads(block_joined, head_count)
    scores = masked_scores(queries, keys_in, labels, factor)
    highest = jnp.max(scores, axis=-1, keepdims=True)
    raised = jnp.exp(scores - highest)
    totals = jnp.sum(raised, axis=-1, keepdims=True)
    weights_low = (raised / totals).astype(jnp.bfloat16)
    context = jnp.einsum("hqk,khd->qhd", weights_low, values_in, preferred_element_type=jnp.float32)
    return (context, (highest + jnp.log(totals))[:, :, 0])


def attend_backward(packed, head_count, factor):
    block_joined, log_totals, context_grad, labels = packed
    queries, keys_in, values_in = split_heads(block_joined, head_count)
    scores = masked_scores(queries, keys_in, labels, factor)
    weights_full = jnp.exp(scores - log_totals[:, :, None])
    weights_low = weights_full.astype(jnp.bfloat16)
    values_grad = jnp.einsum(
        "hqk,qhd->khd", weights_low, context_grad, preferred_element_type=jnp.float32
    )
    weights_grad = jnp.einsum(
        "qhd,khd->hqk", context_grad, values_in, preferred_element_type=jnp.float32
    )
    inner_sum = jnp.sum(weights_full * weights_grad, axis=-1, keepdims=True)
    scores_grad = (weights_full * (weights_grad - inner_sum)).astype(jnp.bfloat16)
    queries_grad = (
        jnp.einsum("hqk,khd->qhd", scores_grad, keys_in, preferred_element_type=jnp.float32)
        * factor
    )
    keys_grad = (
        jnp.einsum("hqk,qhd->khd", scores_grad, queries, preferred_element_type=jnp.float32)
        * factor
    )
    merged = jnp.concatenate([queries_grad, keys_grad, values_grad], axis=1)
    return merged.reshape(merged.shape[0], -1).astype(jnp.bfloat16)


def contract_rows(left, right):
    return lax.dot_general(
        left, right, (((0,), (0,)), ((), ())), preferred_element_type=jnp.float32
    )


def contract_cols(left, right):
    return lax.dot_general(
        left, right, (((1,), (1,)), ((), ())), preferred_element_type=jnp.float32
    )


def body(
    tokens,
    segments,
    head_mask,
    unit_mask,
    hidden_mask,
    layer_gates,
    qkv_weight,
    out_weight,
    norm_gain,
    norm_bias,
    up_weight,
    down_weight,
    cotangent,
    owner_slot,
    master,
    left_stats,
    right_stats,
    left_root,
    right_root,
):
    row_count = tokens.shape[0]
    width = tokens.shape[1]
    head_count = head_mask.shape[0]
    head_width = width // head_count
    block_rows = segments.shape[1]
    block_count = segments.shape[0]
    factor = 1.0 / math.sqrt(head_width)
    model_size = lax.axis_size("mp")
    share = FF // model_size
    part_rows = SB // model_size
    total_tokens = row_count * lax.axis_size("dp") * model_size
    head_gate = head_mask.astype(jnp.float32)
    unit_gate = unit_mask.astype(jnp.float32)
    hidden_gate = hidden_mask.astype(jnp.float32)
    inputs = tokens.astype(jnp.float32)
    back_full = cotangent.astype(jnp.float32)
    qkv_full, out_full, up_full, down_full = (
        lax.all_gather(qkv_weight, "mp", axis=0, tiled=True),
        lax.all_gather(out_weight, "mp", axis=0, tiled=True),
        lax.all_gather(up_weight, "mp", axis=1, tiled=True),
        lax.all_gather(down_weight, "mp", axis=1, tiled=True),
    )
    joined_qkv = jnp.dot(tokens, qkv_full, preferred_element_type=jnp.float32).astype(jnp.bfloat16)
    joined_blocks = joined_qkv.reshape(block_count, block_rows, 3 * width)
    context, log_totals = lax.map(
        partial(attend_forward, head_count=head_count, factor=factor), (joined_blocks, segments)
    )
    context = context.reshape(row_count, head_count, head_width)
    gated_low = (context * head_gate[None, :, None]).reshape(row_count, width).astype(jnp.bfloat16)
    attn_out = jnp.dot(gated_low, out_full, preferred_element_type=jnp.float32)
    summed = inputs + layer_gates[0] * attn_out
    hidden, norm_pull = jax.vjp(normalize, summed, norm_gain, norm_bias, hidden_gate)
    hidden_low = hidden.astype(jnp.bfloat16)
    pre_act = jnp.dot(hidden_low, up_full, preferred_element_type=jnp.float32)
    active, gelu_pull = jax.vjp(gelu_exact, pre_act)
    active_low = (active * unit_gate).astype(jnp.bfloat16)
    branch = contract_cols(active_low, down_full)
    output = (hidden + layer_gates[1] * branch).astype(jnp.bfloat16)
    back_rounded = (layer_gates[1] * back_full).astype(jnp.bfloat16)
    qkv_full, out_full, up_full, down_full = (
        lax.all_gather(qkv_weight, "mp", axis=0, tiled=True),
        lax.all_gather(out_weight, "mp", axis=0, tiled=True),
        lax.all_gather(up_weight, "mp", axis=1, tiled=True),
        lax.all_gather(down_weight, "mp", axis=1, tiled=True),
    )
    grad_active = jnp.dot(back_rounded, down_full, preferred_element_type=jnp.float32)
    unit_grad = jnp.sum(grad_active * active, axis=0)
    grad_inner = gelu_pull(grad_active * unit_gate)[0].astype(jnp.bfloat16)
    hidden_back = contract_cols(grad_inner, up_full)
    up_term = contract_rows(grad_inner, hidden_low)
    down_term = contract_rows(active_low, back_rounded)
    unit_local = (
        lax.psum_scatter(
            jnp.stack([up_term, down_term], axis=1).astype(jnp.bfloat16),
            "mp",
            scatter_dimension=0,
            tiled=True,
        )
        .astype(jnp.float32)
        .transpose(1, 2, 0)
    )
    summed_grad, gain_grad, bias_grad, mask_grad = norm_pull(back_full + hidden_back)
    layer_grad = jnp.stack([jnp.sum(summed_grad * attn_out), jnp.sum(back_full * branch)])
    out_back = (layer_gates[0] * summed_grad).astype(jnp.bfloat16)
    gated_grad = contract_cols(out_back, out_full).astype(jnp.bfloat16)
    gated_heads = gated_grad.reshape(row_count, head_count, head_width)
    head_grad = jnp.sum(context * gated_heads.astype(jnp.float32), axis=(0, 2))
    context_grad = gated_heads * head_mask.astype(jnp.bfloat16)[None, :, None]
    joined_grad = lax.map(
        partial(attend_backward, head_count=head_count, factor=factor),
        (
            joined_blocks,
            log_totals,
            context_grad.reshape(block_count, block_rows, head_count, head_width),
            segments,
        ),
    )
    joined_grad = joined_grad.reshape(row_count, 3 * width)
    input_grad = summed_grad + contract_cols(joined_grad, qkv_full)
    tiles = width // SB
    qkv_term = jnp.einsum(
        "tri,tcj->rcij",
        tokens.reshape(row_count, tiles, SB),
        joined_grad.reshape(row_count, 3 * tiles, SB),
        preferred_element_type=jnp.float32,
    )
    out_term = jnp.einsum(
        "tri,tcj->rcij",
        gated_low.reshape(row_count, tiles, SB),
        out_back.reshape(row_count, tiles, SB),
        preferred_element_type=jnp.float32,
    )
    attn_terms = jnp.concatenate(
        [
            qkv_term.reshape(-1, model_size, part_rows, SB),
            out_term.reshape(-1, model_size, part_rows, SB),
        ],
        axis=0,
    )
    attn_rows = (
        lax.psum_scatter(attn_terms.astype(jnp.bfloat16), "mp", scatter_dimension=1, tiled=True)
        .astype(jnp.float32)
        .reshape(-1, part_rows, SB)
    )
    unit_split = unit_local.reshape(2, tiles, model_size, part_rows, share)
    unit_rows = lax.all_to_all(
        unit_split.astype(jnp.bfloat16), "mp", split_axis=2, concat_axis=4, tiled=True
    ).astype(unit_split.dtype)
    unit_rows = (
        unit_rows.reshape(2, tiles, part_rows, FF // SB, SB)
        .transpose(0, 1, 3, 2, 4)
        .reshape(-1, part_rows, SB)
    )
    all_rows = jnp.concatenate([attn_rows, unit_rows], axis=0)
    slot_count = owner_slot.shape[0]
    pick = (owner_slot[None, :] == jnp.arange(slot_count)[:, None]).astype(jnp.bfloat16)
    flat_rows = all_rows.astype(jnp.bfloat16).reshape(slot_count, -1)
    slotted = jnp.dot(pick, flat_rows, preferred_element_type=jnp.float32).reshape(all_rows.shape)
    owned = lax.psum_scatter(
        slotted.astype(jnp.bfloat16), "dp", scatter_dimension=0, tiled=True
    ).astype(jnp.float32)
    full_grad = lax.all_gather(owned.astype(jnp.bfloat16), "mp", axis=1, tiled=True).astype(
        owned.dtype
    )
    row_start = lax.axis_index("mp") * part_rows
    columns = lax.dynamic_slice_in_dim(full_grad, row_start, part_rows, 2)
    left_new = BETA * left_stats + (1.0 - BETA) * jnp.einsum(
        "srj,skj->srk", owned, full_grad, precision=HIGH
    )
    right_new = BETA * right_stats + (1.0 - BETA) * jnp.einsum(
        "sjr,sjk->srk", columns, full_grad, precision=HIGH
    )
    left_part = jnp.einsum("sri,sij->srj", left_root, full_grad, precision=HIGH)
    update = jnp.einsum("srj,sjk->srk", left_part, right_root, precision=HIGH)
    weight_new = master - RATE * update
    norm_grad = jnp.stack([gain_grad, bias_grad])
    norm_grad, mask_grad, head_grad, layer_grad, unit_grad = lax.psum(
        (norm_grad, mask_grad, head_grad, layer_grad, unit_grad), ("dp", "mp")
    )
    norm_new = jnp.stack([norm_gain, norm_bias]) - 0.2 / math.sqrt(total_tokens) * norm_grad
    return (
        output,
        input_grad,
        head_grad,
        unit_grad,
        mask_grad,
        layer_grad,
        norm_grad,
        norm_new,
        owned,
        left_new,
        right_new,
        weight_new,
        weight_new.astype(jnp.bfloat16),
    )


F32 = jnp.float32
BF = jnp.bfloat16
MESH = pl.DeviceIdType.MESH
LOG2E = 1.4426950408889634
ROWS = 1024
D = 768
HD = 64
BLK = 512
NT_DIMS = (((1,), (1,)), ((), ()))
NN_DIMS = (((1,), (0,)), ((), ()))


def nn(left, right):
    return lax.dot_general(left, right, NN_DIMS, preferred_element_type=F32)


def nt(left, right):
    return lax.dot_general(left, right, NT_DIMS, preferred_element_type=F32)


def coords():
    d = lax.axis_index("dp")
    m = lax.axis_index("mp")
    return d // 2, d % 2, m // 2, m % 2


def at(z, x, y, c):
    return (2 * z + x, 2 * y + c)


def gelu_parts(x):
    ax = jnp.abs(x)
    e = jnp.exp2(x * x * (-0.5 * LOG2E))
    t = 1.0 / (1.0 + (0.3275911 * math.sqrt(0.5)) * ax)
    poly = t * (
        0.5 * 0.254829592
        + t
        * (
            -0.5 * 0.284496736
            + t * (0.5 * 1.421413741 + t * (-0.5 * 1.453152027 + t * (0.5 * 1.061405429)))
        )
    )
    tail = poly * e
    cdf = jnp.where(x < 0, tail, 1.0 - tail)
    active = x * cdf
    return active, cdf + x * (e * (1.0 / math.sqrt(2.0 * math.pi)))


def colsum(v):
    return jnp.sum(v, axis=0, keepdims=True)


def row_norm(summed):
    centre = summed - jnp.mean(summed, axis=-1, keepdims=True)
    spread = jnp.mean(centre * centre, axis=-1, keepdims=True)
    inv = lax.rsqrt(spread + EPS)
    return centre * inv, inv


def one_row(v):
    return jnp.concatenate([v[i : i + 1] for i in range(v.shape[0])], axis=1)


def many_rows(v):
    return jnp.concatenate([v[:, 128 * i : 128 * i + 128] for i in range(v.shape[1] // 128)], axis=0)


def head_lanes(heads):
    which = lax.broadcasted_iota(jnp.int32, (1, D), 1) // HD
    row = jnp.zeros((1, D), F32)
    for h in range(12):
        row = row + jnp.where(which == h, heads[h].astype(F32), 0.0)
    return row


HALF = BLK // 2


def first_rows(segs):
    values = segs[...].astype(F32)
    begin = jnp.zeros((2, 1), F32)
    for item in range(6):
        count = jnp.sum(jnp.where(values == item, 1.0, 0.0), axis=1, keepdims=True)
        before = jnp.sum(jnp.where(values < item, 1.0, 0.0), axis=1, keepdims=True)
        begin = begin + jnp.where(count == HALF, before, 0.0)
    return begin


def turning(begin, sign):
    row = lax.broadcasted_iota(jnp.int32, (BLK, BLK), 0).astype(F32)
    col = lax.broadcasted_iota(jnp.int32, (BLK, BLK), 1).astype(F32)
    off = sign * (col - row) - begin
    return jnp.where((off == 0) | (off == -BLK), 1.0, 0.0)


def turn_labels(segs, begin, segcol, segrow):
    for b in range(2):
        hot = turning(begin[b : b + 1], 1)[HALF:, :]
        column = jnp.sum(hot * segs[b : b + 1, :].astype(F32), axis=1, keepdims=True)
        segcol[b] = column
        segrow[b] = jnp.broadcast_to(column, (HALF, 128)).T[0:1, :]


MOVED = (8, 8, 4)
LEFT = 8 - MOVED[2]
NPIECE = 8


def forward_kernel(
    gates,
    heads,
    tokens_in,
    cot_in,
    segs,
    units,
    hidden,
    gain_in,
    bias_in,
    qkv_in,
    out_in,
    up_in,
    down_in,
    o_out,
    o_joined,
    o_ctx,
    o_ctxT,
    o_tokT,
    o_sgrad,
    o_sums,
    o_far,
    o_wq,
    o_wo,
    lse,
    small,
    wq,
    wo,
    wu,
    wd,
    joined,
    ctx,
    ctxT,
    tokT,
    attn,
    blow,
    bT,
    branch,
    hback,
    grads,
    got1,
    got2,
    tokens,
    cot,
    segcol,
    segrow,
    ugate,
    vec,
    send_sem,
    recv_sem,
    loc_sem,
    out_sem,
    c_send,
    c_recv,
    x_send,
    x_recv,
):
    z, x, y, c = coords()
    hT = tokT
    hlow = ctx
    act, inner, outv = (joined.at[:, pl.ds(D * i, D)] for i in range(3))
    m = 2 * y + c
    ms = 2 * y + 1 - c
    my = 2 * (1 - y) + c
    mys = 2 * (1 - y) + 1 - c
    sib = at(z, x, y, 1 - c)
    ypeer = at(z, x, 1 - y, c)
    xpeer = at(z, 1 - x, y, c)
    zpeer = at(z + 1 - 2 * (z % 2), x, y, c)
    g0 = gates[0]
    g1 = gates[1]

    barrier = pltpu.get_barrier_semaphore()
    for peer in (sib, ypeer, xpeer, zpeer):
        pl.semaphore_signal(barrier, inc=1, device_id=peer, device_id_type=MESH)
    loads = (
        pltpu.make_async_copy(tokens_in, blow, out_sem.at[6]),
        pltpu.make_async_copy(cot_in, ctx, out_sem.at[7]),
    )
    for copy in loads:
        copy.start()
    begin = first_rows(segs)
    pl.semaphore_wait(barrier, 4)

    def spot(j):
        if j < 3:
            return 0, 192, pl.ds(768 * j, 768)
        if j == 3:
            return 1, 192, slice(None)
        return 2 + (j - 4) // 2, 768, pl.ds(384 * (j % 2), 384)

    def full(j, i, h=None):
        which, n, cols = spot(j)
        ref = (wq, wo, wu, wd)[which]
        if h is None:
            return ref.at[i, :, cols]
        return ref.at[i, pl.ds(pl.multiple_of(h * (n // 2), 16), n // 2), cols]

    def own(j, h=None):
        which, n, cols = spot(j)
        ref = (qkv_in, out_in, up_in, down_in)[which]
        if h is None:
            return ref.at[:, cols]
        return ref.at[pl.ds(pl.multiple_of(h * (n // 2), 16), n // 2), cols]

    def remote(src, dst, j, k, dev):
        return pltpu.make_async_remote_copy(
            src_ref=src,
            dst_ref=dst,
            send_sem=send_sem.at[j, k],
            recv_sem=recv_sem.at[j, k],
            device_id=dev,
            device_id_type=MESH,
        )

    def s1(j):
        return remote(own(j), full(j, m), j, 0, sib)

    def half_of(j):
        return (x, xpeer) if j < 4 else (z % 2, zpeer)

    def s2(j):
        h, _ = half_of(j)
        return remote(own(j, h), full(j, m, h), j, 1, ypeer)

    def s3(j):
        h, peer = half_of(j)
        return remote(full(j, my, h), full(j, my, h), j, 2, peer)

    def s4(j):
        h, _ = half_of(j)
        return remote(full(j, my, h), full(j, my, h), j, 3, sib)

    def s5(j):
        h, _ = half_of(j)
        return remote(full(j, my, 1 - h), full(j, my, 1 - h), j, 4, sib)

    def local(j):
        return pltpu.make_async_copy(own(j), full(j, m), loc_sem.at[j])

    def first(j):
        s2(j).start()
        s1(j).start()
        local(j).start()

    def second(j):
        s2(j).wait_recv()
        s3(j).start()
        s4(j).start()

    def third(j):
        s3(j).wait_recv()
        s5(j).start()

    def finish_near(j):
        local(j).wait()
        s1(j).wait_recv()

    def finish_far(j):
        s4(j).wait_recv()
        s5(j).wait_recv()

    def finish_sends(j):
        for s in (s1, s2, s3, s4, s5):
            s(j).wait_send()

    for j in range(3):
        first(j)

    turn_labels(segs, begin, segcol, segrow)
    for copy in loads:
        copy.wait()
    def turn(src, dst):
        @pl.loop(0, 2)
        def _(b):
            hot = turning(jnp.where(b == 0, begin[0:1], begin[1:2]), 1).astype(BF)
            rows = pl.ds(pl.multiple_of(b * BLK, BLK), BLK)
            dst[rows, :] = nn(hot, src[rows, :]).astype(BF)

    def backs(lo, hi):
        @pl.loop(lo, hi)
        def _(r):
            rows = pl.ds(pl.multiple_of(r * 256, 256), 256)
            low = (g1 * cot[rows, :].astype(F32)).astype(BF)
            blow[rows, :] = low
            bT[:, rows] = low.T

    turn(blow, tokens)

    near_sum = (attn, branch, hback)

    def project(j, near):
        yy = y if near else 1 - y

        @pl.loop(0, 2)
        def _(r):
            rows = pl.ds(pl.multiple_of(r * 512, 512), 512)
            w = wq[pl.ds(2 * yy, 2), :, pl.ds(768 * j, 768)].reshape(SB, D)
            one = nn(tokens[rows, pl.ds(pl.multiple_of(SB * yy, 128), SB)], w)
            if near:
                near_sum[j][rows, :] = one
            else:
                joined[rows, pl.ds(768 * j, 768)] = (near_sum[j][rows, :] + one).astype(BF)

    for j in range(3):
        finish_near(j)
    project(0, True)
    second(0)
    turn(ctx, cot)
    for i in range(4):
        ugate[i] = one_row(units[6 * i : 6 * i + 6, :].astype(F32))
    vec[0:1, :] = head_lanes(heads)
    vec[1:2, :] = one_row(hidden[...].astype(F32))
    vec[2:3, :] = one_row(gain_in[...])
    vec[3:4, :] = one_row(bias_in[...])
    hgate, mgate, gain, bias = (vec.at[i : i + 1] for i in range(4))
    project(1, True)
    second(1)
    project(2, True)
    third(0)
    backs(0, 2)
    second(2)
    for j in range(3, NPIECE):
        first(j)
    tokT[...] = tokens[...].T
    tok_copy = pltpu.make_async_copy(tokT, o_tokT, out_sem.at[0])
    tok_copy.start()
    third(1)
    backs(2, 4)
    finish_far(0)
    project(0, False)
    third(2)
    finish_far(1)
    project(1, False)
    finish_far(2)
    wq_copy = pltpu.make_async_copy(wq, o_wq, out_sem.at[1])
    wq_copy.start()
    project(2, False)
    joined_copy = pltpu.make_async_copy(joined, o_joined, out_sem.at[2])
    joined_copy.start()

    scale = LOG2E / math.sqrt(HD)
    half_iota = lax.broadcasted_iota(jnp.int32, (1, 128), 1) // HD
    halves = [(half_iota == e).astype(F32).astype(BF) for e in range(2)]

    def by_head(v):
        return jnp.concatenate([v * halves[0], v * halves[1]], axis=0)

    def attend(i):
        b = i // 6
        p = i % 6
        lane = pl.multiple_of(p * 128, 128)
        for part in range(2):
            rows = pl.ds(pl.multiple_of(b * BLK + part * HALF, HALF), HALF)
            q = joined[rows, pl.ds(lane, 128)]
            k = joined[rows, pl.ds(D + lane, 128)]
            v = joined[rows, pl.ds(2 * D + lane, 128)]
            s = nt(by_head(k), q).reshape(2, HALF, HALF) * scale
            if part:
                s = jnp.where(segcol[b] == segrow[b], s, MASKED)
            top = jnp.max(s, axis=1, keepdims=True)
            pr = jnp.exp2(s - top)
            tot = jnp.sum(pr, axis=1, keepdims=True)
            low = (pr * (1.0 / tot)).astype(BF).reshape(BLK, HALF)
            lse[pl.ds(2 * i, 2), :, part * HALF : part * HALF + HALF] = top + jnp.log(tot) * LOG2E
            total = nn(by_head(v).T, low)
            ctxT[pl.ds(lane, 128), rows] = total.astype(BF)
            ctx[rows, pl.ds(lane, 128)] = total.T.astype(BF)

    plan = {
        0: [lambda: second(3)],
        5: [lambda: second(4), lambda: third(3)],
    }

    @pl.loop(0, 12)
    def _(i):
        attend(i)
        for at_step, todo in plan.items():

            @pl.when(i == at_step)
            def _(todo=todo):
                for f in todo:
                    f()

    ctx_copy = pltpu.make_async_copy(ctx, o_ctx, out_sem.at[3])
    ctx_copy.start()
    ctxT_copy = pltpu.make_async_copy(ctxT, o_ctxT, out_sem.at[4])
    ctxT_copy.start()
    finish_near(3)
    finish_far(3)
    wo_copy = pltpu.make_async_copy(wo, o_wo, out_sem.at[5])
    wo_copy.start()

    joined_copy.wait()
    tok_copy.wait()
    ctx_copy.wait()

    @pl.loop(0, 4)
    def _(r):
        rows = pl.ds(pl.multiple_of(r * 256, 256), 256)
        gated = ctx[rows, :] * hgate[...].astype(BF)
        a = nn(gated, wo[...].reshape(D, D))
        attn[rows, :] = a
        normed, _ = row_norm(tokens[rows, :].astype(F32) + g0 * a)
        low = ((normed * gain[...] + bias[...]) * mgate[...]).astype(BF)
        hlow[rows, :] = low
        hT[:, rows] = low.T

    small[...] = jnp.zeros_like(small)

    def feed(f, between={}):
        u = 2 * ((y + f // 2) % 2) + f % 2
        begin = f == 0
        w_up = wu.at[u]
        w_down = wd.at[u]

        @pl.loop(0, 2)
        def _(r):
            rows = pl.ds(pl.multiple_of(r * 512, 512), 512)
            pre = nn(hlow[rows, :], w_up[...])
            back = nn(blow[rows, :], w_down[...])
            active, slope = gelu_parts(pre)
            gate = ugate[u]
            small[pl.ds(u, 1), :] += colsum(back * active)
            a_low = (active * gate).astype(BF)
            i_low = (back * gate * slope).astype(BF)
            act[rows, :] = a_low
            inner[rows, :] = i_low
            up_part = nt(a_low, w_down[...])
            back_part = nt(i_low, w_up[...])
            if begin:
                branch[rows, :] = up_part
                hback[rows, :] = back_part
            else:
                branch[rows, :] += up_part
                hback[rows, :] += back_part
            for at_row, todo in between.items():
                pl.when(r == at_row)(todo)

        for which, (left, right) in enumerate(((hT, inner), (bT, act))):

            @pl.loop(0, 2)
            def _(r, which=which, left=left, right=right):
                rr = pl.ds(pl.multiple_of(r * SB, 128), SB)
                g = nn(left[rr, :], right[...]).astype(BF)
                for j in range(2):
                    grads[f, 4 * which + 2 * r + j] = g[:, SB * j : SB * j + SB].reshape(
                        2, 2, 2, 48, SB
                    )

    def swap1(f):
        return pltpu.make_async_remote_copy(
            src_ref=grads.at[f, :, 1 - c],
            dst_ref=got1.at[f],
            send_sem=c_send.at[f],
            recv_sem=c_recv.at[f],
            device_id=sib,
            device_id_type=MESH,
        )

    def swap2(f):
        return pltpu.make_async_remote_copy(
            src_ref=grads.at[f, pl.ds(0, MOVED[f]), c, :, 1 - x],
            dst_ref=got2.at[f, pl.ds(0, MOVED[f])],
            send_sem=x_send.at[f],
            recv_sem=x_recv.at[f],
            device_id=xpeer,
            device_id_type=MESH,
        )

    def plus(left, right):
        return (left.astype(F32) + right.astype(F32)).astype(BF)

    def sum1(f):
        swap1(f).wait_recv()

        @pl.loop(0, 8)
        def _(i):
            grads[f, i, c] = plus(grads[f, i, c], got1[f, i])

    for j in range(4, NPIECE):
        finish_near(j)

    def spread(f):
        sum1(f)
        swap2(f).start()

    def finish(f):
        swap2(f).wait_recv()

        @pl.loop(0, MOVED[f])
        def _(i):
            for yy in range(2):
                grads[f, i, c, yy, x] = plus(grads[f, i, c, yy, x], got2[f, i, yy])

        sums_copy(f).start()

    def sums_copy(f):
        return pltpu.make_async_copy(
            grads.at[f, pl.ds(0, MOVED[f]), c, :, x],
            o_sums.at[f, pl.ds(0, MOVED[f])],
            out_sem.at[9 + f],
        )

    def in_turn(*steps):
        def run():
            for step, i in steps:
                step(i)

        return run

    feed(0, {0: in_turn((second, 5), (third, 4)), 1: in_turn((second, 6))})
    swap1(0).start()
    feed(1, {0: in_turn((second, 7), (third, 5), (spread, 0)), 1: in_turn((third, 6))})
    swap1(1).start()
    third(7)
    for j in range(4, NPIECE):
        finish_far(j)
    feed(2, {0: in_turn((spread, 1))})
    swap1(2).start()
    feed(3, {0: in_turn((spread, 2)), 1: in_turn((finish, 0))})
    swap1(3).start()

    lane = lax.broadcasted_iota(jnp.int32, (1, D), 1)

    @pl.loop(0, 4)
    def _(r):
        rows = pl.ds(pl.multiple_of(r * 256, 256), 256)
        a = attn[rows, :]
        normed, inv = row_norm(tokens[rows, :].astype(F32) + g0 * a)
        plain = normed * gain[...] + bias[...]
        back = cot[rows, :].astype(F32)
        br = branch[rows, :]
        outv[rows, :] = (plain * mgate[...] + g1 * br).astype(BF)
        total = back + hback[rows, :]
        masked = total * mgate[...]
        small[4:5, :] += colsum(masked * normed)
        small[5:6, :] += colsum(masked)
        small[6:7, :] += colsum(total * plain)
        n = masked * gain[...]
        grad = (
            n
            - jnp.mean(n, axis=-1, keepdims=True)
            - normed * jnp.mean(n * normed, axis=-1, keepdims=True)
        ) * inv
        hback[rows, :] = grad
        small[7:8, :] += colsum(grad * a)
        small[8:9, :] += colsum(back * br)

    out_copy = pltpu.make_async_copy(outv, o_out, out_sem.at[6])
    out_copy.start()
    sgrad_copy = pltpu.make_async_copy(hback, o_sgrad, out_sem.at[7])
    sgrad_copy.start()
    sum1(3)
    grad_copies = [
        pltpu.make_async_copy(
            grads.at[2, pl.ds(MOVED[2], LEFT), c], o_far.at[pl.ds(0, LEFT)], out_sem.at[8]
        ),
        pltpu.make_async_copy(grads.at[3, :, c], o_far.at[pl.ds(LEFT, 8)], out_sem.at[12]),
    ]
    for copy in grad_copies:
        copy.start()
    finish(1)
    finish(2)
    for f in range(3):
        sums_copy(f).wait()
    for copy in grad_copies:
        copy.wait()
    for copy in (wq_copy, ctxT_copy, wo_copy, out_copy, sgrad_copy):
        copy.wait()
    for f in range(4):
        swap1(f).wait_send()
    for f in range(3):
        swap2(f).wait_send()
    for j in range(NPIECE):
        finish_sends(j)


def run_forward(*arrays):
    sds = jax.ShapeDtypeStruct
    outs = (
        sds((ROWS, D), BF),
        sds((ROWS, 3 * D), BF),
        sds((ROWS, D), BF),
        sds((D, ROWS), BF),
        sds((D, ROWS), BF),
        sds((ROWS, D), F32),
        sds((3, 8, 2, 48, SB), BF),
        sds((LEFT + 8, 2, 2, 48, SB), BF),
        sds((4, 192, 3 * D), BF),
        sds((4, 192, D), BF),
        sds((24, 1, BLK), F32),
        sds((16, D), F32),
    )
    any_ = pl.BlockSpec(memory_space=pl.ANY)
    vm = pl.BlockSpec(memory_space=pltpu.VMEM)
    sm = pl.BlockSpec(memory_space=pltpu.SMEM)
    return pl.pallas_call(
        forward_kernel,
        out_shape=outs,
        in_specs=[sm] * 2 + [any_] * 2 + [vm] * 5 + [any_] * 4,
        out_specs=[any_] * 10 + [vm] * 2,
        scratch_shapes=[
            pltpu.VMEM((4, 192, 3 * D), BF),
            pltpu.VMEM((4, 192, D), BF),
            pltpu.VMEM((4, D, D), BF),
            pltpu.VMEM((4, D, D), BF),
            pltpu.VMEM((ROWS, 3 * D), BF),
            pltpu.VMEM((ROWS, D), BF),
            pltpu.VMEM((D, ROWS), BF),
            pltpu.VMEM((D, ROWS), BF),
            pltpu.VMEM((ROWS, D), F32),
            pltpu.VMEM((ROWS, D), BF),
            pltpu.VMEM((D, ROWS), BF),
            pltpu.VMEM((ROWS, D), F32),
            pltpu.VMEM((ROWS, D), F32),
            pltpu.VMEM((4, 8, 2, 2, 2, 48, SB), BF),
            pltpu.VMEM((4, 8, 2, 2, 48, SB), BF),
            pltpu.VMEM((3, 8, 2, 48, SB), BF),
            pltpu.VMEM((ROWS, D), BF),
            pltpu.VMEM((ROWS, D), BF),
            pltpu.VMEM((2, HALF, 1), F32),
            pltpu.VMEM((2, 1, HALF), F32),
            pltpu.VMEM((4, 1, D), F32),
            pltpu.VMEM((8, D), F32),
            pltpu.SemaphoreType.DMA((NPIECE, 5)),
            pltpu.SemaphoreType.DMA((NPIECE, 5)),
            pltpu.SemaphoreType.DMA((NPIECE,)),
            pltpu.SemaphoreType.DMA((13,)),
            pltpu.SemaphoreType.DMA((4,)),
            pltpu.SemaphoreType.DMA((4,)),
            pltpu.SemaphoreType.DMA((3,)),
            pltpu.SemaphoreType.DMA((3,)),
        ],
        compiler_params=pltpu.CompilerParams(
            collective_id=1, has_side_effects=True, vmem_limit_bytes=64 << 20
        ),
    )(*arrays)


SENT = (12, 13, 14, 15, 0, 2, 4, 6, 8, 10, 1, 3, 5, 7, 9, 11)
GROUPS = (None,) * 4 + ((32, 4, 2), (36, 6, 3), (42, 6, 3))
FF_BLOCKS = 32
PARTS = 3
PER = 6 // PARTS


def backward_kernel(
    gates,
    heads,
    order,
    small_in,
    segs,
    lse,
    sums_in,
    far_in,
    joined_in,
    ctx_in,
    ctxT_in,
    tokT_in,
    sgrad_in,
    wq_in,
    wo_in,
    out_in,
    o_out,
    o_igrad,
    o_full,
    small_out,
    joined,
    ctx,
    ctxT,
    tokT,
    sgrad,
    wq,
    wo,
    outb,
    cgrad,
    igrad,
    ownv,
    farv,
    gotx,
    goty,
    ga,
    got1,
    got2,
    got3,
    part,
    gotz,
    total,
    slots,
    gz,
    gfull,
    sm_all,
    sm_rows,
    sm_lanes,
    sm_z,
    sm_back,
    sm_got1,
    sm_got2,
    sm_got3,
    segcol,
    segrow,
    hrow,
    hcol,
    load_sem,
    half_sem,
    ff_send,
    ff_recv,
    send_sem,
    recv_sem,
    z_send,
    z_recv,
    a_send,
    a_recv,
    f_send,
    f_recv,
    s_send,
    s_recv,
    out_sem,
):
    z, x, y, c = coords()
    g0 = gates[0]
    sib = at(z, x, y, 1 - c)
    ypeer = at(z, x, 1 - y, c)
    xpeer = at(z, 1 - x, y, c)
    diag = at(z, 1 - x, 1 - y, c)
    zpeers = [at((z + k) % 4, x, y, c) for k in (1, 2, 3)]

    loads = [
        pltpu.make_async_copy(src, dst, load_sem.at[i])
        for i, (src, dst) in enumerate(
            (
                (sgrad_in, sgrad),
                (wo_in, wo),
                (ctx_in, ctx),
                (ctxT_in, ctxT),
                (joined_in, joined),
                (tokT_in, tokT),
                (wq_in, wq),
                (out_in, ctx),
            )
        )
    ]
    halves_in = [
        pltpu.make_async_copy(sums_in.at[pl.ds(0, 2), :, y], ownv.at[pl.ds(0, 2)], half_sem.at[0]),
        pltpu.make_async_copy(far_in.at[:, :, x], farv, half_sem.at[1]),
        pltpu.make_async_copy(
            sums_in.at[2, pl.ds(0, MOVED[2]), y], ownv.at[2, pl.ds(0, MOVED[2])], half_sem.at[2]
        ),
    ]
    for copy in loads[:4]:
        copy.start()

    barrier = pltpu.get_barrier_semaphore()
    for peer in [sib, ypeer, xpeer, diag] + zpeers:
        pl.semaphore_signal(barrier, inc=1, device_id=peer, device_id_type=MESH)
    pl.semaphore_wait(barrier, 7)

    def remote(src, dst, sems, dev):
        return pltpu.make_async_remote_copy(
            src_ref=src,
            dst_ref=dst,
            send_sem=sems[0],
            recv_sem=sems[1],
            device_id=dev,
            device_id_type=MESH,
        )

    def pair(g, k):
        return send_sem.at[g, k], recv_sem.at[g, k]

    def first_block(f):
        return 8 * (2 * ((y + f // 2) % 2) + f % 2)

    def span(g):
        return (first_block(g), 8) if g < 4 else GROUPS[g][:2]

    def over_y(i):
        src, to = (
            (lambda: sums_in.at[0, :, 1 - y], goty.at[2]),
            (lambda: sums_in.at[1, :, 1 - y], goty.at[3]),
            (lambda: sums_in.at[2, pl.ds(0, MOVED[2]), 1 - y], goty.at[0, pl.ds(0, MOVED[2])]),
            (lambda: farv.at[pl.ds(0, LEFT), 1 - y], goty.at[0, pl.ds(MOVED[2], LEFT)]),
            (lambda: farv.at[pl.ds(LEFT, 8), 1 - y], goty.at[1]),
        )[i]
        return remote(src(), to, (ff_send.at[i], ff_recv.at[i]), ypeer)

    def over_x(i):
        part = (pl.ds(0, LEFT), pl.ds(LEFT, 8))[i]
        return remote(
            far_in.at[part, :, 1 - x], gotx.at[part], (ff_send.at[5 + i], ff_recv.at[5 + i]), xpeer
        )

    def mine(g, first, count):
        return ga.at[pl.ds(GROUPS[g][0] + first - FF_BLOCKS, count), c]

    def swap1(g):
        base, count, _ = GROUPS[g]
        src = ga.at[pl.ds(base - FF_BLOCKS, count), 1 - c]
        return remote(src, got1.at[pl.ds(base - FF_BLOCKS, count)], pair(g, 0), sib)

    def swap2(g):
        base, count, n = GROUPS[g]
        rest = count - n
        to = base - FF_BLOCKS
        found = [
            remote(mine(g, n, rest).at[:, :, 1 - x], got2.at[pl.ds(to + n, rest)], pair(g, 2), xpeer)
        ]
        if n:
            found.append(remote(mine(g, 0, n).at[:, 1 - y], got2.at[pl.ds(to, n)], pair(g, 1), ypeer))
        return found

    def swap3(g):
        base, count, n = GROUPS[g]
        rest = count - n
        to = base - FF_BLOCKS
        found = [
            remote(mine(g, n, rest).at[:, 1 - y, x], got3.at[pl.ds(to + n, rest)], pair(g, 4), ypeer)
        ]
        if n:
            found.append(remote(mine(g, 0, n).at[:, y, 1 - x], got3.at[pl.ds(to, n)], pair(g, 3), xpeer))
        return found

    def plus(left, right):
        return (left.astype(F32) + right.astype(F32)).astype(BF)

    def step1(g):
        base, count, _ = GROUPS[g]
        swap1(g).wait_recv()

        @pl.loop(base - FF_BLOCKS, base - FF_BLOCKS + count)
        def _(i):
            ga[i, c] = plus(ga[i, c], got1[i])

        for copy in swap2(g):
            copy.start()

    def step2(g):
        base, count, n = GROUPS[g]
        for copy in swap2(g):
            copy.wait_recv()

        @pl.loop(base - FF_BLOCKS, base - FF_BLOCKS + n)
        def _(i):
            ga[i, c, y] = plus(ga[i, c, y], got2[i])

        @pl.loop(base - FF_BLOCKS + n, base - FF_BLOCKS + count)
        def _(i):
            for yy in range(2):
                ga[i, c, yy, x] = plus(ga[i, c, yy, x], got2[i, yy])

        for copy in swap3(g):
            copy.start()

    def feed_far(n):
        over_x(n).wait_recv()

        @pl.loop(*((0, LEFT), (LEFT, LEFT + 8))[n])
        def _(i):
            farv[i] = plus(farv[i], gotx[i])

        over_y(3 + n).start()

    spare = 1 + c

    def unit(zz):
        return zz - (zz + 3 - spare) // 4

    def swapz(g, k):
        base, count = span(g)
        return remote(
            part.at[pl.ds(base, count), unit((z + k) % 4)],
            gotz.at[k - 1, pl.ds(base, count)],
            (z_send.at[g, k - 1], z_recv.at[g, k - 1]),
            zpeers[k - 1],
        )

    def step3(g):
        base, count = span(g)
        if g < 4:
            for i in ((2, 3), (4,), (0,), (1,))[g]:
                over_y(i).wait_recv()
        else:
            for copy in swap3(g):
                copy.wait_recv()
        moved = (8, 8, MOVED[2], 0)[g] if g < 4 else 0

        if moved:

            @pl.loop(0, moved)
            def _(i):
                part[base + i] = plus(ownv[g, i], goty[g, i]).reshape(3, 16, SB)

        @pl.loop(moved, count)
        def _(i):
            if g < 4:
                value = plus(farv[i - (8 - LEFT) if g == 2 else LEFT + i, y], goty[g, i])
            else:
                value = plus(ga[base - FF_BLOCKS + i, c, y, x], got3[base - FF_BLOCKS + i])
            part[base + i] = value.reshape(3, 16, SB)

        for k in (1, 2, 3):

            @pl.when((z + k) % 4 != spare)
            def _(k=k):
                swapz(g, k).start()

    def step4(g):
        base, count = span(g)

        @pl.when(z != spare)
        def _():
            for k in (1, 2, 3):
                swapz(g, k).wait_recv()

            @pl.loop(0, count)
            def _(i):
                value = part[base + i, unit(z)].astype(F32)
                for k in range(3):
                    value = value + gotz[k, base + i].astype(F32)
                total[base + i] = value.astype(BF)

    def small_copy(k):
        rows = pl.ds(pl.multiple_of(8 * c, 8), 8)
        away = pl.ds(pl.multiple_of(8 * (1 - c), 8), 8)
        lanes = pl.ds(pl.multiple_of(SB * y, 128), SB)
        other = pl.ds(pl.multiple_of(SB * (1 - y), 128), SB)
        src, dst, dev = (
            (sm_all.at[away], sm_got1, sib),
            (sm_rows.at[:, other], sm_got2, ypeer),
            (sm_lanes, sm_got3, xpeer),
            (sm_z.at[z], sm_z.at[z], zpeers[0]),
            (sm_z.at[z], sm_z.at[z], zpeers[1]),
            (sm_z.at[z], sm_z.at[z], zpeers[2]),
            (sm_back.at[rows, lanes], sm_back.at[rows, lanes], ypeer),
            (sm_back.at[rows], sm_back.at[rows], sib),
        )[k]
        return remote(src, dst, (s_send.at[k], s_recv.at[k]), dev)

    def small_take(stage):
        rows = pl.ds(pl.multiple_of(8 * c, 8), 8)
        away = pl.ds(pl.multiple_of(8 * (1 - c), 8), 8)
        lanes = pl.ds(pl.multiple_of(SB * y, 128), SB)
        other = pl.ds(pl.multiple_of(SB * (1 - y), 128), SB)
        if stage == 0:
            small_copy(0).wait_recv()
            sm_rows[...] = sm_all[rows, :] + sm_got1[...]
            small_copy(1).start()
        elif stage == 1:
            small_copy(1).wait_recv()
            sm_lanes[...] = sm_rows[:, lanes] + sm_got2[...]
            small_copy(2).start()
        elif stage == 2:
            small_copy(2).wait_recv()
            sm_z[z] = sm_lanes[...] + sm_got3[...]
            for k in (3, 4, 5):
                small_copy(k).start()
        elif stage == 3:
            for k in (1, 2, 3):
                sender = (z + 4 - k) % 4
                remote(
                    sm_z.at[sender], sm_z.at[sender], (s_send.at[2 + k], s_recv.at[2 + k]), zpeers[k - 1]
                ).wait_recv()
            sm_back[rows, lanes] = sm_z[0] + sm_z[1] + sm_z[2] + sm_z[3]
            small_copy(6).start()
        elif stage == 4:
            remote(
                sm_back.at[rows, other], sm_back.at[rows, other], (s_send.at[6], s_recv.at[6]), ypeer
            ).wait_recv()
            small_copy(7).start()
        else:
            remote(sm_back.at[away], sm_back.at[away], (s_send.at[7], s_recv.at[7]), sib).wait_recv()
            small_out[...] = sm_back[...]

    for n in range(2):
        over_x(n).start()
    for i in range(3):
        over_y(i).start()
    for copy in [loads[4]] + halves_in + loads[5:7]:
        copy.start()

    begin = first_rows(segs)
    turn_labels(segs, begin, segcol, segrow)
    hrow[...] = head_lanes(heads)
    hcol[...] = jnp.broadcast_to(hrow[...], (8, D)).T[:, 0:1]
    hgate = hrow
    sm_all[...] = small_in[...]
    loads[0].wait()
    loads[1].wait()
    loads[2].wait()

    @pl.loop(0, 4)
    def _(r):
        rows = pl.ds(pl.multiple_of(r * 256, 256), 256)
        low = (g0 * sgrad[rows, :]).astype(BF)
        outb[rows, :] = low
        grad = nt(low, wo[...].reshape(D, D)).astype(BF)
        sm_all[9:10, :] += colsum(ctx[rows, :].astype(F32) * grad.astype(F32))
        cgrad[rows, :] = grad * hgate[...].astype(BF)

    small_copy(0).start()
    loads[7].start()
    loads[3].wait()

    def weight_tiles(left, right, lane, rowgate, places):
        g = nn(left[...], right[:, pl.ds(lane, SB)])
        if rowgate is not None:
            g = g * rowgate[...]
        for r in range(2):
            ga[places[r]] = g[SB * r : SB * r + SB].astype(BF).reshape(2, 2, 2, 48, SB)

    for j in range(2):
        weight_tiles(ctxT, outb, SB * j, hcol, (SENT.index(12 + j), SENT.index(14 + j)))

    swap1(4).start()
    loads[4].wait()

    scale = LOG2E / math.sqrt(HD)
    factor = 1.0 / math.sqrt(HD)
    half_iota = lax.broadcasted_iota(jnp.int32, (1, 128), 1) // HD
    halves = [(half_iota == e).astype(F32).astype(BF) for e in range(2)]

    def by_head(v):
        return jnp.concatenate([v * halves[0], v * halves[1]], axis=0)

    def of_head(v):
        return jnp.where(half_iota == 0, v[:HALF], v[HALF:])

    def attend_back(i):
        p = i // 2
        b = i % 2
        lane = pl.multiple_of(p * 128, 128)
        for part in range(2):
            rows = pl.ds(pl.multiple_of(b * BLK + part * HALF, HALF), HALF)
            q = joined[rows, pl.ds(lane, 128)]
            k = joined[rows, pl.ds(D + lane, 128)]
            v = joined[rows, pl.ds(2 * D + lane, 128)]
            do = cgrad[rows, pl.ds(lane, 128)]
            k2 = by_head(k)
            s = nt(k2, q).reshape(2, HALF, HALF) * scale
            if part:
                s = jnp.where(segcol[b] == segrow[b], s, MASKED)
            first = 2 * (b * 6 + p)
            pr = jnp.exp2(s - lse[pl.ds(first, 2), :, part * HALF : part * HALF + HALF])
            dp = nt(by_head(v), do).reshape(2, HALF, HALF)
            delta = jnp.sum(pr * dp, axis=1, keepdims=True)
            ds = (pr * (dp - delta)).astype(BF).reshape(BLK, HALF)
            dqT = nn(k2.T, ds)
            dk = of_head(nn(ds, q))
            dv = of_head(nn(pr.astype(BF).reshape(BLK, HALF), do))
            joined[rows, pl.ds(lane, 128)] = (dqT * factor).T.astype(BF)
            joined[rows, pl.ds(D + lane, 128)] = (dk * factor).astype(BF)
            joined[rows, pl.ds(2 * D + lane, 128)] = dv.astype(BF)

    def qkv_tiles(h):
        at_h = SENT.index(h)

        @pl.loop(0, 3)
        def _(j):
            lane = pl.multiple_of(SB * (2 * j + h), 128)
            weight_tiles(tokT, joined, lane, None, (at_h + j, at_h + 3 + j))

    def middle():
        loads[5].wait()
        qkv_tiles(0)
        swap1(5).start()

    def first_sums():
        halves_in[0].wait()
        halves_in[2].wait()
        halves_in[1].wait()
        feed_far(0)
        step3(2)

    plan = {
        0: [lambda: small_take(0)],
        1: [lambda: step1(4), first_sums],
        5: [middle],
        6: [lambda: step1(5), lambda: small_take(1)],
        7: [lambda: feed_far(1), lambda: step3(3)],
        9: [lambda: step3(0)],
        11: [lambda: step2(4)],
    }

    @pl.loop(0, 12)
    def _(i):
        attend_back(i)
        for at_step, todo in plan.items():

            @pl.when(i == at_step)
            def _(todo=todo):
                for f in todo:
                    f()

    qkv_tiles(1)
    swap1(6).start()
    loads[6].wait()

    def input_rows(lo, hi):
        @pl.loop(lo, hi)
        def _(r):
            rows = pl.ds(pl.multiple_of(r * 512, 512), 512)
            igrad[rows, :] = sgrad[rows, :] + nt(joined[rows, :], wq[...].reshape(D, 3 * D))

    step3(1)
    step1(6)
    small_take(2)
    input_rows(0, 1)
    step4(2)
    step3(4)
    step2(5)
    step4(3)
    input_rows(1, 2)
    def turn_back():
        loads[7].wait()

        @pl.loop(0, 6)
        def _(t):
            b = t // 3
            hot = turning(jnp.where(b == 0, begin[0:1], begin[1:2]), -1).astype(BF)
            rows = pl.ds(pl.multiple_of(b * BLK, BLK), BLK)
            cols = pl.ds(pl.multiple_of(t % 3 * 256, 256), 256)
            cgrad[rows, cols] = nn(hot, ctx[rows, cols]).astype(BF)
            rest = igrad[rows, cols]
            value = None
            for _ in range(3):
                high = rest.astype(BF)
                rest = rest - high.astype(F32)
                one = nn(hot, high)
                value = one if value is None else value + one
            igrad[rows, cols] = value

    step2(6)
    step3(5)
    turn_back()
    igrad_copy = pltpu.make_async_copy(igrad, o_igrad, out_sem.at[0])
    igrad_copy.start()
    out_copy = pltpu.make_async_copy(cgrad, o_out, out_sem.at[1])
    out_copy.start()
    step4(0)
    step3(6)
    step4(1)
    step4(4)
    small_take(3)
    step4(5)
    step4(6)

    def deal(n, k, to, u):
        return remote(
            slots.at[to, :, n],
            gz.at[:, n, :, u],
            (a_send.at[n, k - 1], a_recv.at[n, k - 1]),
            zpeers[k - 1],
        )

    @pl.when(z != spare)
    def _():
        @pl.loop(0, 48)
        def _(s):
            slots[s // 12, s // 6 % 2, s // PER % PARTS, s % PER] = total[order[s]]

        for n in range(PARTS):
            for k in (1, 2, 3):
                deal(n, k, (z + k) % 4, unit(z)).start()
            gz[:, n, :, unit(z)] = slots[z, :, n]

    def piece(n, cc, yy, xx):
        return gfull.at[n, :, 4 * cc + 2 * yy + xx]

    others = ((y, 1 - x), (1 - y, x), (1 - y, 1 - x))

    def near(n, k):
        src = gz.at[1 - x if k in (0, 2) else x, n]
        sems = (f_send.at[n, k], f_recv.at[n, k])
        return remote(src, piece(n, c, y, x), sems, (xpeer, ypeer, diag, sib)[k])

    def onward(n, k):
        yy, xx = others[k]
        to = piece(n, c, yy, xx)
        return remote(to, to, (f_send.at[n, 4 + k], f_recv.at[n, 4 + k]), sib)

    def pass_on(n):
        for k in range(3):
            near(n, k).wait_recv()
            onward(n, k).start()

    for n in range(PARTS):
        for k in (1, 2, 3):
            sender = (z + 4 - k) % 4

            @pl.when(sender != spare)
            def _(n=n, k=k, sender=sender):
                deal(n, k, z, unit(sender)).wait_recv()

        for k in range(4):
            near(n, k).start()
        gfull[n, :, 4 * c + 2 * y + x] = gz[x, n]
        if n:
            pass_on(n - 1)
    small_take(4)
    pass_on(PARTS - 1)
    small_take(5)
    for n in range(PARTS):
        near(n, 3).wait_recv()
        for k in range(3):
            onward(n, k).wait_recv()
    full_copy = pltpu.make_async_copy(gfull, o_full, out_sem.at[2])
    full_copy.start()
    for n in range(PARTS):
        for k in range(4):
            near(n, k).wait_send()
        for k in range(3):
            onward(n, k).wait_send()

        @pl.when(z != spare)
        def _(n=n):
            for k in (1, 2, 3):
                deal(n, k, (z + k) % 4, unit(z)).wait_send()

    for g in range(len(GROUPS)):
        for k in (1, 2, 3):

            @pl.when((z + k) % 4 != spare)
            def _(g=g, k=k):
                swapz(g, k).wait_send()

    for k in range(8):
        small_copy(k).wait_send()
    for g in range(4, len(GROUPS)):
        for copy in [swap1(g)] + swap2(g) + swap3(g):
            copy.wait_send()
    for i in range(5):
        over_y(i).wait_send()
    for n in range(2):
        over_x(n).wait_send()
    igrad_copy.wait()
    out_copy.wait()
    full_copy.wait()


def run_backward(*arrays):
    sds = jax.ShapeDtypeStruct
    outs = (sds((ROWS, D), BF), sds((ROWS, D), F32), sds((PARTS, PER, 8, 3, 16, SB), BF), sds((16, D), F32))
    any_ = pl.BlockSpec(memory_space=pl.ANY)
    vm = pl.BlockSpec(memory_space=pltpu.VMEM)
    sm = pl.BlockSpec(memory_space=pltpu.SMEM)
    dma = pltpu.SemaphoreType.DMA
    return pl.pallas_call(
        backward_kernel,
        out_shape=outs,
        in_specs=[sm] * 3 + [vm] * 3 + [any_] * 10,
        out_specs=[any_] * 3 + [vm],
        scratch_shapes=[
            pltpu.VMEM((ROWS, 3 * D), BF),
            pltpu.VMEM((ROWS, D), BF),
            pltpu.VMEM((D, ROWS), BF),
            pltpu.VMEM((D, ROWS), BF),
            pltpu.VMEM((ROWS, D), F32),
            pltpu.VMEM((4, 192, 3 * D), BF),
            pltpu.VMEM((4, 192, D), BF),
            pltpu.VMEM((ROWS, D), BF),
            pltpu.VMEM((ROWS, D), BF),
            pltpu.VMEM((ROWS, D), F32),
            pltpu.VMEM((3, 8, 48, SB), BF),
            pltpu.VMEM((LEFT + 8, 2, 48, SB), BF),
            pltpu.VMEM((LEFT + 8, 2, 48, SB), BF),
            pltpu.VMEM((4, 8, 48, SB), BF),
            pltpu.VMEM((16, 2, 2, 2, 48, SB), BF),
            pltpu.VMEM((16, 2, 2, 48, SB), BF),
            pltpu.VMEM((16, 2, 48, SB), BF),
            pltpu.VMEM((16, 48, SB), BF),
            pltpu.VMEM((48, 3, 16, SB), BF),
            pltpu.VMEM((3, 48, 16, SB), BF),
            pltpu.VMEM((48, 16, SB), BF),
            pltpu.VMEM((4, 2, PARTS, PER, 16, SB), BF),
            pltpu.VMEM((2, PARTS, PER, 3, 16, SB), BF),
            pltpu.VMEM((PARTS, PER, 8, 3, 16, SB), BF),
            pltpu.VMEM((16, D), F32),
            pltpu.VMEM((8, D), F32),
            pltpu.VMEM((8, SB), F32),
            pltpu.VMEM((4, 8, SB), F32),
            pltpu.VMEM((16, D), F32),
            pltpu.VMEM((8, D), F32),
            pltpu.VMEM((8, SB), F32),
            pltpu.VMEM((8, SB), F32),
            pltpu.VMEM((2, HALF, 1), F32),
            pltpu.VMEM((2, 1, HALF), F32),
            pltpu.VMEM((1, D), F32),
            pltpu.VMEM((D, 1), F32),
            dma((8,)),
            dma((3,)),
            dma((7,)),
            dma((7,)),
            dma((7, 5)),
            dma((7, 5)),
            dma((7, 3)),
            dma((7, 3)),
            dma((PARTS, 3)),
            dma((PARTS, 3)),
            dma((PARTS, 7)),
            dma((PARTS, 7)),
            dma((8,)),
            dma((8,)),
            dma((3,)),
        ],
        compiler_params=pltpu.CompilerParams(
            collective_id=2, has_side_effects=True, vmem_limit_bytes=64 << 20
        ),
    )(*arrays)


def split(value):
    high = value.astype(BF)
    return high, (value - high.astype(F32)).astype(BF)


def update_kernel(
    small,
    gain,
    bias,
    full,
    master,
    left_stats,
    right_stats,
    left_root,
    right_root,
    out_in,
    igrad_in,
    o_grad,
    o_left,
    o_right,
    o_new,
    o_copy,
    o_unit,
    o_hidden,
    o_head,
    o_layer,
    o_norm,
    o_norm_new,
    o_out,
    o_igrad,
    turned,
    stage_out,
    stage_igrad,
    sem,
):
    slot = pl.program_id(0)
    moves_in = (
        pltpu.make_async_copy(out_in, stage_out, sem.at[0]),
        pltpu.make_async_copy(igrad_in, stage_igrad, sem.at[1]),
    )
    moves = (
        pltpu.make_async_copy(stage_out, o_out, sem.at[2]),
        pltpu.make_async_copy(stage_igrad, o_igrad, sem.at[3]),
    )

    @pl.when(slot == 0)
    def _():
        for move in moves_in:
            move.start()
        for i in range(4):
            o_unit[6 * i : 6 * i + 6, :] = many_rows(small[i : i + 1, :])
        o_hidden[...] = many_rows(small[6:7, :])
        o_norm[...] = small[4:6, :]
        rate = 0.2 / math.sqrt(ROWS * 32)
        o_norm_new[0:1, :] = one_row(gain[...]) - rate * small[4:5, :]
        o_norm_new[1:2, :] = one_row(bias[...]) - rate * small[5:6, :]
        lane = lax.broadcasted_iota(jnp.int32, (16, D), 1) // HD
        row = lax.broadcasted_iota(jnp.int32, (16, D), 0)
        by_head = jnp.sum(jnp.where(lane == row, small[9:10, :], 0.0), axis=1, keepdims=True)
        square = lax.broadcasted_iota(jnp.int32, (16, 128), 1)
        diagonal = square == lax.broadcasted_iota(jnp.int32, (16, 128), 0)
        o_head[...] = jnp.sum(jnp.where(diagonal, by_head, 0.0), axis=0, keepdims=True)[:, :12]
        pair = jnp.sum(small[7:9, :], axis=1, keepdims=True)
        first = lax.broadcasted_iota(jnp.int32, (1, 2), 1) == 0
        o_layer[...] = jnp.where(first, pair[0:1], pair[1:2])

    start = pl.multiple_of(lax.axis_index("mp") * 96, 16)
    own = full[0, pl.ds(start, 96), :]
    whole = full[0]
    o_grad[0] = own.astype(F32)
    o_left[0] = BETA * left_stats[0] + (1.0 - BETA) * nt(own, whole)
    turned[...] = whole.T
    root_high, root_low = split(left_root[0])
    stack = nn(jnp.concatenate([turned[pl.ds(start, 96), :], root_high, root_low], axis=0), whole)
    o_right[0] = BETA * right_stats[0] + (1.0 - BETA) * stack[:96]
    part_high, part_low = split(stack[96:192] + stack[192:])
    right_high, right_low = split(right_root[0])
    pair = nn(jnp.concatenate([part_high, part_low], axis=0), right_high)
    update = pair[:96] + pair[96:] + nn(part_high, right_low)
    new = master[0] - RATE * update
    o_new[0] = new
    o_copy[0] = new.astype(BF)

    @pl.when(slot == 2)
    def _():
        for first, then in zip(moves_in, moves):
            first.wait()
            then.start()

    @pl.when(slot == 5)
    def _():
        for move in moves:
            move.wait()


def run_update(*arrays):
    sds = jax.ShapeDtypeStruct
    whole = pl.BlockSpec((1, SB, SB), lambda s: (s, 0, 0))
    rows = pl.BlockSpec((1, 96, SB), lambda s: (s, 0, 0))
    any_ = pl.BlockSpec(memory_space=pl.ANY)

    def const(*shape):
        return pl.BlockSpec(shape, lambda s: (0, 0))

    flat = const(6, 128)
    return pl.pallas_call(
        update_kernel,
        grid=(6,),
        out_shape=(sds((6, 96, SB), F32),) * 4
        + (
            sds((6, 96, SB), BF),
            sds((24, 128), F32),
            sds((6, 128), F32),
            sds((1, 12), F32),
            sds((1, 2), F32),
            sds((2, D), F32),
            sds((2, D), F32),
            sds((ROWS, D), BF),
            sds((ROWS, D), F32),
        ),
        in_specs=[const(16, D), flat, flat, whole] + [rows] * 4 + [whole] + [any_] * 2,
        out_specs=[rows] * 5
        + [const(24, 128), flat, const(1, 12), const(1, 2), const(2, D), const(2, D), any_, any_],
        scratch_shapes=[
            pltpu.VMEM((SB, SB), BF),
            pltpu.VMEM((ROWS, D), BF),
            pltpu.VMEM((ROWS, D), F32),
            pltpu.SemaphoreType.DMA((4,)),
        ],
        compiler_params=pltpu.CompilerParams(vmem_limit_bytes=64 << 20),
    )(*arrays)


PLACE = tuple(FF_BLOCKS + SENT.index(b) for b in range(16)) + tuple(
    8 * (col // 2) + 4 * which + 2 * row + col % 2 for which in range(2) for row in range(2) for col in range(8)
)


def fast_body(
    tokens,
    segments,
    head_mask,
    unit_mask,
    hidden_mask,
    layer_gates,
    qkv_weight,
    out_weight,
    norm_gain,
    norm_bias,
    up_weight,
    down_weight,
    cotangent,
    owner_slot,
    master,
    left_stats,
    right_stats,
    left_root,
    right_root,
):
    gain = norm_gain.reshape(6, 128)
    bias = norm_bias.reshape(6, 128)
    (output, joined, ctx, ctxT, tokT, summed_grad, sums, far, wq, wo, lse, small) = run_forward(
        layer_gates,
        head_mask,
        tokens,
        cotangent,
        segments,
        unit_mask.reshape(24, 128),
        hidden_mask.reshape(6, 128),
        gain,
        bias,
        qkv_weight,
        out_weight,
        up_weight,
        down_weight,
    )
    slot_order = jnp.sum(
        jnp.where(owner_slot[None, :] == jnp.arange(48)[:, None], jnp.asarray(PLACE)[None, :], 0), axis=1
    )
    output, input_grad, full, small = run_backward(
        layer_gates,
        head_mask,
        slot_order,
        small,
        segments,
        lse,
        sums,
        far,
        joined,
        ctx,
        ctxT,
        tokT,
        summed_grad,
        wq,
        wo,
        output,
    )
    (
        owned,
        left_new,
        right_new,
        weight_new,
        weight_copy,
        unit_grad,
        hidden_grad,
        head_grad,
        layer_grad,
        norm_grad,
        norm_new,
        output,
        input_grad,
    ) = run_update(
        small,
        gain,
        bias,
        full.reshape(6, SB, SB),
        master,
        left_stats,
        right_stats,
        left_root,
        right_root,
        output,
        input_grad,
    )
    return (
        output,
        input_grad,
        head_grad.reshape(12),
        unit_grad.reshape(FF),
        hidden_grad.reshape(D),
        layer_grad.reshape(2),
        norm_grad,
        norm_new,
        owned,
        left_new,
        right_new,
        weight_new,
        weight_copy,
    )


def solution(mesh):
    return jax.shard_map(
        fast_body if dict(mesh.shape) == {"dp": 8, "mp": 4} else body,
        mesh=mesh,
        in_specs=(
            P(("dp", "mp"), None),
            P(("dp", "mp"), None),
            P(),
            P(),
            P(),
            P(),
            P("mp", None),
            P("mp", None),
            P(),
            P(),
            P(None, "mp"),
            P(None, "mp"),
            P(("dp", "mp"), None),
            P(),
            P("dp", "mp", None),
            P("dp", "mp", None),
            P("dp", "mp", None),
            P("dp", "mp", None),
            P("dp", None, None),
        ),
        out_specs=(
            P(("dp", "mp"), None),
            P(("dp", "mp"), None),
            P(),
            P(),
            P(),
            P(),
            P(),
            P(),
            P("dp", "mp", None),
            P("dp", "mp", None),
            P("dp", "mp", None),
            P("dp", "mp", None),
            P("dp", "mp", None),
        ),
        check_vma=False,
    )
```
